256 devices in a mesh: beam: 32 (over z, x), tm: 8 (over y, core).
Axes of the slice: x: 4, y: 4, z: 8, core: 2. Of those that a mesh axis runs over, the one named last changes fastest.
Arguments:
- voltages: float32 [32, 2, 2, 128, 8192], P('beam', None, None, 'tm'), may hold values from -20 to 20
- filter_taps: float32 [8, 8192], replicated, may hold values from -2 to 2
Outputs:
- cleaned: float32 [32, 2, 128, 8192], P('beam', None, 'tm')
The draws below stay inside these ranges and needn't reach their ends.
All inputs are finite; a program needn't handle non-finite values.
Results may differ from the reference program's by a relative error of at most 0.000058.
Values sent between devices are 32-bit elements; how exact they have to be, the bound alone decides.
No kernel may reach another device: no remote copies, remote signals or barrier semaphores. Data moves between devices by JAX's collectives and lax.ppermute only.
A program may use at most 64 MiB of HBM per device.

```python
import math
import jax
import jax.numpy as jnp
from jax import lax

CHANNELS = 8192
TAPS = 8
FRAMES = 128
BEAMS = 32


def draw_voltages(key, part):
    noise_key = jax.random.fold_in(jax.random.fold_in(key, 17), 0)
    shape = (BEAMS, 2, 2, FRAMES, CHANNELS)
    base = jnp.clip(jax.random.normal(noise_key, shape, jnp.float32), -6.0, 6.0) * 0.5
    beam_pos = jnp.arange(BEAMS, dtype=jnp.float32).reshape(BEAMS, 1, 1, 1, 1) / max(BEAMS - 1, 1)
    sample_pos = (jnp.arange(FRAMES, dtype=jnp.float32)[:, None] * CHANNELS + jnp.arange(CHANNELS, dtype=jnp.float32)[None, :]) / (FRAMES * CHANNELS)
    gain = jnp.exp(0.5 * math.log(3.0) * beam_pos + 0.5 * math.log(10.0) * sample_pos[None, None, None])
    return base * gain


def noise(own_key, extent, deviation, limit, held_as=jnp.bfloat16):
    return jnp.clip(deviation * jax.random.normal(own_key, extent, jnp.float32), -limit, limit).astype(held_as)


def setup_inputs(seed: int = 0) -> dict:
    arg_keys = jax.random.split(jax.random.key(seed), 3)
    return {
        "voltages": draw_voltages(jax.random.fold_in(arg_keys[2], 71), 0),
        "filter_taps": noise(arg_keys[1], (TAPS, CHANNELS), TAPS ** -0.5, 2.0, jnp.float32),
    }


def reference(voltages, filter_taps):

    def one_beam(beam_volts):
        padded = jnp.concatenate([beam_volts, jnp.zeros((2, 2, TAPS - 1, CHANNELS), beam_volts.dtype)], axis=2)
        filtered = jnp.zeros_like(beam_volts)
        for tap_index in range(TAPS):
            filtered = filtered + filter_taps[tap_index] * padded[:, :, tap_index:tap_index + FRAMES]
        spectrum = jnp.fft.fft(filtered[:, 0] + 1j * filtered[:, 1], axis=-1) / math.sqrt(CHANNELS)
        return jnp.real(spectrum) ** 2 + jnp.imag(spectrum) ** 2
    powers = lax.map(one_beam, voltages)
    channel_sum = lax.optimization_barrier(jnp.sum(lax.optimization_barrier(jnp.sum(powers, axis=2)) / FRAMES, axis=0))
    return powers - channel_sum[None, :, None, :] / BEAMS
```

```python
import functools
import math

import jax
import jax.numpy as jnp
import ml_dtypes
import numpy as np
from jax import lax
from jax.experimental import pallas as pl
from jax.experimental.pallas import tpu as pltpu
from jax.sharding import PartitionSpec as P

LANES = 128
ROWS = 64
CHANNELS = ROWS * LANES
TAPS = 8
FRAMES = 16
HELD = 9
AHEAD = 4
BACK = 3
BOTH = ("beam", "tm")
X, Y, Z = 4, 4, 8

RING4 = ((1, 0, 3, 2), (3, 2, 1, 0))
RING8 = ((1, 0, 3, 2, 5, 4, 7, 6), (7, 2, 1, 4, 3, 6, 5, 0), (3, 6, 5, 0, 7, 2, 1, 4))


def place(z, x, y, core):
    return ((z * X + x) * Y + y) * 2 + core


def swap_pairs(axis, partner):
    pairs = []
    for z in range(Z):
        for x in range(X):
            for y in range(Y):
                there = {
                    "z": lambda: (partner[z], x, y),
                    "x": lambda: (z, partner[x], y),
                    "y": lambda: (z, x, partner[y]),
                }[axis]()
                pairs.append((place(z, x, y, 1), place(*there, 1)))
    return pairs


def in_two(table):
    high = table.astype(ml_dtypes.bfloat16)
    low = (table - high.astype(np.float64)).astype(ml_dtypes.bfloat16)
    return high, low


def dft_tables():
    q = np.arange(ROWS)
    angle = 2.0 * np.pi * (np.outer(q, q) % ROWS) / ROWS
    cos, sin = np.cos(angle), np.sin(angle)
    first = np.block([[cos, sin], [-sin, cos]])
    high, low = in_two(first)
    first = np.block([[high, high], [low, low]])
    lane = np.arange(LANES)
    order = np.concatenate([np.arange(0, LANES, 2), np.arange(1, LANES, 2)])
    angle = 2.0 * np.pi * (np.outer(order, lane) % LANES) / LANES
    cos, sin = np.cos(angle), np.sin(angle)
    second = np.block([[cos, sin], [-sin, cos]])
    second = np.concatenate(in_two(second), axis=0)
    angle = 2.0 * np.pi * np.outer(q, lane) / CHANNELS
    twist = np.stack([np.cos(angle), np.sin(angle)]).astype(np.float32)
    return first, second, twist


def halves(values):
    high = values.astype(jnp.bfloat16)
    low = (values - high.astype(jnp.float32)).astype(jnp.bfloat16)
    return high, low


def power_rows(frames, first_ref, second_ref, twist_ref):
    count = len(frames)
    cols = [jnp.concatenate([re, im], axis=0) for re, im in frames]
    high, low = halves(jnp.concatenate(cols, axis=1))
    both = jnp.dot(
        first_ref[...],
        jnp.concatenate([high, low], axis=0),
        preferred_element_type=jnp.float32,
    )
    section = both[: 2 * ROWS] + both[2 * ROWS :]
    cos, sin = twist_ref[0], twist_ref[1]
    rows = []
    for g in range(count):
        re = section[:ROWS, g * LANES : (g + 1) * LANES]
        im = section[ROWS:, g * LANES : (g + 1) * LANES]
        rows.append(jnp.concatenate([re * cos + im * sin, im * cos - re * sin], axis=1))
    high, low = halves(jnp.concatenate(rows, axis=0))
    across = (((1,), (1,)), ((), ()))
    table = second_ref[...]
    both = lax.dot_general(table, high, across, preferred_element_type=jnp.float32)
    both += lax.dot_general(table, low, across, preferred_element_type=jnp.float32)
    spec = both[: 2 * LANES] + both[2 * LANES :]
    re, im = spec[:LANES], spec[LANES:]
    powers = (re * re + im * im) * (1.0 / CHANNELS)
    left = lax.broadcasted_iota(jnp.int32, (ROWS, LANES), 1) < ROWS
    out = []
    for g in range(0, count, 2):
        even = powers[:ROWS, g * ROWS : (g + 2) * ROWS]
        odd = powers[ROWS:, g * ROWS : (g + 2) * ROWS]
        out.append(jnp.where(left, even, pltpu.roll(odd, ROWS, 1)))
        out.append(jnp.where(left, pltpu.roll(even, ROWS, 1), odd))
    return out


def held_kernel(volt_ref, taps_ref, first_ref, second_ref, twist_ref, pow_ref, part_ref, sum_ref, filt_ref):
    keep = lax.axis_index("tm") > 0

    def strip(s, _):
        at = pl.multiple_of(s * 64, 64)
        rows = pl.ds(pl.multiple_of(s * 8, 8), 8)
        taps = [taps_ref[pl.ds(at + t, 8, stride=8), :] for t in range(TAPS)]
        for p in range(2):
            for c in range(2):
                x = [volt_ref[p, c, f // 8, pl.ds(at + f % 8, 8, stride=8), :] for f in range(FRAMES)]
                for f in range(HELD + AHEAD):
                    total = taps[0] * x[f]
                    for t in range(1, min(TAPS, FRAMES - f)):
                        total = total + taps[t] * x[f + t]
                    if f < HELD:
                        filt_ref[p, c, f, rows, :] = total
                    else:
                        part_ref[p, c, f - HELD, rows, :] = total
                for j in range(BACK):
                    total = taps[BACK - j] * x[0]
                    for t in range(BACK - j + 1, TAPS):
                        total = total + taps[t] * x[t - BACK + j]
                    part_ref[p, c, AHEAD + j, rows, :] = jnp.where(keep, total, 0.0)
        return 0

    lax.fori_loop(0, ROWS // 8, strip, 0)
    sums = [None, None]
    for start in range(0, HELD, 2):
        which = [(p, f) for f in range(start, min(start + 2, HELD)) for p in range(2)]
        frames = [(filt_ref[p, 0, f], filt_ref[p, 1, f]) for p, f in which]
        for (p, f), power in zip(which, power_rows(frames, first_ref, second_ref, twist_ref)):
            pow_ref[p, f] = power
            sums[p] = power if sums[p] is None else sums[p] + power
    for p in range(2):
        sum_ref[p] = sums[p]


def rim_kernel(part_ref, later_ref, earlier_ref, taps_ref, first_ref, second_ref, twist_ref, had_ref, pow_ref, back_ref, sum_ref):
    taps = [taps_ref[pl.ds(t, ROWS, stride=8), :] for t in range(TAPS)]

    def finished(p, j):
        out = []
        for c in range(2):
            total = part_ref[p, c, j]
            if j < AHEAD:
                for i in range(j + 1):
                    t = FRAMES + i - HELD - j
                    total = total + taps[t] * later_ref[p, c, pl.ds(i, ROWS, stride=AHEAD), :]
            else:
                for t in range(BACK - (j - AHEAD)):
                    i = 4 - BACK + (j - AHEAD) + t
                    total = total + taps[t] * earlier_ref[p, c, pl.ds(i, ROWS, stride=4), :]
            out.append(total)
        return tuple(out)

    sums = [had_ref[0], had_ref[1]]
    for start in range(0, AHEAD + BACK, 2):
        which = [(p, j) for j in range(start, min(start + 2, AHEAD + BACK)) for p in range(2)]
        frames = [finished(p, j) for p, j in which]
        for (p, j), power in zip(which, power_rows(frames, first_ref, second_ref, twist_ref)):
            if j < AHEAD:
                pow_ref[p, j] = power
            else:
                back_ref[p, j - AHEAD] = power
            sums[p] = sums[p] + power
    for p in range(2):
        sum_ref[p * ROWS : (p + 1) * ROWS, :] = sums[p]


def clean_kernel(scale, held_ref, ahead_ref, back_ref, sum_ref, out_ref):
    for p in range(2):
        base = sum_ref[p * ROWS : (p + 1) * ROWS, :] * scale
        for f in range(FRAMES):
            if f < HELD:
                power = held_ref[p, f]
            elif f < HELD + AHEAD:
                power = ahead_ref[p, f - HELD]
            else:
                power = back_ref[p, f - HELD - AHEAD]
            out_ref[p, f // 8, pl.ds(f % 8, ROWS, stride=8), :] = power - base


def on_core(kernel, out_shape, scratch=(), cost=None):
    return lambda *args: pl.pallas_call(
        kernel,
        out_shape=[jax.ShapeDtypeStruct(s, jnp.float32) for s in out_shape],
        in_specs=[pl.BlockSpec(memory_space=pltpu.VMEM)] * len(args),
        out_specs=[pl.BlockSpec(memory_space=pltpu.VMEM)] * len(out_shape),
        scratch_shapes=[pltpu.VMEM(s, jnp.float32) for s in scratch],
        compiler_params=pltpu.CompilerParams(vmem_limit_bytes=16 << 20),
        cost_estimate=cost,
    )(*args)


def by_rows(x):
    lead, frames = x.shape[:-2], x.shape[-2]
    x = x.reshape(*lead, frames, ROWS, LANES)
    return jnp.swapaxes(x, -3, -2).reshape(*lead, ROWS * frames, LANES)


def total_over_all(sums):
    up = [(i, i + 1) for i in range(0, 2 * X * Y * Z, 2)]
    sums = sums + lax.ppermute(sums, BOTH, up)
    for axis, ring in (("y", RING4), ("x", RING4), ("z", RING8)):
        for partner in ring:
            sums = sums + lax.ppermute(sums, BOTH, swap_pairs(axis, partner))
    other = lax.ppermute(sums, BOTH, [(b, a) for a, b in up])
    return jnp.where(lax.axis_index("tm") % 2 == 1, sums, other)


def body(voltages, filter_taps):
    volts = voltages[0]
    first, second, twist = (jnp.asarray(t) for t in dft_tables())
    devices = lax.axis_size("tm")
    later = lax.ppermute(volts[:, :, :AHEAD], "tm", [(i, i - 1) for i in range(1, devices)])
    earlier = lax.ppermute(volts[:, :, FRAMES - 4 :], "tm", [(i, (i + 1) % devices) for i in range(devices)])
    tiles = by_rows(volts.reshape(2, 2, 2, 8, CHANNELS))
    taps = by_rows(filter_taps)
    held, part, had = on_core(
        held_kernel,
        [(2, HELD, ROWS, LANES), (2, 2, AHEAD + BACK, ROWS, LANES), (2, ROWS, LANES)],
        scratch=[(2, 2, HELD, ROWS, LANES)],
        cost=pl.CostEstimate(flops=2 * 10**9, bytes_accessed=6 << 20, transcendentals=0),
    )(tiles, taps, first, second, twist)
    ahead, back, sums = on_core(
        rim_kernel,
        [(2, AHEAD, ROWS, LANES), (2, BACK, ROWS, LANES), (2 * ROWS, LANES)],
    )(part, by_rows(later), by_rows(earlier), taps, first, second, twist, had)
    back = lax.ppermute(back, "tm", [(i, (i - 1) % devices) for i in range(devices)])
    total = total_over_all(sums)
    scale = 1.0 / (FRAMES * devices * lax.axis_size("beam"))
    (out,) = on_core(functools.partial(clean_kernel, scale), [(2, 2, 8 * ROWS, LANES)])(held, ahead, back, total)
    out = jnp.swapaxes(out.reshape(2, 2, ROWS, 8, LANES), 2, 3)
    return out.reshape(1, 2, FRAMES, CHANNELS)


def solution(mesh):
    placed = (P("beam", None, None, "tm", None), P())
    return jax.shard_map(
        body, mesh=mesh, in_specs=placed, out_specs=P("beam", None, "tm", None), check_vma=False
    )
```

```python
import functools
import math

import jax
import jax.numpy as jnp
import ml_dtypes
import numpy as np
from jax import lax
from jax.experimental import pallas as pl
from jax.experimental.pallas import tpu as pltpu
from jax.sharding import PartitionSpec as P

LANES = 128
ROWS = 64
CHANNELS = ROWS * LANES
TAPS = 8
FRAMES = 16
HELD = 9
AHEAD = 4
BACK = 3
BOTH = ("beam", "tm")
X, Y, Z = 4, 4, 8

RING4 = ((1, 0, 3, 2), (3, 2, 1, 0))
RING8 = ((1, 0, 3, 2, 5, 4, 7, 6), (7, 2, 1, 4, 3, 6, 5, 0), (3, 6, 5, 0, 7, 2, 1, 4))


def place(z, x, y, core):
    return ((z * X + x) * Y + y) * 2 + core


def swap_pairs(axis, partner):
    pairs = []
    for z in range(Z):
        for x in range(X):
            for y in range(Y):
                there = {
                    "z": lambda: (partner[z], x, y),
                    "x": lambda: (z, partner[x], y),
                    "y": lambda: (z, x, partner[y]),
                }[axis]()
                pairs += [(place(z, x, y, c), place(*there, 1 - c)) for c in range(2)]
    return pairs


def kept_half():
    tm, beam = lax.axis_index("tm"), lax.axis_index("beam")
    return (tm % 2 + tm // 2 + beam % X + beam // X) % 2


def in_two(table):
    high = table.astype(ml_dtypes.bfloat16)
    low = (table - high.astype(np.float64)).astype(ml_dtypes.bfloat16)
    return high, low


def dft_tables():
    q = np.arange(ROWS)
    angle = 2.0 * np.pi * (np.outer(q, q) % ROWS) / ROWS
    cos, sin = np.cos(angle), np.sin(angle)
    first = np.block([[cos, sin], [-sin, cos]])
    high, low = in_two(first)
    first = np.block([[high, high], [low, low]])
    lane = np.arange(LANES)
    order = np.concatenate([np.arange(0, LANES, 2), np.arange(1, LANES, 2)])
    angle = 2.0 * np.pi * (np.outer(order, lane) % LANES) / LANES
    cos, sin = np.cos(angle), np.sin(angle)
    second = np.block([[cos, sin], [-sin, cos]])
    second = np.concatenate(in_two(second), axis=0)
    angle = 2.0 * np.pi * np.outer(q, lane) / CHANNELS
    twist = np.stack([np.cos(angle), np.sin(angle)]).astype(np.float32)
    return first, second, twist


def halves(values):
    high = values.astype(jnp.bfloat16)
    low = (values - high.astype(jnp.float32)).astype(jnp.bfloat16)
    return high, low


def power_rows(frames, first_ref, second_ref, twist_ref):
    count = len(frames)
    cols = [jnp.concatenate([re, im], axis=0) for re, im in frames]
    high, low = halves(jnp.concatenate(cols, axis=1))
    both = jnp.dot(
        first_ref[...],
        jnp.concatenate([high, low], axis=0),
        preferred_element_type=jnp.float32,
    )
    section = both[: 2 * ROWS] + both[2 * ROWS :]
    cos, sin = twist_ref[0], twist_ref[1]
    rows = []
    for g in range(count):
        re = section[:ROWS, g * LANES : (g + 1) * LANES]
        im = section[ROWS:, g * LANES : (g + 1) * LANES]
        rows.append(jnp.concatenate([re * cos + im * sin, im * cos - re * sin], axis=1))
    high, low = halves(jnp.concatenate(rows, axis=0))
    across = (((1,), (1,)), ((), ()))
    table = second_ref[...]
    both = lax.dot_general(table, high, across, preferred_element_type=jnp.float32)
    both += lax.dot_general(table, low, across, preferred_element_type=jnp.float32)
    spec = both[: 2 * LANES] + both[2 * LANES :]
    re, im = spec[:LANES], spec[LANES:]
    powers = (re * re + im * im) * (1.0 / CHANNELS)
    left = lax.broadcasted_iota(jnp.int32, (ROWS, LANES), 1) < ROWS
    out = []
    for g in range(0, count, 2):
        even = powers[:ROWS, g * ROWS : (g + 2) * ROWS]
        odd = powers[ROWS:, g * ROWS : (g + 2) * ROWS]
        out.append(jnp.where(left, even, pltpu.roll(odd, ROWS, 1)))
        out.append(jnp.where(left, pltpu.roll(even, ROWS, 1), odd))
    return out


def held_kernel(volt_ref, taps_ref, first_ref, second_ref, twist_ref, pow_ref, part_ref, sum_ref, filt_ref):
    keep = lax.axis_index("tm") > 0

    def strip(s, _):
        at = pl.multiple_of(s * 64, 64)
        rows = pl.ds(pl.multiple_of(s * 8, 8), 8)
        taps = [taps_ref[pl.ds(at + t, 8, stride=8), :] for t in range(TAPS)]
        for p in range(2):
            for c in range(2):
                x = [volt_ref[p, c, f // 8, pl.ds(at + f % 8, 8, stride=8), :] for f in range(FRAMES)]
                for f in range(HELD + AHEAD):
                    total = taps[0] * x[f]
                    for t in range(1, min(TAPS, FRAMES - f)):
                        total = total + taps[t] * x[f + t]
                    if f < HELD:
                        filt_ref[p, c, f, rows, :] = total
                    else:
                        part_ref[p, c, f - HELD, rows, :] = total
                for j in range(BACK):
                    total = taps[BACK - j] * x[0]
                    for t in range(BACK - j + 1, TAPS):
                        total = total + taps[t] * x[t - BACK + j]
                    part_ref[p, c, AHEAD + j, rows, :] = jnp.where(keep, total, 0.0)
        return 0

    lax.fori_loop(0, ROWS // 8, strip, 0)
    sums = [None, None]
    for start in range(0, HELD, 2):
        which = [(p, f) for f in range(start, min(start + 2, HELD)) for p in range(2)]
        frames = [(filt_ref[p, 0, f], filt_ref[p, 1, f]) for p, f in which]
        for (p, f), power in zip(which, power_rows(frames, first_ref, second_ref, twist_ref)):
            pow_ref[p, f] = power
            sums[p] = power if sums[p] is None else sums[p] + power
    for p in range(2):
        sum_ref[p] = sums[p]


def rim_kernel(part_ref, later_ref, earlier_ref, taps_ref, first_ref, second_ref, twist_ref, had_ref, pow_ref, back_ref, mine_ref, send_ref):
    taps = [taps_ref[pl.ds(t, ROWS, stride=8), :] for t in range(TAPS)]

    def finished(p, j):
        out = []
        for c in range(2):
            total = part_ref[p, c, j]
            if j < AHEAD:
                for i in range(j + 1):
                    t = FRAMES + i - HELD - j
                    total = total + taps[t] * later_ref[p, c, pl.ds(i, ROWS, stride=AHEAD), :]
            else:
                for t in range(BACK - (j - AHEAD)):
                    i = 4 - BACK + (j - AHEAD) + t
                    total = total + taps[t] * earlier_ref[p, c, pl.ds(i, ROWS, stride=4), :]
            out.append(total)
        return tuple(out)

    sums = [had_ref[0], had_ref[1]]
    for start in range(0, AHEAD + BACK, 2):
        which = [(p, j) for j in range(start, min(start + 2, AHEAD + BACK)) for p in range(2)]
        frames = [finished(p, j) for p, j in which]
        for (p, j), power in zip(which, power_rows(frames, first_ref, second_ref, twist_ref)):
            if j < AHEAD:
                pow_ref[p, j] = power
            else:
                back_ref[p, j - AHEAD] = power
            sums[p] = sums[p] + power
    keeps_second = kept_half() == 1
    mine_ref[...] = jnp.where(keeps_second, sums[1], sums[0])
    send_ref[...] = jnp.where(keeps_second, sums[0], sums[1])


def clean_kernel(scale, held_ref, ahead_ref, back_ref, mine_ref, other_ref, out_ref):
    keeps_second = kept_half() == 1
    mine, other = mine_ref[...] * scale, other_ref[...] * scale
    for p in range(2):
        base = jnp.where(keeps_second, mine, other) if p else jnp.where(keeps_second, other, mine)
        for f in range(FRAMES):
            if f < HELD:
                power = held_ref[p, f]
            elif f < HELD + AHEAD:
                power = ahead_ref[p, f - HELD]
            else:
                power = back_ref[p, f - HELD - AHEAD]
            out_ref[p, f // 8, pl.ds(f % 8, ROWS, stride=8), :] = power - base


def on_core(kernel, out_shape, scratch=(), cost=None):
    return lambda *args: pl.pallas_call(
        kernel,
        out_shape=[jax.ShapeDtypeStruct(s, jnp.float32) for s in out_shape],
        in_specs=[pl.BlockSpec(memory_space=pltpu.VMEM)] * len(args),
        out_specs=[pl.BlockSpec(memory_space=pltpu.VMEM)] * len(out_shape),
        scratch_shapes=[pltpu.VMEM(s, jnp.float32) for s in scratch],
        compiler_params=pltpu.CompilerParams(vmem_limit_bytes=16 << 20),
        cost_estimate=cost,
    )(*args)


def by_rows(x):
    lead, frames = x.shape[:-2], x.shape[-2]
    x = x.reshape(*lead, frames, ROWS, LANES)
    return jnp.swapaxes(x, -3, -2).reshape(*lead, ROWS * frames, LANES)


def total_over_all(mine, send, back):
    cores = [(i, i ^ 1) for i in range(2 * X * Y * Z)]
    left = [(i, (i - 1) % (2 * Y)) for i in range(2 * Y)]
    sums = mine + lax.ppermute(send, BOTH, cores)
    steps = [("y", r) for r in RING4] + [("x", r) for r in RING4] + [("z", r) for r in RING8]
    for n, (axis, partner) in enumerate(steps):
        if n == 1:
            sums, back = lax.optimization_barrier((sums, back))
            back = lax.ppermute(back, "tm", left)
        sums = sums + lax.ppermute(sums, BOTH, swap_pairs(axis, partner))
        if n == 4:
            sums, back = lax.optimization_barrier((sums, back))
    return sums, lax.ppermute(sums, BOTH, cores), back


def body(voltages, filter_taps):
    volts = voltages[0]
    first, second, twist = (jnp.asarray(t) for t in dft_tables())
    devices = lax.axis_size("tm")
    later = lax.ppermute(volts[:, :, :AHEAD], "tm", [(i, i - 1) for i in range(1, devices)])
    earlier = lax.ppermute(volts[:, :, FRAMES - 4 :], "tm", [(i, (i + 1) % devices) for i in range(devices)])
    tiles = by_rows(volts.reshape(2, 2, 2, 8, CHANNELS))
    taps = by_rows(filter_taps)
    held, part, had = on_core(
        held_kernel,
        [(2, HELD, ROWS, LANES), (2, 2, AHEAD + BACK, ROWS, LANES), (2, ROWS, LANES)],
        scratch=[(2, 2, HELD, ROWS, LANES)],
        cost=pl.CostEstimate(flops=2 * 10**9, bytes_accessed=6 << 20, transcendentals=0),
    )(tiles, taps, first, second, twist)
    ahead, back, mine, send = on_core(
        rim_kernel,
        [(2, AHEAD, ROWS, LANES), (2, BACK, ROWS, LANES), (ROWS, LANES), (ROWS, LANES)],
    )(part, by_rows(later), by_rows(earlier), taps, first, second, twist, had)
    mine, other, back = total_over_all(mine, send, back)
    scale = 1.0 / (FRAMES * devices * lax.axis_size("beam"))
    (out,) = on_core(functools.partial(clean_kernel, scale), [(2, 2, 8 * ROWS, LANES)])(held, ahead, back, mine, other)
    out = jnp.swapaxes(out.reshape(2, 2, ROWS, 8, LANES), 2, 3)
    return out.reshape(1, 2, FRAMES, CHANNELS)


def solution(mesh):
    placed = (P("beam", None, None, "tm", None), P())
    return jax.shard_map(
        body, mesh=mesh, in_specs=placed, out_specs=P("beam", None, "tm", None), check_vma=False
    )
```

```python
import functools
import math

import jax
import jax.numpy as jnp
import ml_dtypes
import numpy as np
from jax import lax
from jax.experimental import pallas as pl
from jax.experimental.pallas import tpu as pltpu
from jax.sharding import PartitionSpec as P

LANES = 128
ROWS = 64
CHANNELS = ROWS * LANES
TAPS = 8
FRAMES = 16
HELD = 9
AHEAD = 4
BACK = 3
SHORT = pl.CostEstimate(flops=1000, bytes_accessed=1000, transcendentals=0)
BOTH = ("beam", "tm")
X, Y, Z = 4, 4, 8

RING4 = ((1, 0, 3, 2), (3, 2, 1, 0))
RING8 = ((1, 0, 3, 2, 5, 4, 7, 6), (7, 2, 1, 4, 3, 6, 5, 0), (3, 6, 5, 0, 7, 2, 1, 4))


def place(z, x, y, core):
    return ((z * X + x) * Y + y) * 2 + core


def swap_pairs(axis, partner):
    pairs = []
    for z in range(Z):
        for x in range(X):
            for y in range(Y):
                there = {
                    "z": lambda: (partner[z], x, y),
                    "x": lambda: (z, partner[x], y),
                    "y": lambda: (z, x, partner[y]),
                }[axis]()
                pairs += [(place(z, x, y, c), place(*there, 1 - c)) for c in range(2)]
    return pairs


def kept_half():
    tm, beam = lax.axis_index("tm"), lax.axis_index("beam")
    return (tm % 2 + tm // 2 + beam % X + beam // X) % 2


def in_two(table):
    high = table.astype(ml_dtypes.bfloat16)
    low = (table - high.astype(np.float64)).astype(ml_dtypes.bfloat16)
    return high, low


def dft_tables():
    q = np.arange(ROWS)
    angle = 2.0 * np.pi * (np.outer(q, q) % ROWS) / ROWS
    cos, sin = np.cos(angle), np.sin(angle)
    first = np.block([[cos, sin], [-sin, cos]])
    high, low = in_two(first)
    first = np.block([[high, high], [low, low]])
    lane = np.arange(LANES)
    order = np.concatenate([np.arange(0, LANES, 2), np.arange(1, LANES, 2)])
    angle = 2.0 * np.pi * (np.outer(order, lane) % LANES) / LANES
    cos, sin = np.cos(angle), np.sin(angle)
    second = np.block([[cos, sin], [-sin, cos]])
    second = np.concatenate(in_two(second), axis=0)
    angle = 2.0 * np.pi * np.outer(q, lane) / CHANNELS
    twist = np.stack([np.cos(angle), np.sin(angle)]).astype(np.float32)
    return np.concatenate([first, second], axis=0), twist


def halves(values):
    high = values.astype(jnp.bfloat16)
    low = (values - high.astype(jnp.float32)).astype(jnp.bfloat16)
    return high, low


def power_rows(frames, table_ref, twist_ref):
    count = len(frames)
    cols = [jnp.concatenate([re, im], axis=0) for re, im in frames]
    high, low = halves(jnp.concatenate(cols, axis=1))
    both = jnp.dot(
        table_ref[: 4 * ROWS],
        jnp.concatenate([high, low], axis=0),
        preferred_element_type=jnp.float32,
    )
    section = both[: 2 * ROWS] + both[2 * ROWS :]
    cos, sin = twist_ref[0], twist_ref[1]
    rows = []
    for g in range(count):
        re = section[:ROWS, g * LANES : (g + 1) * LANES]
        im = section[ROWS:, g * LANES : (g + 1) * LANES]
        rows.append(jnp.concatenate([re * cos + im * sin, im * cos - re * sin], axis=1))
    high, low = halves(jnp.concatenate(rows, axis=0))
    across = (((1,), (1,)), ((), ()))
    table = table_ref[4 * ROWS :]
    both = lax.dot_general(table, high, across, preferred_element_type=jnp.float32)
    both += lax.dot_general(table, low, across, preferred_element_type=jnp.float32)
    spec = both[: 2 * LANES] + both[2 * LANES :]
    re, im = spec[:LANES], spec[LANES:]
    powers = (re * re + im * im) * (1.0 / CHANNELS)
    left = lax.broadcasted_iota(jnp.int32, (ROWS, LANES), 1) < ROWS
    out = []
    for g in range(0, count, 2):
        even = powers[:ROWS, g * ROWS : (g + 2) * ROWS]
        odd = powers[ROWS:, g * ROWS : (g + 2) * ROWS]
        out.append(jnp.where(left, even, pltpu.roll(odd, ROWS, 1)))
        out.append(jnp.where(left, pltpu.roll(even, ROWS, 1), odd))
    return out


def rim_copies(volt_ref, out_ref, sems, last):
    half, at = (1, 8 - AHEAD) if last else (0, 0)
    return [
        pltpu.make_async_copy(volt_ref.at[p, c, half, :, at : at + AHEAD, :], out_ref.at[p, c], sems.at[2 * p + c])
        for p in range(2)
        for c in range(2)
    ]


def rim_kernel(volt_ref, cross_ref, near_ref, sems):
    for core in range(2):

        @pl.when(lax.axis_index("tm") % 2 == core)
        def _():
            copies = rim_copies(volt_ref, near_ref, sems.at[0], core == 0)
            copies += rim_copies(volt_ref, cross_ref, sems.at[1], core == 1)
            for copy in copies:
                copy.start()
            for copy in copies:
                copy.wait()


def held_kernel(
    volt_in, taps_in, table_in, twist_in,
    pow_ref, part_ref, sum_ref, taps_ref, table_ref, twist_ref,
    volt_ref, filt_ref, strip_sems, table_sems,
):
    def strip_copy(s):
        rows = pl.ds(pl.multiple_of(s * 64, 64), 64)
        return pltpu.make_async_copy(volt_in.at[:, :, :, rows, :], volt_ref.at[:, :, :, rows, :], strip_sems.at[s])

    taps_copy = pltpu.make_async_copy(taps_in, taps_ref, table_sems.at[0])
    table_copy = pltpu.make_async_copy(table_in, table_ref, table_sems.at[1])
    twist_copy = pltpu.make_async_copy(twist_in, twist_ref, table_sems.at[2])
    taps_copy.start()
    for s in range(ROWS // 8):
        strip_copy(s).start()
    table_copy.start()
    twist_copy.start()
    taps_copy.wait()
    keep = lax.axis_index("tm") > 0

    def strip(s, _):
        strip_copy(s).wait()
        at = pl.multiple_of(s * 64, 64)
        rows = pl.ds(pl.multiple_of(s * 8, 8), 8)
        taps = [taps_ref[pl.ds(at + t, 8, stride=8), :] for t in range(TAPS)]
        for p in range(2):
            for c in range(2):
                x = [volt_ref[p, c, f // 8, pl.ds(at + f % 8, 8, stride=8), :] for f in range(FRAMES)]
                for f in range(HELD + AHEAD):
                    total = taps[0] * x[f]
                    for t in range(1, min(TAPS, FRAMES - f)):
                        total = total + taps[t] * x[f + t]
                    if f < HELD:
                        filt_ref[p, c, f, rows, :] = total
                    else:
                        part_ref[p, c, f - HELD, rows, :] = total
                for j in range(BACK):
                    total = taps[BACK - j] * x[0]
                    for t in range(BACK - j + 1, TAPS):
                        total = total + taps[t] * x[t - BACK + j]
                    part_ref[p, c, AHEAD + j, rows, :] = jnp.where(keep, total, 0.0)
        return 0

    lax.fori_loop(0, ROWS // 8, strip, 0)
    table_copy.wait()
    twist_copy.wait()
    sums = [None, None]
    for start in range(0, HELD, 2):
        which = [(p, f) for f in range(start, min(start + 2, HELD)) for p in range(2)]
        frames = [(filt_ref[p, 0, f], filt_ref[p, 1, f]) for p, f in which]
        for (p, f), power in zip(which, power_rows(frames, table_ref, twist_ref)):
            pow_ref[p, f] = power
            sums[p] = power if sums[p] is None else sums[p] + power
    for p in range(2):
        sum_ref[p] = sums[p]


def rim_powers(role, part_ref, came_ref, taps_ref, table_ref, twist_ref, sums, keep, store):
    slots = AHEAD if role == "ahead" else BACK
    taps = [taps_ref[pl.ds(t, ROWS, stride=8), :] for t in range(TAPS)]

    def finished(p, j):
        out = []
        for c in range(2):
            if role == "ahead":
                terms = [(FRAMES + i - HELD - j, i) for i in range(j + 1)]
                total = part_ref[p, c, j]
            else:
                terms = [(t, AHEAD - BACK + j + t) for t in range(BACK - j)]
                total = part_ref[p, c, AHEAD + j]
            rest = None
            for t, i in terms:
                term = taps[t] * came_ref[p, c, pl.ds(i, ROWS, stride=AHEAD), :]
                rest = term if rest is None else rest + term
            out.append(total + (rest if keep is None else jnp.where(keep, rest, 0.0)))
        return tuple(out)

    for start in range(0, slots, 2):
        which = [(p, j) for j in range(start, min(start + 2, slots)) for p in range(2)]
        frames = [finished(p, j) for p, j in which]
        for (p, j), power in zip(which, power_rows(frames, table_ref, twist_ref)):
            store[p, j] = power
            sums[p] = sums[p] + power
    return sums


def near_kernel(part_ref, near_ref, taps_ref, table_ref, twist_ref, had_ref, early_ref, sum_ref):
    for core, role in enumerate(("ahead", "back")):

        @pl.when(lax.axis_index("tm") % 2 == core)
        def _():
            sums = [had_ref[0], had_ref[1]]
            sums = rim_powers(role, part_ref, near_ref, taps_ref, table_ref, twist_ref, sums, None, early_ref)
            sum_ref[0], sum_ref[1] = sums


def cross_kernel(last, part_ref, cross_ref, taps_ref, table_ref, twist_ref, had_ref, early_ref, ahead_ref, back_ref, mine_ref, send_ref):
    tm = lax.axis_index("tm")
    for core, role in enumerate(("back", "ahead")):

        @pl.when(tm % 2 == core)
        def _():
            sums = [had_ref[0], had_ref[1]]
            store, keep = (back_ref, None) if core == 0 else (ahead_ref, tm < last)
            sums = rim_powers(role, part_ref, cross_ref, taps_ref, table_ref, twist_ref, sums, keep, store)
            for p in range(2):
                if core == 0:
                    ahead_ref[p] = early_ref[p]
                else:
                    back_ref[p] = early_ref[p, :BACK]
            keeps_second = kept_half() == 1
            mine_ref[...] = jnp.where(keeps_second, sums[1], sums[0])
            send_ref[...] = jnp.where(keeps_second, sums[0], sums[1])


def clean_kernel(scale, held_ref, ahead_ref, back_ref, mine_ref, other_ref, out_ref):
    keeps_second = kept_half() == 1
    mine, other = mine_ref[...] * scale, other_ref[...] * scale
    for p in range(2):
        base = jnp.where(keeps_second, mine, other) if p else jnp.where(keeps_second, other, mine)
        for f in range(FRAMES):
            if f < HELD:
                power = held_ref[p, f]
            elif f < HELD + AHEAD:
                power = ahead_ref[p, f - HELD]
            else:
                power = back_ref[p, f - HELD - AHEAD]
            out_ref[p, f // 8, pl.ds(f % 8, ROWS, stride=8), :] = power - base


def on_core(kernel, out_shape, scratch=(), far=False, vmem=16 << 20, cost=None):
    space = pl.ANY if far else pltpu.VMEM
    where = pltpu.VMEM if far else jax.ShapeDtypeStruct
    shapes = [s if not isinstance(s, tuple) else where(s, jnp.float32) for s in out_shape]
    return lambda *args: pl.pallas_call(
        kernel,
        out_shape=shapes,
        in_specs=[pl.BlockSpec(memory_space=space)] * len(args),
        out_specs=[pl.BlockSpec(memory_space=pltpu.VMEM)] * len(out_shape),
        scratch_shapes=[pltpu.VMEM(s, jnp.float32) if isinstance(s, tuple) else s for s in scratch],
        compiler_params=pltpu.CompilerParams(vmem_limit_bytes=vmem),
        cost_estimate=cost,
    )(*args)


def in_hbm(x):
    return pltpu.with_memory_space_constraint(x, pltpu.HBM)


def by_rows(x):
    lead, frames = x.shape[:-2], x.shape[-2]
    x = x.reshape(*lead, frames, ROWS, LANES)
    return jnp.swapaxes(x, -3, -2).reshape(*lead, ROWS * frames, LANES)


def total_over_all(mine, send, back):
    cores = [(i, i ^ 1) for i in range(2 * X * Y * Z)]
    left = [(i, (i - 1) % (2 * Y)) for i in range(2 * Y)]
    sums = mine + lax.ppermute(send, BOTH, cores)
    steps = [("y", r) for r in RING4] + [("x", r) for r in RING4] + [("z", r) for r in RING8]
    for n, (axis, partner) in enumerate(steps):
        if n == 1:
            sums, back = lax.optimization_barrier((sums, back))
            back = lax.ppermute(back, "tm", left)
        sums = sums + lax.ppermute(sums, BOTH, swap_pairs(axis, partner))
        if n == 4:
            sums, back = lax.optimization_barrier((sums, back))
    return sums, lax.ppermute(sums, BOTH, cores), back


def body(voltages, filter_taps):
    devices = lax.axis_size("tm")
    table, twist = (jnp.asarray(t) for t in dft_tables())
    tiles = jnp.swapaxes(voltages[0].reshape(2, 2, 2, 8, ROWS, LANES), 3, 4)
    rim = (2, 2, ROWS, AHEAD, LANES)
    rows = (2, 2, ROWS * AHEAD, LANES)
    cross, near = on_core(
        rim_kernel,
        [rim, rim],
        scratch=[pltpu.SemaphoreType.DMA((2, 4))],
        far=True,
        cost=SHORT,
    )(in_hbm(tiles))
    near = lax.ppermute(near.reshape(rows), "tm", [(i, i ^ 1) for i in range(devices)])
    cross = lax.ppermute(cross.reshape(rows), "tm", [(i, (i + 1 if i % 2 else i - 1) % devices) for i in range(devices)])
    strips = (2, 2, 2, ROWS * 8, LANES)
    held, part, had, taps, table, twist = on_core(
        held_kernel,
        [
            (2, HELD, ROWS, LANES),
            (2, 2, AHEAD + BACK, ROWS, LANES),
            (2, ROWS, LANES),
            (ROWS * TAPS, LANES),
            pltpu.VMEM(table.shape, table.dtype),
            twist.shape,
        ],
        scratch=[
            strips,
            (2, 2, HELD, ROWS, LANES),
            pltpu.SemaphoreType.DMA((ROWS // 8,)),
            pltpu.SemaphoreType.DMA((3,)),
        ],
        far=True,
        cost=pl.CostEstimate(flops=2 * 10**9, bytes_accessed=6 << 20, transcendentals=0),
    )(in_hbm(tiles.reshape(strips)), in_hbm(by_rows(filter_taps)), in_hbm(table), in_hbm(twist))
    early, had = on_core(
        near_kernel,
        [(2, AHEAD, ROWS, LANES), (2, ROWS, LANES)],
        cost=pl.CostEstimate(flops=10**9, bytes_accessed=3 << 20, transcendentals=0),
    )(part, near, taps, table, twist, had)
    ahead, back, mine, send = on_core(
        functools.partial(cross_kernel, devices - 1),
        [(2, AHEAD, ROWS, LANES), (2, BACK, ROWS, LANES), (ROWS, LANES), (ROWS, LANES)],
    )(part, cross, taps, table, twist, had, early)
    mine, other, back = total_over_all(mine, send, back)
    scale = 1.0 / (FRAMES * devices * lax.axis_size("beam"))
    (out,) = on_core(functools.partial(clean_kernel, scale), [(2, 2, 8 * ROWS, LANES)])(held, ahead, back, mine, other)
    out = jnp.swapaxes(out.reshape(2, 2, ROWS, 8, LANES), 2, 3)
    return out.reshape(1, 2, FRAMES, CHANNELS)


def solution(mesh):
    placed = (P("beam", None, None, "tm", None), P())
    return jax.shard_map(
        body, mesh=mesh, in_specs=placed, out_specs=P("beam", None, "tm", None), check_vma=False
    )
```

```python
import functools
import math

import jax
import jax.numpy as jnp
import ml_dtypes
import numpy as np
from jax import lax
from jax.experimental import pallas as pl
from jax.experimental.pallas import tpu as pltpu
from jax.sharding import PartitionSpec as P

LANES = 128
ROWS = 64
CHANNELS = ROWS * LANES
TAPS = 8
FRAMES = 16
HELD = 9
AHEAD = 4
BACK = 3
SHORT = pl.CostEstimate(flops=1000, bytes_accessed=1000, transcendentals=0)
BOTH = ("beam", "tm")
X, Y, Z = 4, 4, 8

RING4 = ((1, 0, 3, 2), (3, 2, 1, 0))
RING8 = ((1, 0, 3, 2, 5, 4, 7, 6), (7, 2, 1, 4, 3, 6, 5, 0), (3, 6, 5, 0, 7, 2, 1, 4))


def place(z, x, y, core):
    return ((z * X + x) * Y + y) * 2 + core


def swap_pairs(axis, partner):
    pairs = []
    for z in range(Z):
        for x in range(X):
            for y in range(Y):
                there = {
                    "z": lambda: (partner[z], x, y),
                    "x": lambda: (z, partner[x], y),
                    "y": lambda: (z, x, partner[y]),
                }[axis]()
                pairs += [(place(z, x, y, c), place(*there, 1 - c)) for c in range(2)]
    return pairs


def kept_half():
    tm, beam = lax.axis_index("tm"), lax.axis_index("beam")
    return (tm % 2 + tm // 2 + beam % X + beam // X) % 2


def in_two(table):
    high = table.astype(ml_dtypes.bfloat16)
    low = (table - high.astype(np.float64)).astype(ml_dtypes.bfloat16)
    return high, low


def dft_tables():
    q = np.arange(ROWS)
    angle = 2.0 * np.pi * (np.outer(q, q) % ROWS) / ROWS
    cos, sin = np.cos(angle), np.sin(angle)
    first = np.block([[cos, sin], [-sin, cos]])
    high, low = in_two(first)
    first = np.block([[high, high], [low, low]])
    lane = np.arange(LANES)
    order = np.concatenate([np.arange(0, LANES, 2), np.arange(1, LANES, 2)])
    angle = 2.0 * np.pi * (np.outer(order, lane) % LANES) / LANES
    cos, sin = np.cos(angle), np.sin(angle)
    second = np.block([[cos, sin], [-sin, cos]])
    second = np.concatenate(in_two(second), axis=0)
    angle = 2.0 * np.pi * np.outer(q, lane) / CHANNELS
    twist = np.stack([np.cos(angle), np.sin(angle)]).astype(np.float32)
    return np.concatenate([first, second], axis=0), twist


def halves(values):
    high = values.astype(jnp.bfloat16)
    low = (values - high.astype(jnp.float32)).astype(jnp.bfloat16)
    return high, low


def power_rows(frames, table_ref, twist_ref):
    count = len(frames)
    cols = [jnp.concatenate([re, im], axis=0) for re, im in frames]
    high, low = halves(jnp.concatenate(cols, axis=1))
    both = jnp.dot(
        table_ref[: 4 * ROWS],
        jnp.concatenate([high, low], axis=0),
        preferred_element_type=jnp.float32,
    )
    section = both[: 2 * ROWS] + both[2 * ROWS :]
    cos, sin = twist_ref[0], twist_ref[1]
    rows = []
    for g in range(count):
        re = section[:ROWS, g * LANES : (g + 1) * LANES]
        im = section[ROWS:, g * LANES : (g + 1) * LANES]
        rows.append(jnp.concatenate([re * cos + im * sin, im * cos - re * sin], axis=1))
    high, low = halves(jnp.concatenate(rows, axis=0))
    across = (((1,), (1,)), ((), ()))
    table = table_ref[4 * ROWS :]
    both = lax.dot_general(table, high, across, preferred_element_type=jnp.float32)
    both += lax.dot_general(table, low, across, preferred_element_type=jnp.float32)
    spec = both[: 2 * LANES] + both[2 * LANES :]
    re, im = spec[:LANES], spec[LANES:]
    powers = (re * re + im * im) * (1.0 / CHANNELS)
    left = lax.broadcasted_iota(jnp.int32, (ROWS, LANES), 1) < ROWS
    out = []
    for g in range(0, count, 2):
        even = powers[:ROWS, g * ROWS : (g + 2) * ROWS]
        odd = powers[ROWS:, g * ROWS : (g + 2) * ROWS]
        out.append(jnp.where(left, even, pltpu.roll(odd, ROWS, 1)))
        out.append(jnp.where(left, pltpu.roll(even, ROWS, 1), odd))
    return out


def rim_copies(volt_ref, out_ref, sems, last):
    half, at = (1, 8 - AHEAD) if last else (0, 0)
    return [
        pltpu.make_async_copy(volt_ref.at[p, c, half, :, at : at + AHEAD, :], out_ref.at[p, c], sems.at[2 * p + c])
        for p in range(2)
        for c in range(2)
    ]


def rim_kernel(volt_ref, cross_ref, near_ref, sems):
    for core in range(2):

        @pl.when(lax.axis_index("tm") % 2 == core)
        def _():
            copies = rim_copies(volt_ref, near_ref, sems.at[0], core == 0)
            copies += rim_copies(volt_ref, cross_ref, sems.at[1], core == 1)
            for copy in copies:
                copy.start()
            for copy in copies:
                copy.wait()


def held_kernel(
    volt_in, taps_in, table_in, twist_in,
    pow_ref, part_ref, sum_ref, taps_ref, table_ref, twist_ref,
    volt_ref, filt_ref, strip_sems, table_sems,
):
    def strip_copy(s):
        rows = pl.ds(pl.multiple_of(s * 64, 64), 64)
        return pltpu.make_async_copy(volt_in.at[:, :, :, rows, :], volt_ref.at[:, :, :, rows, :], strip_sems.at[s])

    taps_copy = pltpu.make_async_copy(taps_in, taps_ref, table_sems.at[0])
    table_copy = pltpu.make_async_copy(table_in, table_ref, table_sems.at[1])
    twist_copy = pltpu.make_async_copy(twist_in, twist_ref, table_sems.at[2])
    taps_copy.start()
    for s in range(ROWS // 8):
        strip_copy(s).start()
    table_copy.start()
    twist_copy.start()
    taps_copy.wait()
    keep = lax.axis_index("tm") > 0

    def strip(s, _):
        strip_copy(s).wait()
        at = pl.multiple_of(s * 64, 64)
        rows = pl.ds(pl.multiple_of(s * 8, 8), 8)
        taps = [taps_ref[pl.ds(at + t, 8, stride=8), :] for t in range(TAPS)]
        for p in range(2):
            for c in range(2):
                x = [volt_ref[p, c, f // 8, pl.ds(at + f % 8, 8, stride=8), :] for f in range(FRAMES)]
                for f in range(HELD + AHEAD):
                    total = taps[0] * x[f]
                    for t in range(1, min(TAPS, FRAMES - f)):
                        total = total + taps[t] * x[f + t]
                    if f < HELD:
                        filt_ref[p, c, f, rows, :] = total
                    else:
                        part_ref[p, c, f - HELD, rows, :] = total
                for j in range(BACK):
                    total = taps[BACK - j] * x[0]
                    for t in range(BACK - j + 1, TAPS):
                        total = total + taps[t] * x[t - BACK + j]
                    part_ref[p, c, AHEAD + j, rows, :] = jnp.where(keep, total, 0.0)
        return 0

    lax.fori_loop(0, ROWS // 8, strip, 0)
    table_copy.wait()
    twist_copy.wait()
    sums = [None, None]
    for start in range(0, HELD, 2):
        which = [(p, f) for f in range(start, min(start + 2, HELD)) for p in range(2)]
        frames = [(filt_ref[p, 0, f], filt_ref[p, 1, f]) for p, f in which]
        for (p, f), power in zip(which, power_rows(frames, table_ref, twist_ref)):
            pow_ref[p, f] = power
            sums[p] = power if sums[p] is None else sums[p] + power
    for p in range(2):
        sum_ref[p] = sums[p]


def rim_powers(role, part_ref, came_ref, taps_ref, table_ref, twist_ref, sums, keep, store):
    slots = AHEAD if role == "ahead" else BACK
    taps = [taps_ref[pl.ds(t, ROWS, stride=8), :] for t in range(TAPS)]

    def finished(p, j):
        out = []
        for c in range(2):
            if role == "ahead":
                terms = [(FRAMES + i - HELD - j, i) for i in range(j + 1)]
                total = part_ref[p, c, j]
            else:
                terms = [(t, AHEAD - BACK + j + t) for t in range(BACK - j)]
                total = part_ref[p, c, AHEAD + j]
            rest = None
            for t, i in terms:
                term = taps[t] * came_ref[p, c, pl.ds(i, ROWS, stride=AHEAD), :]
                rest = term if rest is None else rest + term
            out.append(total + (rest if keep is None else jnp.where(keep, rest, 0.0)))
        return tuple(out)

    for start in range(0, slots, 2):
        which = [(p, j) for j in range(start, min(start + 2, slots)) for p in range(2)]
        frames = [finished(p, j) for p, j in which]
        for (p, j), power in zip(which, power_rows(frames, table_ref, twist_ref)):
            store[p, j] = power
            sums[p] = sums[p] + power
    return sums


def near_kernel(part_ref, near_ref, taps_ref, table_ref, twist_ref, had_ref, early_ref, sum_ref):
    for core, role in enumerate(("ahead", "back")):

        @pl.when(lax.axis_index("tm") % 2 == core)
        def _():
            sums = [had_ref[0], had_ref[1]]
            sums = rim_powers(role, part_ref, near_ref, taps_ref, table_ref, twist_ref, sums, None, early_ref)
            sum_ref[0], sum_ref[1] = sums


def cross_kernel(last, part_ref, cross_ref, taps_ref, table_ref, twist_ref, had_ref, early_ref, ahead_ref, back_ref, mine_ref, send_ref):
    tm = lax.axis_index("tm")
    for core, role in enumerate(("back", "ahead")):

        @pl.when(tm % 2 == core)
        def _():
            sums = [had_ref[0], had_ref[1]]
            store, keep = (back_ref, None) if core == 0 else (ahead_ref, tm < last)
            sums = rim_powers(role, part_ref, cross_ref, taps_ref, table_ref, twist_ref, sums, keep, store)
            for p in range(2):
                if core == 0:
                    ahead_ref[p] = early_ref[p]
                else:
                    back_ref[p] = early_ref[p, :BACK]
            keeps_second = kept_half() == 1
            mine_ref[...] = jnp.where(keeps_second, sums[1], sums[0])
            send_ref[...] = jnp.where(keeps_second, sums[0], sums[1])


def clean_kernel(scale, own, held_ref, ahead_ref, back_ref, sum_ref, *refs):
    out_ref, tile_ref, sems = refs[-3:]
    p = kept_half() if own else 1 - kept_half()
    base = sum_ref[...] * scale
    copies = []
    for half in range(2):
        for f in range(8 * half, 8 * half + 8):
            if f < HELD:
                power = held_ref[p, f]
            elif f < HELD + AHEAD:
                power = ahead_ref[p, f - HELD]
            else:
                power = back_ref[p, f - HELD - AHEAD]
            tile_ref[half, pl.ds(f % 8, ROWS, stride=8), :] = power - base
        copies.append(pltpu.make_async_copy(tile_ref.at[half], out_ref.at[p, half], sems.at[half]))
        copies[-1].start()
    for copy in copies:
        copy.wait()


def clean(scale, own, *args):
    far = [pl.BlockSpec(memory_space=pl.ANY)]
    return pl.pallas_call(
        functools.partial(clean_kernel, scale, own),
        out_shape=pltpu.HBM((2, 2, 8 * ROWS, LANES), jnp.float32),
        in_specs=[pl.BlockSpec(memory_space=pltpu.VMEM)] * 4 + far * (len(args) - 4),
        out_specs=far[0],
        scratch_shapes=[pltpu.VMEM((2, 8 * ROWS, LANES), jnp.float32), pltpu.SemaphoreType.DMA((2,))],
        input_output_aliases={} if own else {4: 0},
        compiler_params=pltpu.CompilerParams(vmem_limit_bytes=16 << 20),
        cost_estimate=pl.CostEstimate(flops=10**6, bytes_accessed=2 << 20, transcendentals=0),
    )(*args)


def on_core(kernel, out_shape, scratch=(), far=False, vmem=16 << 20, cost=None):
    space = pl.ANY if far else pltpu.VMEM
    where = pltpu.VMEM if far else jax.ShapeDtypeStruct
    shapes = [s if not isinstance(s, tuple) else where(s, jnp.float32) for s in out_shape]
    return lambda *args: pl.pallas_call(
        kernel,
        out_shape=shapes,
        in_specs=[pl.BlockSpec(memory_space=space)] * len(args),
        out_specs=[pl.BlockSpec(memory_space=pltpu.VMEM)] * len(out_shape),
        scratch_shapes=[pltpu.VMEM(s, jnp.float32) if isinstance(s, tuple) else s for s in scratch],
        compiler_params=pltpu.CompilerParams(vmem_limit_bytes=vmem),
        cost_estimate=cost,
    )(*args)


def in_hbm(x):
    return pltpu.with_memory_space_constraint(x, pltpu.HBM)


def by_rows(x):
    lead, frames = x.shape[:-2], x.shape[-2]
    x = x.reshape(*lead, frames, ROWS, LANES)
    return jnp.swapaxes(x, -3, -2).reshape(*lead, ROWS * frames, LANES)


def total_over_all(mine, send, back):
    cores = [(i, i ^ 1) for i in range(2 * X * Y * Z)]
    left = [(i, (i - 1) % (2 * Y)) for i in range(2 * Y)]
    sums = mine + lax.ppermute(send, BOTH, cores)
    steps = [("y", r) for r in RING4] + [("x", r) for r in RING4] + [("z", r) for r in RING8]
    for n, (axis, partner) in enumerate(steps):
        if n == 2:
            sums, back = lax.optimization_barrier((sums, back))
            back = lax.ppermute(back, "tm", left)
        sums = sums + lax.ppermute(sums, BOTH, swap_pairs(axis, partner))
        if n == 5:
            sums, back = lax.optimization_barrier((sums, back))
    return sums, lax.ppermute(sums, BOTH, cores), back


def body(voltages, filter_taps):
    devices = lax.axis_size("tm")
    table, twist = (jnp.asarray(t) for t in dft_tables())
    tiles = jnp.swapaxes(voltages[0].reshape(2, 2, 2, 8, ROWS, LANES), 3, 4)
    rim = (2, 2, ROWS, AHEAD, LANES)
    rows = (2, 2, ROWS * AHEAD, LANES)
    cross, near = on_core(
        rim_kernel,
        [rim, rim],
        scratch=[pltpu.SemaphoreType.DMA((2, 4))],
        far=True,
        cost=SHORT,
    )(in_hbm(tiles))
    near = lax.ppermute(near.reshape(rows), "tm", [(i, i ^ 1) for i in range(devices)])
    cross = lax.ppermute(cross.reshape(rows), "tm", [(i, (i + 1 if i % 2 else i - 1) % devices) for i in range(devices)])
    strips = (2, 2, 2, ROWS * 8, LANES)
    held, part, had, taps, table, twist = on_core(
        held_kernel,
        [
            (2, HELD, ROWS, LANES),
            (2, 2, AHEAD + BACK, ROWS, LANES),
            (2, ROWS, LANES),
            (ROWS * TAPS, LANES),
            pltpu.VMEM(table.shape, table.dtype),
            twist.shape,
        ],
        scratch=[
            strips,
            (2, 2, HELD, ROWS, LANES),
            pltpu.SemaphoreType.DMA((ROWS // 8,)),
            pltpu.SemaphoreType.DMA((3,)),
        ],
        far=True,
        cost=pl.CostEstimate(flops=2 * 10**9, bytes_accessed=6 << 20, transcendentals=0),
    )(in_hbm(tiles.reshape(strips)), in_hbm(by_rows(filter_taps)), in_hbm(table), in_hbm(twist))
    early, had = on_core(
        near_kernel,
        [(2, AHEAD, ROWS, LANES), (2, ROWS, LANES)],
        cost=pl.CostEstimate(flops=10**9, bytes_accessed=3 << 20, transcendentals=0),
    )(part, near, taps, table, twist, had)
    ahead, back, mine, send = on_core(
        functools.partial(cross_kernel, devices - 1),
        [(2, AHEAD, ROWS, LANES), (2, BACK, ROWS, LANES), (ROWS, LANES), (ROWS, LANES)],
    )(part, cross, taps, table, twist, had, early)
    mine, other, back = total_over_all(mine, send, back)
    scale = 1.0 / (FRAMES * devices * lax.axis_size("beam"))
    out = clean(scale, True, held, ahead, back, mine)
    out = clean(scale, False, held, ahead, back, other, out)
    out = jnp.swapaxes(out.reshape(2, 2, ROWS, 8, LANES), 2, 3)
    return out.reshape(1, 2, FRAMES, CHANNELS)


def solution(mesh):
    placed = (P("beam", None, None, "tm", None), P())
    return jax.shard_map(
        body, mesh=mesh, in_specs=placed, out_specs=P("beam", None, "tm", None), check_vma=False
    )
```

```python
import functools
import math

import jax
import jax.numpy as jnp
import ml_dtypes
import numpy as np
from jax import lax
from jax.experimental import pallas as pl
from jax.experimental.pallas import tpu as pltpu
from jax.sharding import PartitionSpec as P

LANES = 128
ROWS = 64
CHANNELS = ROWS * LANES
TAPS = 8
FRAMES = 16
HELD = 9
AHEAD = 4
BACK = 3
SHORT = pl.CostEstimate(flops=1000, bytes_accessed=1000, transcendentals=0)
BOTH = ("beam", "tm")
X, Y, Z = 4, 4, 8

RING4 = ((1, 0, 3, 2), (3, 2, 1, 0))
RING8 = ((1, 0, 3, 2, 5, 4, 7, 6), (7, 2, 1, 4, 3, 6, 5, 0), (3, 6, 5, 0, 7, 2, 1, 4))


def place(z, x, y, core):
    return ((z * X + x) * Y + y) * 2 + core


def swap_pairs(axis, partner):
    pairs = []
    for z in range(Z):
        for x in range(X):
            for y in range(Y):
                there = {
                    "z": lambda: (partner[z], x, y),
                    "x": lambda: (z, partner[x], y),
                    "y": lambda: (z, x, partner[y]),
                }[axis]()
                pairs += [(place(z, x, y, c), place(*there, 1 - c)) for c in range(2)]
    return pairs


def kept_half():
    tm, beam = lax.axis_index("tm"), lax.axis_index("beam")
    return (tm % 2 + tm // 2 + beam % X + beam // X) % 2


def in_two(table):
    high = table.astype(ml_dtypes.bfloat16)
    low = (table - high.astype(np.float64)).astype(ml_dtypes.bfloat16)
    return high, low


def dft_tables():
    q = np.arange(ROWS)
    angle = 2.0 * np.pi * (np.outer(q, q) % ROWS) / ROWS
    cos, sin = np.cos(angle), np.sin(angle)
    first = np.block([[cos, sin], [-sin, cos]])
    high, low = in_two(first)
    first = np.block([[high, high], [low, low]])
    lane = np.arange(LANES)
    order = np.concatenate([np.arange(0, LANES, 2), np.arange(1, LANES, 2)])
    angle = 2.0 * np.pi * (np.outer(order, lane) % LANES) / LANES
    cos, sin = np.cos(angle), np.sin(angle)
    second = np.block([[cos, sin], [-sin, cos]])
    second = np.concatenate(in_two(second), axis=0)
    angle = 2.0 * np.pi * np.outer(q, lane) / CHANNELS
    twist = np.stack([np.cos(angle), np.sin(angle)]).astype(np.float32)
    return np.concatenate([first, second], axis=0), twist


def halves(values):
    high = values.astype(jnp.bfloat16)
    low = (values - high.astype(jnp.float32)).astype(jnp.bfloat16)
    return high, low


def power_rows(frames, table_ref, twist_ref):
    count = len(frames)
    cols = [jnp.concatenate([re, im], axis=0) for re, im in frames]
    high, low = halves(jnp.concatenate(cols, axis=1))
    both = jnp.dot(
        table_ref[: 4 * ROWS],
        jnp.concatenate([high, low], axis=0),
        preferred_element_type=jnp.float32,
    )
    section = both[: 2 * ROWS] + both[2 * ROWS :]
    cos, sin = twist_ref[0], twist_ref[1]
    rows = []
    for g in range(count):
        re = section[:ROWS, g * LANES : (g + 1) * LANES]
        im = section[ROWS:, g * LANES : (g + 1) * LANES]
        rows.append(jnp.concatenate([re * cos + im * sin, im * cos - re * sin], axis=1))
    high, low = halves(jnp.concatenate(rows, axis=0))
    across = (((1,), (1,)), ((), ()))
    table = table_ref[4 * ROWS :]
    both = lax.dot_general(table, high, across, preferred_element_type=jnp.float32)
    both += lax.dot_general(table, low, across, preferred_element_type=jnp.float32)
    spec = both[: 2 * LANES] + both[2 * LANES :]
    re, im = spec[:LANES], spec[LANES:]
    powers = (re * re + im * im) * (1.0 / CHANNELS)
    left = lax.broadcasted_iota(jnp.int32, (ROWS, LANES), 1) < ROWS
    out = []
    for g in range(0, count, 2):
        even = powers[:ROWS, g * ROWS : (g + 2) * ROWS]
        odd = powers[ROWS:, g * ROWS : (g + 2) * ROWS]
        out.append(jnp.where(left, even, pltpu.roll(odd, ROWS, 1)))
        out.append(jnp.where(left, pltpu.roll(even, ROWS, 1), odd))
    return out


def rim_copies(volt_ref, out_ref, sems, last):
    half, at = (1, 8 - AHEAD) if last else (0, 0)
    return [
        pltpu.make_async_copy(volt_ref.at[p, c, half, :, at : at + AHEAD, :], out_ref.at[p, c], sems.at[2 * p + c])
        for p in range(2)
        for c in range(2)
    ]


def rim_kernel(volt_ref, cross_ref, near_ref, sems):
    for core in range(2):

        @pl.when(lax.axis_index("tm") % 2 == core)
        def _():
            copies = rim_copies(volt_ref, near_ref, sems.at[0], core == 0)
            copies += rim_copies(volt_ref, cross_ref, sems.at[1], core == 1)
            for copy in copies:
                copy.start()
            for copy in copies:
                copy.wait()


def held_kernel(
    volt_in, taps_in, table_in, twist_in,
    pow_ref, part_ref, sum_ref, taps_ref, table_ref, twist_ref,
    volt_ref, filt_ref, strip_sems, table_sems,
):
    def strip_copy(s):
        rows = pl.ds(pl.multiple_of(s * 64, 64), 64)
        return pltpu.make_async_copy(volt_in.at[:, :, :, rows, :], volt_ref.at[:, :, :, rows, :], strip_sems.at[s])

    taps_copy = pltpu.make_async_copy(taps_in, taps_ref, table_sems.at[0])
    table_copy = pltpu.make_async_copy(table_in, table_ref, table_sems.at[1])
    twist_copy = pltpu.make_async_copy(twist_in, twist_ref, table_sems.at[2])
    taps_copy.start()
    for s in range(ROWS // 8):
        strip_copy(s).start()
    table_copy.start()
    twist_copy.start()
    taps_copy.wait()
    keep = lax.axis_index("tm") > 0

    def strip(s, _):
        strip_copy(s).wait()
        at = pl.multiple_of(s * 64, 64)
        rows = pl.ds(pl.multiple_of(s * 8, 8), 8)
        taps = [taps_ref[pl.ds(at + t, 8, stride=8), :] for t in range(TAPS)]
        for p in range(2):
            for c in range(2):
                x = [volt_ref[p, c, f // 8, pl.ds(at + f % 8, 8, stride=8), :] for f in range(FRAMES)]
                for f in range(HELD + AHEAD):
                    total = taps[0] * x[f]
                    for t in range(1, min(TAPS, FRAMES - f)):
                        total = total + taps[t] * x[f + t]
                    if f < HELD:
                        filt_ref[p, c, f, rows, :] = total
                    else:
                        part_ref[p, c, f - HELD, rows, :] = total
                for j in range(BACK):
                    total = taps[BACK - j] * x[0]
                    for t in range(BACK - j + 1, TAPS):
                        total = total + taps[t] * x[t - BACK + j]
                    part_ref[p, c, AHEAD + j, rows, :] = jnp.where(keep, total, 0.0)
        return 0

    lax.fori_loop(0, ROWS // 8, strip, 0)
    table_copy.wait()
    twist_copy.wait()
    sums = [None, None]
    for start in range(0, HELD, 2):
        which = [(p, f) for f in range(start, min(start + 2, HELD)) for p in range(2)]
        frames = [(filt_ref[p, 0, f], filt_ref[p, 1, f]) for p, f in which]
        for (p, f), power in zip(which, power_rows(frames, table_ref, twist_ref)):
            pow_ref[p, f] = power
            sums[p] = power if sums[p] is None else sums[p] + power
    for p in range(2):
        sum_ref[p] = sums[p]


def rim_powers(role, part_ref, came_ref, taps_ref, table_ref, twist_ref, sums, keep, store):
    slots = AHEAD if role == "ahead" else BACK
    taps = [taps_ref[pl.ds(t, ROWS, stride=8), :] for t in range(TAPS)]

    def finished(p, j):
        out = []
        for c in range(2):
            if role == "ahead":
                terms = [(FRAMES + i - HELD - j, i) for i in range(j + 1)]
                total = part_ref[p, c, j]
            else:
                terms = [(t, AHEAD - BACK + j + t) for t in range(BACK - j)]
                total = part_ref[p, c, AHEAD + j]
            rest = None
            for t, i in terms:
                term = taps[t] * came_ref[p, c, pl.ds(i, ROWS, stride=AHEAD), :]
                rest = term if rest is None else rest + term
            out.append(total + (rest if keep is None else jnp.where(keep, rest, 0.0)))
        return tuple(out)

    for start in range(0, slots, 2):
        which = [(p, j) for j in range(start, min(start + 2, slots)) for p in range(2)]
        frames = [finished(p, j) for p, j in which]
        for (p, j), power in zip(which, power_rows(frames, table_ref, twist_ref)):
            store[p, j] = power
            sums[p] = sums[p] + power
    return sums


def near_kernel(part_ref, near_ref, taps_ref, table_ref, twist_ref, had_ref, early_ref, sum_ref):
    for core, role in enumerate(("ahead", "back")):

        @pl.when(lax.axis_index("tm") % 2 == core)
        def _():
            sums = [had_ref[0], had_ref[1]]
            sums = rim_powers(role, part_ref, near_ref, taps_ref, table_ref, twist_ref, sums, None, early_ref)
            sum_ref[0], sum_ref[1] = sums


def cross_kernel(last, part_ref, cross_ref, taps_ref, table_ref, twist_ref, had_ref, early_ref, ahead_ref, back_ref, mine_ref, send_ref):
    tm = lax.axis_index("tm")
    for core, role in enumerate(("back", "ahead")):

        @pl.when(tm % 2 == core)
        def _():
            sums = [had_ref[0], had_ref[1]]
            store, keep = (back_ref, None) if core == 0 else (ahead_ref, tm < last)
            sums = rim_powers(role, part_ref, cross_ref, taps_ref, table_ref, twist_ref, sums, keep, store)
            for p in range(2):
                if core == 0:
                    ahead_ref[p] = early_ref[p]
                else:
                    back_ref[p] = early_ref[p, :BACK]
            keeps_second = kept_half() == 1
            mine_ref[...] = jnp.where(keeps_second, sums[1], sums[0])
            send_ref[...] = jnp.where(keeps_second, sums[0], sums[1])


def clean_kernel(scale, *refs):
    held_ref, mine_ref, out_ref, tile_ref, sems = refs[0], refs[1], refs[-3], refs[-2], refs[-1]
    own = kept_half()
    if len(refs) == 5:
        parts = [(own, 0, mine_ref)]
    else:
        ahead_ref, back_ref, other_ref = refs[2:5]
        parts = [(own, 1, mine_ref), (1 - own, 0, other_ref), (1 - own, 1, other_ref)]
    copies = []
    for n, (p, half, sum_ref) in enumerate(parts):
        base = sum_ref[...] * scale
        for f in range(8 * half, 8 * half + 8):
            if f < HELD:
                power = held_ref[p, f]
            elif f < HELD + AHEAD:
                power = ahead_ref[p, f - HELD]
            else:
                power = back_ref[p, f - HELD - AHEAD]
            tile_ref[n, pl.ds(f % 8, ROWS, stride=8), :] = power - base
        copies.append(pltpu.make_async_copy(tile_ref.at[n], out_ref.at[p, half], sems.at[n]))
        copies[-1].start()
    for copy in copies:
        copy.wait()


def clean(scale, *args):
    first = len(args) == 2
    far = [pl.BlockSpec(memory_space=pl.ANY)]
    near = [pl.BlockSpec(memory_space=pltpu.VMEM)]
    parts = 1 if first else 3
    return pl.pallas_call(
        functools.partial(clean_kernel, scale),
        out_shape=pltpu.HBM((2, 2, 8 * ROWS, LANES), jnp.float32),
        in_specs=near * 2 if first else near * 5 + far,
        out_specs=far[0],
        scratch_shapes=[pltpu.VMEM((parts, 8 * ROWS, LANES), jnp.float32), pltpu.SemaphoreType.DMA((parts,))],
        input_output_aliases={} if first else {5: 0},
        compiler_params=pltpu.CompilerParams(vmem_limit_bytes=16 << 20),
        cost_estimate=pl.CostEstimate(flops=10**6, bytes_accessed=2 << 20, transcendentals=0),
    )(*args)


def on_core(kernel, out_shape, scratch=(), far=False, vmem=16 << 20, cost=None):
    space = pl.ANY if far else pltpu.VMEM
    where = pltpu.VMEM if far else jax.ShapeDtypeStruct
    shapes = [s if not isinstance(s, tuple) else where(s, jnp.float32) for s in out_shape]
    return lambda *args: pl.pallas_call(
        kernel,
        out_shape=shapes,
        in_specs=[pl.BlockSpec(memory_space=space)] * len(args),
        out_specs=[pl.BlockSpec(memory_space=pltpu.VMEM)] * len(out_shape),
        scratch_shapes=[pltpu.VMEM(s, jnp.float32) if isinstance(s, tuple) else s for s in scratch],
        compiler_params=pltpu.CompilerParams(vmem_limit_bytes=vmem),
        cost_estimate=cost,
    )(*args)


def in_hbm(x):
    return pltpu.with_memory_space_constraint(x, pltpu.HBM)


def by_rows(x):
    lead, frames = x.shape[:-2], x.shape[-2]
    x = x.reshape(*lead, frames, ROWS, LANES)
    return jnp.swapaxes(x, -3, -2).reshape(*lead, ROWS * frames, LANES)


def total_over_all(mine, send, back):
    cores = [(i, i ^ 1) for i in range(2 * X * Y * Z)]
    left = [(i, (i - 1) % (2 * Y)) for i in range(2 * Y)]
    sums = mine + lax.ppermute(send, BOTH, cores)
    steps = [("y", r) for r in RING4] + [("x", r) for r in RING4] + [("z", r) for r in RING8]
    for n, (axis, partner) in enumerate(steps):
        if n == 2:
            sums, back = lax.optimization_barrier((sums, back))
            back = lax.ppermute(back, "tm", left)
        sums = sums + lax.ppermute(sums, BOTH, swap_pairs(axis, partner))
    return sums, lax.ppermute(sums, BOTH, cores), back


def body(voltages, filter_taps):
    devices = lax.axis_size("tm")
    table, twist = (jnp.asarray(t) for t in dft_tables())
    tiles = jnp.swapaxes(voltages[0].reshape(2, 2, 2, 8, ROWS, LANES), 3, 4)
    rim = (2, 2, ROWS, AHEAD, LANES)
    rows = (2, 2, ROWS * AHEAD, LANES)
    cross, near = on_core(
        rim_kernel,
        [rim, rim],
        scratch=[pltpu.SemaphoreType.DMA((2, 4))],
        far=True,
        cost=SHORT,
    )(in_hbm(tiles))
    near = lax.ppermute(near.reshape(rows), "tm", [(i, i ^ 1) for i in range(devices)])
    cross = lax.ppermute(cross.reshape(rows), "tm", [(i, (i + 1 if i % 2 else i - 1) % devices) for i in range(devices)])
    strips = (2, 2, 2, ROWS * 8, LANES)
    held, part, had, taps, table, twist = on_core(
        held_kernel,
        [
            (2, HELD, ROWS, LANES),
            (2, 2, AHEAD + BACK, ROWS, LANES),
            (2, ROWS, LANES),
            (ROWS * TAPS, LANES),
            pltpu.VMEM(table.shape, table.dtype),
            twist.shape,
        ],
        scratch=[
            strips,
            (2, 2, HELD, ROWS, LANES),
            pltpu.SemaphoreType.DMA((ROWS // 8,)),
            pltpu.SemaphoreType.DMA((3,)),
        ],
        far=True,
        cost=pl.CostEstimate(flops=2 * 10**9, bytes_accessed=6 << 20, transcendentals=0),
    )(in_hbm(tiles.reshape(strips)), in_hbm(by_rows(filter_taps)), in_hbm(table), in_hbm(twist))
    early, had = on_core(
        near_kernel,
        [(2, AHEAD, ROWS, LANES), (2, ROWS, LANES)],
        cost=pl.CostEstimate(flops=10**9, bytes_accessed=3 << 20, transcendentals=0),
    )(part, near, taps, table, twist, had)
    ahead, back, mine, send = on_core(
        functools.partial(cross_kernel, devices - 1),
        [(2, AHEAD, ROWS, LANES), (2, BACK, ROWS, LANES), (ROWS, LANES), (ROWS, LANES)],
    )(part, cross, taps, table, twist, had, early)
    mine, other, back = total_over_all(mine, send, back)
    scale = 1.0 / (FRAMES * devices * lax.axis_size("beam"))
    out = clean(scale, held, mine)
    out = clean(scale, held, mine, ahead, back, other, out)
    out = jnp.swapaxes(out.reshape(2, 2, ROWS, 8, LANES), 2, 3)
    return out.reshape(1, 2, FRAMES, CHANNELS)


def solution(mesh):
    placed = (P("beam", None, None, "tm", None), P())
    return jax.shard_map(
        body, mesh=mesh, in_specs=placed, out_specs=P("beam", None, "tm", None), check_vma=False
    )
```

```python
import functools
import math

import jax
import jax.numpy as jnp
import ml_dtypes
import numpy as np
from jax import lax
from jax.experimental import pallas as pl
from jax.experimental.pallas import tpu as pltpu
from jax.sharding import PartitionSpec as P

LANES = 128
ROWS = 64
CHANNELS = ROWS * LANES
TAPS = 8
FRAMES = 16
HELD = 9
RIM = FRAMES - HELD
AHEAD = (4, 3)
BACK = (3, 4)
AHEAD_AT = (0, AHEAD[0])
BACK_AT = (0, BACK[0])
SHORT = pl.CostEstimate(flops=1000, bytes_accessed=1000, transcendentals=0)
BOTH = ("beam", "tm")
X, Y, Z = 4, 4, 8

RING4 = ((1, 0, 3, 2), (3, 2, 1, 0))
RING8 = ((1, 0, 3, 2, 5, 4, 7, 6), (7, 2, 1, 4, 3, 6, 5, 0), (3, 6, 5, 0, 7, 2, 1, 4))


def place(z, x, y, core):
    return ((z * X + x) * Y + y) * 2 + core


def swap_pairs(axis, partner):
    pairs = []
    for z in range(Z):
        for x in range(X):
            for y in range(Y):
                there = {
                    "z": lambda: (partner[z], x, y),
                    "x": lambda: (z, partner[x], y),
                    "y": lambda: (z, x, partner[y]),
                }[axis]()
                pairs += [(place(z, x, y, c), place(*there, 1 - c)) for c in range(2)]
    return pairs


def kept_half():
    tm, beam = lax.axis_index("tm"), lax.axis_index("beam")
    return (tm % 2 + tm // 2 + beam % X + beam // X) % 2


def in_two(table):
    high = table.astype(ml_dtypes.bfloat16)
    low = (table - high.astype(np.float64)).astype(ml_dtypes.bfloat16)
    return high, low


def dft_tables():
    q = np.arange(ROWS)
    angle = 2.0 * np.pi * (np.outer(q, q) % ROWS) / ROWS
    cos, sin = np.cos(angle), np.sin(angle)
    first = np.block([[cos, sin], [-sin, cos]])
    high, low = in_two(first)
    first = np.block([[high, high], [low, low]])
    lane = np.arange(LANES)
    order = np.concatenate([np.arange(0, LANES, 2), np.arange(1, LANES, 2)])
    angle = 2.0 * np.pi * (np.outer(order, lane) % LANES) / LANES
    cos, sin = np.cos(angle), np.sin(angle)
    second = np.block([[cos, sin], [-sin, cos]])
    second = np.concatenate(in_two(second), axis=0)
    angle = 2.0 * np.pi * np.outer(q, lane) / CHANNELS
    twist = np.stack([np.cos(angle), np.sin(angle)]).astype(np.float32)
    return np.concatenate([first, second], axis=0), twist


def halves(values):
    high = values.astype(jnp.bfloat16)
    low = (values - high.astype(jnp.float32)).astype(jnp.bfloat16)
    return high, low


def power_rows(frames, table_ref, twist_ref):
    count = len(frames)
    cols = [jnp.concatenate([re, im], axis=0) for re, im in frames]
    high, low = halves(jnp.concatenate(cols, axis=1))
    both = jnp.dot(
        table_ref[: 4 * ROWS],
        jnp.concatenate([high, low], axis=0),
        preferred_element_type=jnp.float32,
    )
    section = both[: 2 * ROWS] + both[2 * ROWS :]
    cos, sin = twist_ref[0], twist_ref[1]
    rows = []
    for g in range(count):
        re = section[:ROWS, g * LANES : (g + 1) * LANES]
        im = section[ROWS:, g * LANES : (g + 1) * LANES]
        rows.append(jnp.concatenate([re * cos + im * sin, im * cos - re * sin], axis=1))
    high, low = halves(jnp.concatenate(rows, axis=0))
    across = (((1,), (1,)), ((), ()))
    table = table_ref[4 * ROWS :]
    both = lax.dot_general(table, high, across, preferred_element_type=jnp.float32)
    both += lax.dot_general(table, low, across, preferred_element_type=jnp.float32)
    spec = both[: 2 * LANES] + both[2 * LANES :]
    re, im = spec[:LANES], spec[LANES:]
    powers = (re * re + im * im) * (1.0 / CHANNELS)
    left = lax.broadcasted_iota(jnp.int32, (ROWS, LANES), 1) < ROWS
    out = []
    for g in range(0, count, 2):
        if g + 1 == count:
            out.append(jnp.concatenate([powers[:ROWS, g * ROWS :], powers[ROWS:, g * ROWS :]], axis=1))
            break
        even = powers[:ROWS, g * ROWS : (g + 2) * ROWS]
        odd = powers[ROWS:, g * ROWS : (g + 2) * ROWS]
        out.append(jnp.where(left, even, pltpu.roll(odd, ROWS, 1)))
        out.append(jnp.where(left, pltpu.roll(even, ROWS, 1), odd))
    return out


def rim_copies(volt_ref, out_ref, sems, last):
    copies = []
    for p in range(2):
        for n in range(BACK[p] if last else AHEAD[p]):
            f, slot = (FRAMES - BACK[p] + n, BACK_AT[p] + n) if last else (n, AHEAD_AT[p] + n)
            for c in range(2):
                frame = volt_ref.at[p, c, f // 8, :, f % 8, :]
                copies.append(pltpu.make_async_copy(frame, out_ref.at[c, slot], sems.at[c, slot]))
    return copies


def rim_kernel(volt_ref, cross_ref, near_ref, sems):
    for core in range(2):

        @pl.when(lax.axis_index("tm") % 2 == core)
        def _():
            copies = rim_copies(volt_ref, cross_ref, sems.at[1], core == 1)
            copies += rim_copies(volt_ref, near_ref, sems.at[0], core == 0)
            for copy in copies:
                copy.start()
            for copy in copies:
                copy.wait()


def held_kernel(
    volt_in, taps_in, table_in, twist_in,
    pow_ref, part_ref, sum_ref, taps_ref, table_ref, twist_ref,
    volt_ref, filt_ref, strip_sems, table_sems,
):
    def strip_copy(s):
        rows = pl.ds(pl.multiple_of(s * 64, 64), 64)
        return pltpu.make_async_copy(volt_in.at[:, :, :, rows, :], volt_ref.at[:, :, :, rows, :], strip_sems.at[s])

    taps_copy = pltpu.make_async_copy(taps_in, taps_ref, table_sems.at[0])
    table_copy = pltpu.make_async_copy(table_in, table_ref, table_sems.at[1])
    twist_copy = pltpu.make_async_copy(twist_in, twist_ref, table_sems.at[2])
    taps_copy.start()
    for s in range(ROWS // 8):
        strip_copy(s).start()
    table_copy.start()
    twist_copy.start()
    taps_copy.wait()
    keep = lax.axis_index("tm") > 0

    def strip(s, _):
        strip_copy(s).wait()
        at = pl.multiple_of(s * 64, 64)
        rows = pl.ds(pl.multiple_of(s * 8, 8), 8)
        taps = [taps_ref[pl.ds(at + t, 8, stride=8), :] for t in range(TAPS)]
        for p in range(2):
            for c in range(2):
                x = [volt_ref[p, c, f // 8, pl.ds(at + f % 8, 8, stride=8), :] for f in range(FRAMES)]
                for f in range(HELD + AHEAD[p]):
                    total = taps[0] * x[f]
                    for t in range(1, min(TAPS, FRAMES - f)):
                        total = total + taps[t] * x[f + t]
                    if f < HELD:
                        filt_ref[p, c, f, rows, :] = total
                    else:
                        part_ref[p, c, f - HELD, rows, :] = total
                for j in range(BACK[p]):
                    reach = BACK[p] - j
                    total = taps[reach] * x[0]
                    for t in range(reach + 1, TAPS):
                        total = total + taps[t] * x[t - reach]
                    part_ref[p, c, AHEAD[p] + j, rows, :] = jnp.where(keep, total, 0.0)
        return 0

    lax.fori_loop(0, ROWS // 8, strip, 0)
    table_copy.wait()
    twist_copy.wait()
    sums = [None, None]
    for start in range(0, HELD, 2):
        which = [(p, f) for f in range(start, min(start + 2, HELD)) for p in range(2)]
        frames = [(filt_ref[p, 0, f], filt_ref[p, 1, f]) for p, f in which]
        for (p, f), power in zip(which, power_rows(frames, table_ref, twist_ref)):
            pow_ref[p, f] = power
            sums[p] = power if sums[p] is None else sums[p] + power
    for p in range(2):
        sum_ref[p] = sums[p]


def rim_powers(role, part_ref, came_ref, taps_ref, table_ref, twist_ref, sums, keep, store):
    slots, at = (AHEAD, AHEAD_AT) if role == "ahead" else (BACK, BACK_AT)
    taps = [taps_ref[pl.ds(t, ROWS, stride=8), :] for t in range(TAPS)]

    def finished(p, j):
        out = []
        for c in range(2):
            if role == "ahead":
                terms = [(RIM + i - j, i) for i in range(j + 1)]
                total = part_ref[p, c, j]
            else:
                terms = [(t, j + t) for t in range(BACK[p] - j)]
                total = part_ref[p, c, AHEAD[p] + j]
            rest = None
            for t, i in terms:
                term = taps[t] * came_ref[c, at[p] + i]
                rest = term if rest is None else rest + term
            out.append(total + (rest if keep is None else jnp.where(keep, rest, 0.0)))
        return tuple(out)

    every = [(p, j) for j in range(max(slots)) for p in range(2) if j < slots[p]]
    for start in range(0, RIM, 4):
        which = every[start : start + 4]
        frames = [finished(p, j) for p, j in which]
        for (p, j), power in zip(which, power_rows(frames, table_ref, twist_ref)):
            store[at[p] + j] = power
            sums[p] = sums[p] + power
    return sums


def near_kernel(part_ref, near_ref, taps_ref, table_ref, twist_ref, had_ref, early_ref, sum_ref):
    for core, role in enumerate(("ahead", "back")):

        @pl.when(lax.axis_index("tm") % 2 == core)
        def _():
            sums = [had_ref[0], had_ref[1]]
            sums = rim_powers(role, part_ref, near_ref, taps_ref, table_ref, twist_ref, sums, None, early_ref)
            sum_ref[0], sum_ref[1] = sums


def cross_kernel(last, part_ref, cross_ref, taps_ref, table_ref, twist_ref, had_ref, early_ref, ahead_ref, back_ref, mine_ref, send_ref):
    tm = lax.axis_index("tm")
    for core, role in enumerate(("back", "ahead")):

        @pl.when(tm % 2 == core)
        def _():
            sums = [had_ref[0], had_ref[1]]
            store, keep = (back_ref, None) if core == 0 else (ahead_ref, tm < last)
            sums = rim_powers(role, part_ref, cross_ref, taps_ref, table_ref, twist_ref, sums, keep, store)
            kept_ref = ahead_ref if core == 0 else back_ref
            kept_ref[...] = early_ref[...]
            keeps_second = kept_half() == 1
            mine_ref[...] = jnp.where(keeps_second, sums[1], sums[0])
            send_ref[...] = jnp.where(keeps_second, sums[0], sums[1])


def clean_kernel(scale, *refs):
    held_ref, mine_ref, out_ref, tile_ref, sems = refs[0], refs[1], refs[-3], refs[-2], refs[-1]
    own = kept_half()
    if len(refs) == 5:
        parts = [(own, 0, mine_ref)]
    else:
        ahead_ref, back_ref, other_ref = refs[2:5]
        parts = [(own, 1, mine_ref), (1 - own, 0, other_ref), (1 - own, 1, other_ref)]
    copies = []
    for n, (p, half, sum_ref) in enumerate(parts):
        base = sum_ref[...] * scale
        for f in range(8 * half, 8 * half + 8):
            if f < HELD:
                power = held_ref[p, f]
            elif f < HELD + min(AHEAD):
                power = ahead_ref[jnp.where(p == 0, AHEAD_AT[0], AHEAD_AT[1]) + f - HELD]
            elif f >= FRAMES - min(BACK):
                power = back_ref[jnp.where(p == 0, BACK_AT[0] + BACK[0], BACK_AT[1] + BACK[1]) + f - FRAMES]
            else:
                power = jnp.where(p == 0, ahead_ref[AHEAD_AT[0] + f - HELD], back_ref[BACK_AT[1] + f - FRAMES + BACK[1]])
            tile_ref[n, pl.ds(f % 8, ROWS, stride=8), :] = power - base
        copies.append(pltpu.make_async_copy(tile_ref.at[n], out_ref.at[p, half], sems.at[n]))
        copies[-1].start()
    for copy in copies:
        copy.wait()


def clean(scale, *args):
    first = len(args) == 2
    far = [pl.BlockSpec(memory_space=pl.ANY)]
    near = [pl.BlockSpec(memory_space=pltpu.VMEM)]
    parts = 1 if first else 3
    return pl.pallas_call(
        functools.partial(clean_kernel, scale),
        out_shape=pltpu.HBM((2, 2, 8 * ROWS, LANES), jnp.float32),
        in_specs=near * 2 if first else near * 5 + far,
        out_specs=far[0],
        scratch_shapes=[pltpu.VMEM((parts, 8 * ROWS, LANES), jnp.float32), pltpu.SemaphoreType.DMA((parts,))],
        input_output_aliases={} if first else {5: 0},
        compiler_params=pltpu.CompilerParams(vmem_limit_bytes=16 << 20),
        cost_estimate=pl.CostEstimate(flops=10**6, bytes_accessed=2 << 20, transcendentals=0),
    )(*args)


def on_core(kernel, out_shape, scratch=(), far=False, vmem=16 << 20, cost=None):
    space = pl.ANY if far else pltpu.VMEM
    where = pltpu.VMEM if far else jax.ShapeDtypeStruct
    shapes = [s if not isinstance(s, tuple) else where(s, jnp.float32) for s in out_shape]
    return lambda *args: pl.pallas_call(
        kernel,
        out_shape=shapes,
        in_specs=[pl.BlockSpec(memory_space=space)] * len(args),
        out_specs=[pl.BlockSpec(memory_space=pltpu.VMEM)] * len(out_shape),
        scratch_shapes=[pltpu.VMEM(s, jnp.float32) if isinstance(s, tuple) else s for s in scratch],
        compiler_params=pltpu.CompilerParams(vmem_limit_bytes=vmem),
        cost_estimate=cost,
    )(*args)


def in_hbm(x):
    return pltpu.with_memory_space_constraint(x, pltpu.HBM)


def by_rows(x):
    lead, frames = x.shape[:-2], x.shape[-2]
    x = x.reshape(*lead, frames, ROWS, LANES)
    return jnp.swapaxes(x, -3, -2).reshape(*lead, ROWS * frames, LANES)


def total_over_all(mine, send, back):
    cores = [(i, i ^ 1) for i in range(2 * X * Y * Z)]
    left = [(i, (i - 1) % (2 * Y)) for i in range(2 * Y)]
    sums = mine + lax.ppermute(send, BOTH, cores)
    steps = [("x", r) for r in RING4] + [("y", r) for r in RING4] + [("z", r) for r in RING8]
    for n, (axis, partner) in enumerate(steps):
        if n == 1:
            sums, back = lax.optimization_barrier((sums, back))
            back = lax.ppermute(back, "tm", left)
        sums = sums + lax.ppermute(sums, BOTH, swap_pairs(axis, partner))
    return sums, lax.ppermute(sums, BOTH, cores), back


def body(voltages, filter_taps):
    devices = lax.axis_size("tm")
    table, twist = (jnp.asarray(t) for t in dft_tables())
    tiles = jnp.swapaxes(voltages[0].reshape(2, 2, 2, 8, ROWS, LANES), 3, 4)
    rim = (2, RIM, ROWS, LANES)
    cross, near = on_core(
        rim_kernel,
        [rim, rim],
        scratch=[pltpu.SemaphoreType.DMA((2, 2, RIM))],
        far=True,
        cost=SHORT,
    )(in_hbm(tiles))
    near = lax.ppermute(near, "tm", [(i, i ^ 1) for i in range(devices)])
    cross = lax.ppermute(cross, "tm", [(i, (i + 1 if i % 2 else i - 1) % devices) for i in range(devices)])
    strips = (2, 2, 2, ROWS * 8, LANES)
    held, part, had, taps, table, twist = on_core(
        held_kernel,
        [
            (2, HELD, ROWS, LANES),
            (2, 2, RIM, ROWS, LANES),
            (2, ROWS, LANES),
            (ROWS * TAPS, LANES),
            pltpu.VMEM(table.shape, table.dtype),
            twist.shape,
        ],
        scratch=[
            strips,
            (2, 2, HELD, ROWS, LANES),
            pltpu.SemaphoreType.DMA((ROWS // 8,)),
            pltpu.SemaphoreType.DMA((3,)),
        ],
        far=True,
        cost=pl.CostEstimate(flops=2 * 10**9, bytes_accessed=6 << 20, transcendentals=0),
    )(in_hbm(tiles.reshape(strips)), in_hbm(by_rows(filter_taps)), in_hbm(table), in_hbm(twist))
    early, had = on_core(
        near_kernel,
        [(RIM, ROWS, LANES), (2, ROWS, LANES)],
        cost=pl.CostEstimate(flops=10**9, bytes_accessed=3 << 20, transcendentals=0),
    )(part, near, taps, table, twist, had)
    ahead, back, mine, send = on_core(
        functools.partial(cross_kernel, devices - 1),
        [(RIM, ROWS, LANES), (RIM, ROWS, LANES), (ROWS, LANES), (ROWS, LANES)],
    )(part, cross, taps, table, twist, had, early)
    mine, other, back = total_over_all(mine, send, back)
    scale = 1.0 / (FRAMES * devices * lax.axis_size("beam"))
    out = clean(scale, held, mine)
    out = clean(scale, held, mine, ahead, back, other, out)
    out = jnp.swapaxes(out.reshape(2, 2, ROWS, 8, LANES), 2, 3)
    return out.reshape(1, 2, FRAMES, CHANNELS)


def solution(mesh):
    placed = (P("beam", None, None, "tm", None), P())
    return jax.shard_map(
        body, mesh=mesh, in_specs=placed, out_specs=P("beam", None, "tm", None), check_vma=False
    )
```

```python
import functools
import math

import jax
import jax.numpy as jnp
import ml_dtypes
import numpy as np
from jax import lax
from jax.experimental import pallas as pl
from jax.experimental.pallas import tpu as pltpu
from jax.sharding import PartitionSpec as P

LANES = 128
ROWS = 64
CHANNELS = ROWS * LANES
TAPS = 8
FRAMES = 16
HELD = 9
RIM = FRAMES - HELD
AHEAD = (4, 3)
BACK = (3, 4)
AHEAD_AT = (0, AHEAD[0])
BACK_AT = (0, BACK[0])
SHORT = pl.CostEstimate(flops=1000, bytes_accessed=1000, transcendentals=0)
BOTH = ("beam", "tm")
X, Y, Z = 4, 4, 8

RING4 = ((1, 0, 3, 2), (3, 2, 1, 0))
RING8 = ((1, 0, 3, 2, 5, 4, 7, 6), (2, 3, 0, 1, 6, 7, 4, 5), (7, 6, 5, 4, 3, 2, 1, 0))


def place(z, x, y, core):
    return ((z * X + x) * Y + y) * 2 + core


def swap_pairs(axis, partner):
    pairs = []
    for z in range(Z):
        for x in range(X):
            for y in range(Y):
                there = {
                    "z": lambda: (partner[z], x, y),
                    "x": lambda: (z, partner[x], y),
                    "y": lambda: (z, x, partner[y]),
                }[axis]()
                pairs += [(place(z, x, y, c), place(*there, 1 - c)) for c in range(2)]
    return pairs


def kept_half():
    tm, beam = lax.axis_index("tm"), lax.axis_index("beam")
    z = beam // X
    return (tm % 2 + tm // 2 + beam % X + z + z // 2 + z // 4) % 2


def in_two(table):
    high = table.astype(ml_dtypes.bfloat16)
    low = (table - high.astype(np.float64)).astype(ml_dtypes.bfloat16)
    return high, low


def dft_tables():
    q = np.arange(ROWS)
    angle = 2.0 * np.pi * (np.outer(q, q) % ROWS) / ROWS
    cos, sin = np.cos(angle), np.sin(angle)
    first = np.block([[cos, sin], [-sin, cos]])
    high, low = in_two(first)
    first = np.block([[high, high], [low, low]])
    lane = np.arange(LANES)
    order = np.concatenate([np.arange(0, LANES, 2), np.arange(1, LANES, 2)])
    angle = 2.0 * np.pi * (np.outer(order, lane) % LANES) / LANES
    cos, sin = np.cos(angle), np.sin(angle)
    second = np.block([[cos, sin], [-sin, cos]])
    second = np.concatenate(in_two(second), axis=0)
    angle = 2.0 * np.pi * np.outer(q, lane) / CHANNELS
    twist = np.stack([np.cos(angle), np.sin(angle)]).astype(np.float32)
    return np.concatenate([first, second], axis=0), twist


def halves(values):
    high = values.astype(jnp.bfloat16)
    low = (values - high.astype(jnp.float32)).astype(jnp.bfloat16)
    return high, low


def power_rows(frames, table_ref, twist_ref):
    count = len(frames)
    cols = [jnp.concatenate([re, im], axis=0) for re, im in frames]
    high, low = halves(jnp.concatenate(cols, axis=1))
    both = jnp.dot(
        table_ref[: 4 * ROWS],
        jnp.concatenate([high, low], axis=0),
        preferred_element_type=jnp.float32,
    )
    section = both[: 2 * ROWS] + both[2 * ROWS :]
    cos, sin = twist_ref[0], twist_ref[1]
    rows = []
    for g in range(count):
        re = section[:ROWS, g * LANES : (g + 1) * LANES]
        im = section[ROWS:, g * LANES : (g + 1) * LANES]
        rows.append(jnp.concatenate([re * cos + im * sin, im * cos - re * sin], axis=1))
    high, low = halves(jnp.concatenate(rows, axis=0))
    across = (((1,), (1,)), ((), ()))
    table = table_ref[4 * ROWS :]
    both = lax.dot_general(table, high, across, preferred_element_type=jnp.float32)
    both += lax.dot_general(table, low, across, preferred_element_type=jnp.float32)
    spec = both[: 2 * LANES] + both[2 * LANES :]
    re, im = spec[:LANES], spec[LANES:]
    powers = (re * re + im * im) * (1.0 / CHANNELS)
    left = lax.broadcasted_iota(jnp.int32, (ROWS, LANES), 1) < ROWS
    out = []
    for g in range(0, count, 2):
        if g + 1 == count:
            out.append(jnp.concatenate([powers[:ROWS, g * ROWS :], powers[ROWS:, g * ROWS :]], axis=1))
            break
        even = powers[:ROWS, g * ROWS : (g + 2) * ROWS]
        odd = powers[ROWS:, g * ROWS : (g + 2) * ROWS]
        out.append(jnp.where(left, even, pltpu.roll(odd, ROWS, 1)))
        out.append(jnp.where(left, pltpu.roll(even, ROWS, 1), odd))
    return out


def rim_copies(volt_ref, out_ref, sems, last):
    copies = []
    for p in range(2):
        for n in range(BACK[p] if last else AHEAD[p]):
            f, slot = (FRAMES - BACK[p] + n, BACK_AT[p] + n) if last else (n, AHEAD_AT[p] + n)
            for c in range(2):
                frame = volt_ref.at[p, c, f // 8, :, f % 8, :]
                copies.append(pltpu.make_async_copy(frame, out_ref.at[c, slot], sems.at[c, slot]))
    return copies


def rim_kernel(volt_ref, cross_ref, near_ref, sems):
    for core in range(2):

        @pl.when(lax.axis_index("tm") % 2 == core)
        def _():
            copies = rim_copies(volt_ref, cross_ref, sems.at[1], core == 1)
            copies += rim_copies(volt_ref, near_ref, sems.at[0], core == 0)
            for copy in copies:
                copy.start()
            for copy in copies:
                copy.wait()


def held_kernel(
    volt_in, taps_in, table_in, twist_in,
    pow_ref, part_ref, sum_ref, taps_ref, table_ref, twist_ref,
    volt_ref, filt_ref, strip_sems, table_sems,
):
    def strip_copy(s):
        rows = pl.ds(pl.multiple_of(s * 64, 64), 64)
        return pltpu.make_async_copy(volt_in.at[:, :, :, rows, :], volt_ref.at[:, :, :, rows, :], strip_sems.at[s])

    taps_copy = pltpu.make_async_copy(taps_in, taps_ref, table_sems.at[0])
    table_copy = pltpu.make_async_copy(table_in, table_ref, table_sems.at[1])
    twist_copy = pltpu.make_async_copy(twist_in, twist_ref, table_sems.at[2])
    taps_copy.start()
    for s in range(ROWS // 8):
        strip_copy(s).start()
    table_copy.start()
    twist_copy.start()
    taps_copy.wait()
    keep = lax.axis_index("tm") > 0

    def strip(s, _):
        strip_copy(s).wait()
        at = pl.multiple_of(s * 64, 64)
        rows = pl.ds(pl.multiple_of(s * 8, 8), 8)
        taps = [taps_ref[pl.ds(at + t, 8, stride=8), :] for t in range(TAPS)]
        for p in range(2):
            for c in range(2):
                x = [volt_ref[p, c, f // 8, pl.ds(at + f % 8, 8, stride=8), :] for f in range(FRAMES)]
                for f in range(HELD + AHEAD[p]):
                    total = taps[0] * x[f]
                    for t in range(1, min(TAPS, FRAMES - f)):
                        total = total + taps[t] * x[f + t]
                    if f < HELD:
                        filt_ref[p, c, f, rows, :] = total
                    else:
                        part_ref[p, c, f - HELD, rows, :] = total
                for j in range(BACK[p]):
                    reach = BACK[p] - j
                    total = taps[reach] * x[0]
                    for t in range(reach + 1, TAPS):
                        total = total + taps[t] * x[t - reach]
                    part_ref[p, c, AHEAD[p] + j, rows, :] = jnp.where(keep, total, 0.0)
        return 0

    lax.fori_loop(0, ROWS // 8, strip, 0)
    table_copy.wait()
    twist_copy.wait()
    sums = [None, None]
    for start in range(0, HELD, 2):
        which = [(p, f) for f in range(start, min(start + 2, HELD)) for p in range(2)]
        frames = [(filt_ref[p, 0, f], filt_ref[p, 1, f]) for p, f in which]
        for (p, f), power in zip(which, power_rows(frames, table_ref, twist_ref)):
            pow_ref[p, f] = power
            sums[p] = power if sums[p] is None else sums[p] + power
    for p in range(2):
        sum_ref[p] = sums[p]


def rim_powers(role, part_ref, came_ref, taps_ref, table_ref, twist_ref, sums, keep, store):
    slots, at = (AHEAD, AHEAD_AT) if role == "ahead" else (BACK, BACK_AT)
    taps = [taps_ref[pl.ds(t, ROWS, stride=8), :] for t in range(TAPS)]

    def finished(p, j):
        out = []
        for c in range(2):
            if role == "ahead":
                terms = [(RIM + i - j, i) for i in range(j + 1)]
                total = part_ref[p, c, j]
            else:
                terms = [(t, j + t) for t in range(BACK[p] - j)]
                total = part_ref[p, c, AHEAD[p] + j]
            rest = None
            for t, i in terms:
                term = taps[t] * came_ref[c, at[p] + i]
                rest = term if rest is None else rest + term
            out.append(total + (rest if keep is None else jnp.where(keep, rest, 0.0)))
        return tuple(out)

    every = [(p, j) for j in range(max(slots)) for p in range(2) if j < slots[p]]
    for start in range(0, RIM, 4):
        which = every[start : start + 4]
        frames = [finished(p, j) for p, j in which]
        for (p, j), power in zip(which, power_rows(frames, table_ref, twist_ref)):
            store[at[p] + j] = power
            sums[p] = sums[p] + power
    return sums


def near_kernel(part_ref, near_ref, taps_ref, table_ref, twist_ref, had_ref, early_ref, sum_ref):
    for core, role in enumerate(("ahead", "back")):

        @pl.when(lax.axis_index("tm") % 2 == core)
        def _():
            sums = [had_ref[0], had_ref[1]]
            sums = rim_powers(role, part_ref, near_ref, taps_ref, table_ref, twist_ref, sums, None, early_ref)
            sum_ref[0], sum_ref[1] = sums


def cross_kernel(last, part_ref, cross_ref, taps_ref, table_ref, twist_ref, had_ref, early_ref, ahead_ref, back_ref, mine_ref, send_ref):
    tm = lax.axis_index("tm")
    for core, role in enumerate(("back", "ahead")):

        @pl.when(tm % 2 == core)
        def _():
            sums = [had_ref[0], had_ref[1]]
            store, keep = (back_ref, None) if core == 0 else (ahead_ref, tm < last)
            sums = rim_powers(role, part_ref, cross_ref, taps_ref, table_ref, twist_ref, sums, keep, store)
            kept_ref = ahead_ref if core == 0 else back_ref
            kept_ref[...] = early_ref[...]
            keeps_second = kept_half() == 1
            mine_ref[...] = jnp.where(keeps_second, sums[1], sums[0])
            send_ref[...] = jnp.where(keeps_second, sums[0], sums[1])


def clean_kernel(scale, *refs):
    held_ref, mine_ref, out_ref, tile_ref, sems = refs[0], refs[1], refs[-3], refs[-2], refs[-1]
    own = kept_half()
    if len(refs) == 5:
        parts = [(own, 0, mine_ref)]
    else:
        ahead_ref, back_ref, other_ref = refs[2:5]
        parts = [(own, 1, mine_ref), (1 - own, 0, other_ref), (1 - own, 1, other_ref)]
    copies = []
    for n, (p, half, sum_ref) in enumerate(parts):
        base = sum_ref[...] * scale
        for f in range(8 * half, 8 * half + 8):
            if f < HELD:
                power = held_ref[p, f]
            elif f < HELD + min(AHEAD):
                power = ahead_ref[jnp.where(p == 0, AHEAD_AT[0], AHEAD_AT[1]) + f - HELD]
            elif f >= FRAMES - min(BACK):
                power = back_ref[jnp.where(p == 0, BACK_AT[0] + BACK[0], BACK_AT[1] + BACK[1]) + f - FRAMES]
            else:
                power = jnp.where(p == 0, ahead_ref[AHEAD_AT[0] + f - HELD], back_ref[BACK_AT[1] + f - FRAMES + BACK[1]])
            tile_ref[n, pl.ds(f % 8, ROWS, stride=8), :] = power - base
        copies.append(pltpu.make_async_copy(tile_ref.at[n], out_ref.at[p, half], sems.at[n]))
        copies[-1].start()
    for copy in copies:
        copy.wait()


def clean(scale, *args):
    first = len(args) == 2
    far = [pl.BlockSpec(memory_space=pl.ANY)]
    near = [pl.BlockSpec(memory_space=pltpu.VMEM)]
    parts = 1 if first else 3
    return pl.pallas_call(
        functools.partial(clean_kernel, scale),
        out_shape=pltpu.HBM((2, 2, 8 * ROWS, LANES), jnp.float32),
        in_specs=near * 2 if first else near * 5 + far,
        out_specs=far[0],
        scratch_shapes=[pltpu.VMEM((parts, 8 * ROWS, LANES), jnp.float32), pltpu.SemaphoreType.DMA((parts,))],
        input_output_aliases={} if first else {5: 0},
        compiler_params=pltpu.CompilerParams(vmem_limit_bytes=16 << 20),
        cost_estimate=pl.CostEstimate(flops=10**6, bytes_accessed=2 << 20, transcendentals=0),
    )(*args)


def on_core(kernel, out_shape, scratch=(), far=False, vmem=16 << 20, cost=None):
    space = pl.ANY if far else pltpu.VMEM
    where = pltpu.VMEM if far else jax.ShapeDtypeStruct
    shapes = [s if not isinstance(s, tuple) else where(s, jnp.float32) for s in out_shape]
    return lambda *args: pl.pallas_call(
        kernel,
        out_shape=shapes,
        in_specs=[pl.BlockSpec(memory_space=space)] * len(args),
        out_specs=[pl.BlockSpec(memory_space=pltpu.VMEM)] * len(out_shape),
        scratch_shapes=[pltpu.VMEM(s, jnp.float32) if isinstance(s, tuple) else s for s in scratch],
        compiler_params=pltpu.CompilerParams(vmem_limit_bytes=vmem),
        cost_estimate=cost,
    )(*args)


def in_hbm(x):
    return pltpu.with_memory_space_constraint(x, pltpu.HBM)


def by_rows(x):
    lead, frames = x.shape[:-2], x.shape[-2]
    x = x.reshape(*lead, frames, ROWS, LANES)
    return jnp.swapaxes(x, -3, -2).reshape(*lead, ROWS * frames, LANES)


def total_over_all(mine, send, back):
    cores = [(i, i ^ 1) for i in range(2 * X * Y * Z)]
    left = [(i, (i - 1) % (2 * Y)) for i in range(2 * Y)]
    sums = mine + lax.ppermute(send, BOTH, cores)
    steps = [("x", r) for r in RING4] + [("y", r) for r in RING4] + [("z", r) for r in RING8]
    for n, (axis, partner) in enumerate(steps):
        if n == 1:
            sums, back = lax.optimization_barrier((sums, back))
            back = lax.ppermute(back, "tm", left)
        sums = sums + lax.ppermute(sums, BOTH, swap_pairs(axis, partner))
    return sums, lax.ppermute(sums, BOTH, cores), back


def body(voltages, filter_taps):
    devices = lax.axis_size("tm")
    table, twist = (jnp.asarray(t) for t in dft_tables())
    tiles = jnp.swapaxes(voltages[0].reshape(2, 2, 2, 8, ROWS, LANES), 3, 4)
    rim = (2, RIM, ROWS, LANES)
    cross, near = on_core(
        rim_kernel,
        [rim, rim],
        scratch=[pltpu.SemaphoreType.DMA((2, 2, RIM))],
        far=True,
        cost=SHORT,
    )(in_hbm(tiles))
    near = lax.ppermute(near, "tm", [(i, i ^ 1) for i in range(devices)])
    cross = lax.ppermute(cross, "tm", [(i, (i + 1 if i % 2 else i - 1) % devices) for i in range(devices)])
    strips = (2, 2, 2, ROWS * 8, LANES)
    held, part, had, taps, table, twist = on_core(
        held_kernel,
        [
            (2, HELD, ROWS, LANES),
            (2, 2, RIM, ROWS, LANES),
            (2, ROWS, LANES),
            (ROWS * TAPS, LANES),
            pltpu.VMEM(table.shape, table.dtype),
            twist.shape,
        ],
        scratch=[
            strips,
            (2, 2, HELD, ROWS, LANES),
            pltpu.SemaphoreType.DMA((ROWS // 8,)),
            pltpu.SemaphoreType.DMA((3,)),
        ],
        far=True,
        cost=pl.CostEstimate(flops=2 * 10**9, bytes_accessed=6 << 20, transcendentals=0),
    )(in_hbm(tiles.reshape(strips)), in_hbm(by_rows(filter_taps)), in_hbm(table), in_hbm(twist))
    early, had = on_core(
        near_kernel,
        [(RIM, ROWS, LANES), (2, ROWS, LANES)],
        cost=pl.CostEstimate(flops=10**9, bytes_accessed=3 << 20, transcendentals=0),
    )(part, near, taps, table, twist, had)
    ahead, back, mine, send = on_core(
        functools.partial(cross_kernel, devices - 1),
        [(RIM, ROWS, LANES), (RIM, ROWS, LANES), (ROWS, LANES), (ROWS, LANES)],
    )(part, cross, taps, table, twist, had, early)
    mine, other, back = total_over_all(mine, send, back)
    scale = 1.0 / (FRAMES * devices * lax.axis_size("beam"))
    out = clean(scale, held, mine)
    out = clean(scale, held, mine, ahead, back, other, out)
    out = jnp.swapaxes(out.reshape(2, 2, ROWS, 8, LANES), 2, 3)
    return out.reshape(1, 2, FRAMES, CHANNELS)


def solution(mesh):
    placed = (P("beam", None, None, "tm", None), P())
    return jax.shard_map(
        body, mesh=mesh, in_specs=placed, out_specs=P("beam", None, "tm", None), check_vma=False
    )
```

```python
import functools
import math

import jax
import jax.numpy as jnp
import ml_dtypes
import numpy as np
from jax import lax
from jax.experimental import pallas as pl
from jax.experimental.pallas import tpu as pltpu
from jax.sharding import PartitionSpec as P

LANES = 128
ROWS = 64
CHANNELS = ROWS * LANES
TAPS = 8
FRAMES = 16
HELD = 9
RIM = FRAMES - HELD
SHORT = pl.CostEstimate(flops=1000, bytes_accessed=1000, transcendentals=0)
BOTH = ("beam", "tm")
X, Y, Z = 4, 4, 8

RING4 = ((1, 0, 3, 2), (3, 2, 1, 0))
RING8 = ((1, 0, 3, 2, 5, 4, 7, 6), (2, 3, 0, 1, 6, 7, 4, 5), (7, 6, 5, 4, 3, 2, 1, 0))


def place(z, x, y, core):
    return ((z * X + x) * Y + y) * 2 + core


def swap_pairs(axis, partner):
    pairs = []
    for z in range(Z):
        for x in range(X):
            for y in range(Y):
                there = {
                    "z": lambda: (partner[z], x, y),
                    "x": lambda: (z, partner[x], y),
                    "y": lambda: (z, x, partner[y]),
                }[axis]()
                pairs += [(place(z, x, y, c), place(*there, c if axis == "y" else 1 - c)) for c in range(2)]
    return pairs


def kept_half():
    tm, beam = lax.axis_index("tm"), lax.axis_index("beam")
    z = beam // X
    return (tm + beam % X + z + z // 2 + z // 4) % 2


def in_two(table):
    high = table.astype(ml_dtypes.bfloat16)
    low = (table - high.astype(np.float64)).astype(ml_dtypes.bfloat16)
    return high, low


def dft_tables():
    q = np.arange(ROWS)
    angle = 2.0 * np.pi * (np.outer(q, q) % ROWS) / ROWS
    cos, sin = np.cos(angle), np.sin(angle)
    first = np.block([[cos, sin], [-sin, cos]])
    high, low = in_two(first)
    first = np.block([[high, high], [low, low]])
    lane = np.arange(LANES)
    order = np.concatenate([np.arange(0, LANES, 2), np.arange(1, LANES, 2)])
    angle = 2.0 * np.pi * (np.outer(order, lane) % LANES) / LANES
    cos, sin = np.cos(angle), np.sin(angle)
    second = np.block([[cos, sin], [-sin, cos]])
    second = np.concatenate(in_two(second), axis=0)
    angle = 2.0 * np.pi * np.outer(q, lane) / CHANNELS
    twist = np.stack([np.cos(angle), np.sin(angle)]).astype(np.float32)
    return np.concatenate([first, second], axis=0), twist


def halves(values):
    high = values.astype(jnp.bfloat16)
    low = (values - high.astype(jnp.float32)).astype(jnp.bfloat16)
    return high, low


def power_rows(frames, table_ref, twist_ref):
    count = len(frames)
    cols = [jnp.concatenate([re, im], axis=0) for re, im in frames]
    high, low = halves(jnp.concatenate(cols, axis=1))
    both = jnp.dot(
        table_ref[: 4 * ROWS],
        jnp.concatenate([high, low], axis=0),
        preferred_element_type=jnp.float32,
    )
    section = both[: 2 * ROWS] + both[2 * ROWS :]
    cos, sin = twist_ref[0], twist_ref[1]
    rows = []
    for g in range(count):
        re = section[:ROWS, g * LANES : (g + 1) * LANES]
        im = section[ROWS:, g * LANES : (g + 1) * LANES]
        rows.append(jnp.concatenate([re * cos + im * sin, im * cos - re * sin], axis=1))
    high, low = halves(jnp.concatenate(rows, axis=0))
    across = (((1,), (1,)), ((), ()))
    table = table_ref[4 * ROWS :]
    both = lax.dot_general(table, high, across, preferred_element_type=jnp.float32)
    both += lax.dot_general(table, low, across, preferred_element_type=jnp.float32)
    spec = both[: 2 * LANES] + both[2 * LANES :]
    re, im = spec[:LANES], spec[LANES:]
    powers = (re * re + im * im) * (1.0 / CHANNELS)
    left = lax.broadcasted_iota(jnp.int32, (ROWS, LANES), 1) < ROWS
    out = []
    for g in range(0, count, 2):
        if g + 1 == count:
            out.append(jnp.concatenate([powers[:ROWS, g * ROWS :], powers[ROWS:, g * ROWS :]], axis=1))
            break
        even = powers[:ROWS, g * ROWS : (g + 2) * ROWS]
        odd = powers[ROWS:, g * ROWS : (g + 2) * ROWS]
        out.append(jnp.where(left, even, pltpu.roll(odd, ROWS, 1)))
        out.append(jnp.where(left, pltpu.roll(even, ROWS, 1), odd))
    return out


def rim_copies(volt_ref, out_ref, sems, last):
    p = 1 - kept_half()
    copies = []
    for n in range(RIM):
        f = HELD + n if last else n
        for c in range(2):
            frame = volt_ref.at[p, c, f // 8, :, f % 8, :]
            copies.append(pltpu.make_async_copy(frame, out_ref.at[c, n], sems.at[c, n]))
    return copies


def rim_kernel(volt_ref, cross_ref, near_ref, sems):
    for core in range(2):

        @pl.when(lax.axis_index("tm") % 2 == core)
        def _():
            copies = rim_copies(volt_ref, cross_ref, sems.at[1], core == 1)
            copies += rim_copies(volt_ref, near_ref, sems.at[0], core == 0)
            for copy in copies:
                copy.start()
            for copy in copies:
                copy.wait()


def held_kernel(
    volt_in, taps_in, table_in, twist_in,
    pow_ref, part_ref, mine_ref, send_ref, taps_ref, table_ref, twist_ref,
    volt_ref, filt_ref, strip_sems, table_sems,
):
    def strip_copy(s):
        rows = pl.ds(pl.multiple_of(s * 64, 64), 64)
        return pltpu.make_async_copy(volt_in.at[:, :, :, rows, :], volt_ref.at[:, :, :, rows, :], strip_sems.at[s])

    taps_copy = pltpu.make_async_copy(taps_in, taps_ref, table_sems.at[0])
    table_copy = pltpu.make_async_copy(table_in, table_ref, table_sems.at[1])
    twist_copy = pltpu.make_async_copy(twist_in, twist_ref, table_sems.at[2])
    taps_copy.start()
    for s in range(ROWS // 8):
        strip_copy(s).start()
    table_copy.start()
    twist_copy.start()
    taps_copy.wait()
    keep = lax.axis_index("tm") > 0
    own = kept_half()

    def strip(s, _):
        strip_copy(s).wait()
        at = pl.multiple_of(s * 64, 64)
        rows = pl.ds(pl.multiple_of(s * 8, 8), 8)
        taps = [taps_ref[pl.ds(at + t, 8, stride=8), :] for t in range(TAPS)]
        for p in range(2):
            for c in range(2):
                x = [volt_ref[p, c, f // 8, pl.ds(at + f % 8, 8, stride=8), :] for f in range(FRAMES)]
                for f in range(HELD):
                    total = taps[0] * x[f]
                    for t in range(1, TAPS):
                        total = total + taps[t] * x[f + t]
                    filt_ref[p, c, f, rows, :] = total
        for c in range(2):
            x = [volt_ref[own, c, f // 8, pl.ds(at + f % 8, 8, stride=8), :] for f in range(FRAMES)]
            for j in range(RIM):
                total = taps[0] * x[HELD + j]
                for t in range(1, RIM - j):
                    total = total + taps[t] * x[HELD + j + t]
                part_ref[c, j, rows, :] = total
                reach = RIM - j
                total = taps[reach] * x[0]
                for t in range(reach + 1, TAPS):
                    total = total + taps[t] * x[t - reach]
                part_ref[c, RIM + j, rows, :] = jnp.where(keep, total, 0.0)
        return 0

    lax.fori_loop(0, ROWS // 8, strip, 0)
    table_copy.wait()
    twist_copy.wait()
    sums = [None, None]
    for start in range(0, HELD, 2):
        which = [(p, f) for f in range(start, min(start + 2, HELD)) for p in range(2)]
        frames = [(filt_ref[p, 0, f], filt_ref[p, 1, f]) for p, f in which]
        for (p, f), power in zip(which, power_rows(frames, table_ref, twist_ref)):
            pow_ref[p, f] = power
            sums[p] = power if sums[p] is None else sums[p] + power
    mine_ref[...] = jnp.where(own == 1, sums[1], sums[0])
    send_ref[...] = jnp.where(own == 1, sums[0], sums[1])


def rim_powers(role, part_ref, came_ref, taps_ref, table_ref, twist_ref, total_sum, keep, store):
    taps = [taps_ref[pl.ds(t, ROWS, stride=8), :] for t in range(TAPS)]

    def finished(j):
        out = []
        for c in range(2):
            if role == "ahead":
                terms = [(RIM + i - j, i) for i in range(j + 1)]
                total = part_ref[c, j]
            else:
                terms = [(t, j + t) for t in range(RIM - j)]
                total = part_ref[c, RIM + j]
            rest = None
            for t, i in terms:
                term = taps[t] * came_ref[c, i]
                rest = term if rest is None else rest + term
            out.append(total + (rest if keep is None else jnp.where(keep, rest, 0.0)))
        return tuple(out)

    for start in range(0, RIM, 4):
        which = range(start, min(start + 4, RIM))
        for j, power in zip(which, power_rows([finished(j) for j in which], table_ref, twist_ref)):
            store[j] = power
            total_sum = total_sum + power
    return total_sum


def near_kernel(part_ref, near_ref, taps_ref, table_ref, twist_ref, had_ref, early_ref, sum_ref):
    for core, role in enumerate(("ahead", "back")):

        @pl.when(lax.axis_index("tm") % 2 == core)
        def _():
            sum_ref[...] = rim_powers(
                role, part_ref, near_ref, taps_ref, table_ref, twist_ref, had_ref[...], None, early_ref
            )


def cross_kernel(last, part_ref, cross_ref, taps_ref, table_ref, twist_ref, had_ref, other_ref, early_ref, ahead_ref, back_ref, sum_ref):
    tm = lax.axis_index("tm")
    for core, role in enumerate(("back", "ahead")):

        @pl.when(tm % 2 == core)
        def _():
            store, keep = (back_ref, None) if core == 0 else (ahead_ref, tm < last)
            had = had_ref[...] + other_ref[...]
            sum_ref[...] = rim_powers(
                role, part_ref, cross_ref, taps_ref, table_ref, twist_ref, had, keep, store
            )
            kept_ref = ahead_ref if core == 0 else back_ref
            kept_ref[...] = early_ref[...]


def clean_kernel(scale, held_ref, rim_ref, sum_ref, *refs):
    out_ref, tile_ref, sems = refs[-3:]
    p = kept_half() if len(refs) == 3 else 1 - kept_half()
    base = sum_ref[...] * scale
    copies = []
    for half in range(2):
        for f in range(8 * half, 8 * half + 8):
            power = held_ref[p, f] if f < HELD else rim_ref[f - HELD]
            tile_ref[half, pl.ds(f % 8, ROWS, stride=8), :] = power - base
        copies.append(pltpu.make_async_copy(tile_ref.at[half], out_ref.at[p, half], sems.at[half]))
        copies[-1].start()
    for copy in copies:
        copy.wait()


def clean(scale, *args):
    far = [pl.BlockSpec(memory_space=pl.ANY)]
    return pl.pallas_call(
        functools.partial(clean_kernel, scale),
        out_shape=pltpu.HBM((2, 2, 8 * ROWS, LANES), jnp.float32),
        in_specs=[pl.BlockSpec(memory_space=pltpu.VMEM)] * 3 + far * (len(args) - 3),
        out_specs=far[0],
        scratch_shapes=[pltpu.VMEM((2, 8 * ROWS, LANES), jnp.float32), pltpu.SemaphoreType.DMA((2,))],
        input_output_aliases={3: 0} if len(args) == 4 else {},
        compiler_params=pltpu.CompilerParams(vmem_limit_bytes=16 << 20),
        cost_estimate=pl.CostEstimate(flops=10**6, bytes_accessed=2 << 20, transcendentals=0),
    )(*args)


def on_core(kernel, out_shape, scratch=(), far=False, vmem=16 << 20, cost=None):
    space = pl.ANY if far else pltpu.VMEM
    where = pltpu.VMEM if far else jax.ShapeDtypeStruct
    shapes = [s if not isinstance(s, tuple) else where(s, jnp.float32) for s in out_shape]
    return lambda *args: pl.pallas_call(
        kernel,
        out_shape=shapes,
        in_specs=[pl.BlockSpec(memory_space=space)] * len(args),
        out_specs=[pl.BlockSpec(memory_space=pltpu.VMEM)] * len(out_shape),
        scratch_shapes=[pltpu.VMEM(s, jnp.float32) if isinstance(s, tuple) else s for s in scratch],
        compiler_params=pltpu.CompilerParams(vmem_limit_bytes=vmem),
        cost_estimate=cost,
    )(*args)


def in_hbm(x):
    return pltpu.with_memory_space_constraint(x, pltpu.HBM)


def by_rows(x):
    lead, frames = x.shape[:-2], x.shape[-2]
    x = x.reshape(*lead, frames, ROWS, LANES)
    return jnp.swapaxes(x, -3, -2).reshape(*lead, ROWS * frames, LANES)


CORES = [(i, i ^ 1) for i in range(2 * X * Y * Z)]


def total_over_all(sums, back):
    left = [(i, (i - 1) % (2 * Y)) for i in range(2 * Y)]
    steps = [("x", r) for r in RING4] + [("y", r) for r in RING4] + [("z", r) for r in RING8]
    for n, (axis, partner) in enumerate(steps):
        if n == 1:
            sums, back = lax.optimization_barrier((sums, back))
            back = lax.ppermute(back, "tm", left)
        sums = sums + lax.ppermute(sums, BOTH, swap_pairs(axis, partner))
    return sums, lax.ppermute(sums, BOTH, CORES), back


def body(voltages, filter_taps):
    devices = lax.axis_size("tm")
    table, twist = (jnp.asarray(t) for t in dft_tables())
    tiles = jnp.swapaxes(voltages[0].reshape(2, 2, 2, 8, ROWS, LANES), 3, 4)
    rim = (2, RIM, ROWS, LANES)
    cross, near = on_core(
        rim_kernel,
        [rim, rim],
        scratch=[pltpu.SemaphoreType.DMA((2, 2, RIM))],
        far=True,
        cost=SHORT,
    )(in_hbm(tiles))
    near = lax.ppermute(near, "tm", [(i, i ^ 1) for i in range(devices)])
    cross = lax.ppermute(cross, "tm", [(i, (i + 1 if i % 2 else i - 1) % devices) for i in range(devices)])
    strips = (2, 2, 2, ROWS * 8, LANES)
    held, part, had, send, taps, table, twist = on_core(
        held_kernel,
        [
            (2, HELD, ROWS, LANES),
            (2, 2 * RIM, ROWS, LANES),
            (ROWS, LANES),
            (ROWS, LANES),
            (ROWS * TAPS, LANES),
            pltpu.VMEM(table.shape, table.dtype),
            twist.shape,
        ],
        scratch=[
            strips,
            (2, 2, HELD, ROWS, LANES),
            pltpu.SemaphoreType.DMA((ROWS // 8,)),
            pltpu.SemaphoreType.DMA((3,)),
        ],
        far=True,
        cost=pl.CostEstimate(flops=2 * 10**9, bytes_accessed=6 << 20, transcendentals=0),
    )(in_hbm(tiles.reshape(strips)), in_hbm(by_rows(filter_taps)), in_hbm(table), in_hbm(twist))
    other = lax.ppermute(send, BOTH, CORES)
    early, had = on_core(
        near_kernel,
        [(RIM, ROWS, LANES), (ROWS, LANES)],
        cost=pl.CostEstimate(flops=10**9, bytes_accessed=3 << 20, transcendentals=0),
    )(part, near, taps, table, twist, had)
    ahead, back, sums = on_core(
        functools.partial(cross_kernel, devices - 1),
        [(RIM, ROWS, LANES), (RIM, ROWS, LANES), (ROWS, LANES)],
    )(part, cross, taps, table, twist, had, other, early)
    mine, other, back = total_over_all(sums, back)
    scale = 1.0 / (FRAMES * devices * lax.axis_size("beam"))
    out = clean(scale, held, ahead, mine)
    out = clean(scale, held, back, other, out)
    out = jnp.swapaxes(out.reshape(2, 2, ROWS, 8, LANES), 2, 3)
    return out.reshape(1, 2, FRAMES, CHANNELS)


def solution(mesh):
    placed = (P("beam", None, None, "tm", None), P())
    return jax.shard_map(
        body, mesh=mesh, in_specs=placed, out_specs=P("beam", None, "tm", None), check_vma=False
    )
```

```python
import functools
import math

import jax
import jax.numpy as jnp
import ml_dtypes
import numpy as np
from jax import lax
from jax.experimental import pallas as pl
from jax.experimental.pallas import tpu as pltpu
from jax.sharding import PartitionSpec as P

LANES = 128
ROWS = 64
CHANNELS = ROWS * LANES
TAPS = 8
FRAMES = 16
HELD = 9
RIM = FRAMES - HELD
SHORT = pl.CostEstimate(flops=1000, bytes_accessed=1000, transcendentals=0)
BOTH = ("beam", "tm")
X, Y, Z = 4, 4, 8

YS = ((3, 2, 1, 0), (1, 0, 3, 2))
XS = ((1, 0, 3, 2), (2, 3, 0, 1))
ZS = ((1, 0, 3, 2, 5, 4, 7, 6), (2, 3, 0, 1, 6, 7, 4, 5), (7, 6, 5, 4, 3, 2, 1, 0))


def place(z, x, y, core):
    return ((z * X + x) * Y + y) * 2 + core


def swap_pairs(axis, partner):
    pairs = []
    for z in range(Z):
        for x in range(X):
            for y in range(Y):
                there = {
                    "z": lambda: (partner[z], x, y),
                    "x": lambda: (z, partner[x], y),
                    "y": lambda: (z, x, partner[y]),
                }[axis]()
                pairs += [(place(z, x, y, c), place(*there, c if axis == "y" else 1 - c)) for c in range(2)]
    return pairs


def kept_half():
    tm, beam = lax.axis_index("tm"), lax.axis_index("beam")
    x, z = beam % X, beam // X
    return (tm + x + x // 2 + z + z // 2 + z // 4) % 2


def in_two(table):
    high = table.astype(ml_dtypes.bfloat16)
    low = (table - high.astype(np.float64)).astype(ml_dtypes.bfloat16)
    return high, low


def dft_tables():
    q = np.arange(ROWS)
    angle = 2.0 * np.pi * (np.outer(q, q) % ROWS) / ROWS
    cos, sin = np.cos(angle), np.sin(angle)
    first = np.block([[cos, sin], [-sin, cos]])
    high, low = in_two(first)
    first = np.block([[high, high], [low, low]])
    lane = np.arange(LANES)
    order = np.concatenate([np.arange(0, LANES, 2), np.arange(1, LANES, 2)])
    angle = 2.0 * np.pi * (np.outer(order, lane) % LANES) / LANES
    cos, sin = np.cos(angle), np.sin(angle)
    second = np.block([[cos, sin], [-sin, cos]])
    second = np.concatenate(in_two(second), axis=0)
    angle = 2.0 * np.pi * np.outer(q, lane) / CHANNELS
    twist = np.stack([np.cos(angle), np.sin(angle)]).astype(np.float32)
    return np.concatenate([first, second], axis=0), twist


def halves(values):
    high = values.astype(jnp.bfloat16)
    low = (values - high.astype(jnp.float32)).astype(jnp.bfloat16)
    return high, low


def power_rows(frames, table_ref, twist_ref):
    count = len(frames)
    cols = [jnp.concatenate([re, im], axis=0) for re, im in frames]
    high, low = halves(jnp.concatenate(cols, axis=1))
    both = jnp.dot(
        table_ref[: 4 * ROWS],
        jnp.concatenate([high, low], axis=0),
        preferred_element_type=jnp.float32,
    )
    section = both[: 2 * ROWS] + both[2 * ROWS :]
    cos, sin = twist_ref[0], twist_ref[1]
    rows = []
    for g in range(count):
        re = section[:ROWS, g * LANES : (g + 1) * LANES]
        im = section[ROWS:, g * LANES : (g + 1) * LANES]
        rows.append(jnp.concatenate([re * cos + im * sin, im * cos - re * sin], axis=1))
    high, low = halves(jnp.concatenate(rows, axis=0))
    across = (((1,), (1,)), ((), ()))
    table = table_ref[4 * ROWS :]
    both = lax.dot_general(table, high, across, preferred_element_type=jnp.float32)
    both += lax.dot_general(table, low, across, preferred_element_type=jnp.float32)
    spec = both[: 2 * LANES] + both[2 * LANES :]
    re, im = spec[:LANES], spec[LANES:]
    powers = (re * re + im * im) * (1.0 / CHANNELS)
    left = lax.broadcasted_iota(jnp.int32, (ROWS, LANES), 1) < ROWS
    out = []
    for g in range(0, count, 2):
        if g + 1 == count:
            out.append(jnp.concatenate([powers[:ROWS, g * ROWS :], powers[ROWS:, g * ROWS :]], axis=1))
            break
        even = powers[:ROWS, g * ROWS : (g + 2) * ROWS]
        odd = powers[ROWS:, g * ROWS : (g + 2) * ROWS]
        out.append(jnp.where(left, even, pltpu.roll(odd, ROWS, 1)))
        out.append(jnp.where(left, pltpu.roll(even, ROWS, 1), odd))
    return out


def rim_copies(volt_ref, out_ref, sems, last):
    p = 1 - kept_half()
    copies = []
    for n in range(RIM):
        f = HELD + n if last else n
        for c in range(2):
            frame = volt_ref.at[p, c, f // 8, :, f % 8, :]
            copies.append(pltpu.make_async_copy(frame, out_ref.at[c, n], sems.at[c, n]))
    return copies


def rim_kernel(volt_ref, cross_ref, near_ref, sems):
    for core in range(2):

        @pl.when(lax.axis_index("tm") % 2 == core)
        def _():
            copies = rim_copies(volt_ref, cross_ref, sems.at[1], core == 1)
            copies += rim_copies(volt_ref, near_ref, sems.at[0], core == 0)
            for copy in copies:
                copy.start()
            for copy in copies:
                copy.wait()


def held_kernel(
    volt_in, taps_in, table_in, twist_in,
    pow_ref, part_ref, mine_ref, send_ref, taps_ref, table_ref, twist_ref,
    volt_ref, filt_ref, strip_sems, table_sems,
):
    def strip_copy(s):
        rows = pl.ds(pl.multiple_of(s * 64, 64), 64)
        return pltpu.make_async_copy(volt_in.at[:, :, :, rows, :], volt_ref.at[:, :, :, rows, :], strip_sems.at[s])

    taps_copy = pltpu.make_async_copy(taps_in, taps_ref, table_sems.at[0])
    table_copy = pltpu.make_async_copy(table_in, table_ref, table_sems.at[1])
    twist_copy = pltpu.make_async_copy(twist_in, twist_ref, table_sems.at[2])
    taps_copy.start()
    for s in range(ROWS // 8):
        strip_copy(s).start()
    table_copy.start()
    twist_copy.start()
    taps_copy.wait()
    keep = lax.axis_index("tm") > 0
    own = kept_half()

    def strip(s, _):
        strip_copy(s).wait()
        at = pl.multiple_of(s * 64, 64)
        rows = pl.ds(pl.multiple_of(s * 8, 8), 8)
        taps = [taps_ref[pl.ds(at + t, 8, stride=8), :] for t in range(TAPS)]
        for p in range(2):
            for c in range(2):
                x = [volt_ref[p, c, f // 8, pl.ds(at + f % 8, 8, stride=8), :] for f in range(FRAMES)]
                for f in range(HELD):
                    total = taps[0] * x[f]
                    for t in range(1, TAPS):
                        total = total + taps[t] * x[f + t]
                    filt_ref[p, c, f, rows, :] = total
        for c in range(2):
            x = [volt_ref[own, c, f // 8, pl.ds(at + f % 8, 8, stride=8), :] for f in range(FRAMES)]
            for j in range(RIM):
                total = taps[0] * x[HELD + j]
                for t in range(1, RIM - j):
                    total = total + taps[t] * x[HELD + j + t]
                part_ref[c, j, rows, :] = total
                reach = RIM - j
                total = taps[reach] * x[0]
                for t in range(reach + 1, TAPS):
                    total = total + taps[t] * x[t - reach]
                part_ref[c, RIM + j, rows, :] = jnp.where(keep, total, 0.0)
        return 0

    lax.fori_loop(0, ROWS // 8, strip, 0)
    table_copy.wait()
    twist_copy.wait()
    sums = [None, None]
    for start in range(0, HELD, 2):
        which = [(p, f) for f in range(start, min(start + 2, HELD)) for p in range(2)]
        frames = [(filt_ref[p, 0, f], filt_ref[p, 1, f]) for p, f in which]
        for (p, f), power in zip(which, power_rows(frames, table_ref, twist_ref)):
            pow_ref[p, f] = power
            sums[p] = power if sums[p] is None else sums[p] + power
    mine_ref[...] = jnp.where(own == 1, sums[1], sums[0])
    send_ref[...] = jnp.where(own == 1, sums[0], sums[1])


def rim_powers(role, part_ref, came_ref, taps_ref, table_ref, twist_ref, total_sum, keep, store):
    taps = [taps_ref[pl.ds(t, ROWS, stride=8), :] for t in range(TAPS)]

    def finished(j):
        out = []
        for c in range(2):
            if role == "ahead":
                terms = [(RIM + i - j, i) for i in range(j + 1)]
                total = part_ref[c, j]
            else:
                terms = [(t, j + t) for t in range(RIM - j)]
                total = part_ref[c, RIM + j]
            rest = None
            for t, i in terms:
                term = taps[t] * came_ref[c, i]
                rest = term if rest is None else rest + term
            out.append(total + (rest if keep is None else jnp.where(keep, rest, 0.0)))
        return tuple(out)

    for start in range(0, RIM, 4):
        which = range(start, min(start + 4, RIM))
        for j, power in zip(which, power_rows([finished(j) for j in which], table_ref, twist_ref)):
            store[j] = power
            total_sum = total_sum + power
    return total_sum


def near_kernel(part_ref, near_ref, taps_ref, table_ref, twist_ref, had_ref, early_ref, sum_ref):
    for core, role in enumerate(("ahead", "back")):

        @pl.when(lax.axis_index("tm") % 2 == core)
        def _():
            sum_ref[...] = rim_powers(
                role, part_ref, near_ref, taps_ref, table_ref, twist_ref, had_ref[...], None, early_ref
            )


def cross_kernel(last, part_ref, cross_ref, taps_ref, table_ref, twist_ref, had_ref, other_ref, early_ref, ahead_ref, back_ref, sum_ref):
    tm = lax.axis_index("tm")
    for core, role in enumerate(("back", "ahead")):

        @pl.when(tm % 2 == core)
        def _():
            store, keep = (back_ref, None) if core == 0 else (ahead_ref, tm < last)
            had = had_ref[...] + other_ref[...]
            sum_ref[...] = rim_powers(
                role, part_ref, cross_ref, taps_ref, table_ref, twist_ref, had, keep, store
            )
            kept_ref = ahead_ref if core == 0 else back_ref
            kept_ref[...] = early_ref[...]


def clean_kernel(scale, held_ref, rim_ref, sum_ref, *refs):
    out_ref, tile_ref, sems = refs[-3:]
    p = kept_half() if len(refs) == 3 else 1 - kept_half()
    base = sum_ref[...] * scale
    copies = []
    for half in range(2):
        for f in range(8 * half, 8 * half + 8):
            power = held_ref[p, f] if f < HELD else rim_ref[f - HELD]
            tile_ref[half, pl.ds(f % 8, ROWS, stride=8), :] = power - base
        copies.append(pltpu.make_async_copy(tile_ref.at[half], out_ref.at[p, half], sems.at[half]))
        copies[-1].start()
    for copy in copies:
        copy.wait()


def clean(scale, *args):
    far = [pl.BlockSpec(memory_space=pl.ANY)]
    return pl.pallas_call(
        functools.partial(clean_kernel, scale),
        out_shape=pltpu.HBM((2, 2, 8 * ROWS, LANES), jnp.float32),
        in_specs=[pl.BlockSpec(memory_space=pltpu.VMEM)] * 3 + far * (len(args) - 3),
        out_specs=far[0],
        scratch_shapes=[pltpu.VMEM((2, 8 * ROWS, LANES), jnp.float32), pltpu.SemaphoreType.DMA((2,))],
        input_output_aliases={3: 0} if len(args) == 4 else {},
        compiler_params=pltpu.CompilerParams(vmem_limit_bytes=16 << 20),
        cost_estimate=pl.CostEstimate(flops=10**6, bytes_accessed=2 << 20, transcendentals=0),
    )(*args)


def on_core(kernel, out_shape, scratch=(), far=False, vmem=16 << 20, cost=None):
    space = pl.ANY if far else pltpu.VMEM
    where = pltpu.VMEM if far else jax.ShapeDtypeStruct
    shapes = [s if not isinstance(s, tuple) else where(s, jnp.float32) for s in out_shape]
    return lambda *args: pl.pallas_call(
        kernel,
        out_shape=shapes,
        in_specs=[pl.BlockSpec(memory_space=space)] * len(args),
        out_specs=[pl.BlockSpec(memory_space=pltpu.VMEM)] * len(out_shape),
        scratch_shapes=[pltpu.VMEM(s, jnp.float32) if isinstance(s, tuple) else s for s in scratch],
        compiler_params=pltpu.CompilerParams(vmem_limit_bytes=vmem),
        cost_estimate=cost,
    )(*args)


def in_hbm(x):
    return pltpu.with_memory_space_constraint(x, pltpu.HBM)


def by_rows(x):
    lead, frames = x.shape[:-2], x.shape[-2]
    x = x.reshape(*lead, frames, ROWS, LANES)
    return jnp.swapaxes(x, -3, -2).reshape(*lead, ROWS * frames, LANES)


CORES = [(i, i ^ 1) for i in range(2 * X * Y * Z)]


def total_over_all(sums, back):
    left = [(i, (i - 1) % (2 * Y)) for i in range(2 * Y)]
    steps = [("y", YS[0])] + [("x", r) for r in XS] + [("y", YS[1])] + [("z", r) for r in ZS]
    for n, (axis, partner) in enumerate(steps):
        if n == 1:
            sums, back = lax.optimization_barrier((sums, back))
            back = lax.ppermute(back, "tm", left)
        sums = sums + lax.ppermute(sums, BOTH, swap_pairs(axis, partner))
    return sums, lax.ppermute(sums, BOTH, CORES), back


def body(voltages, filter_taps):
    devices = lax.axis_size("tm")
    table, twist = (jnp.asarray(t) for t in dft_tables())
    tiles = jnp.swapaxes(voltages[0].reshape(2, 2, 2, 8, ROWS, LANES), 3, 4)
    rim = (2, RIM, ROWS, LANES)
    cross, near = on_core(
        rim_kernel,
        [rim, rim],
        scratch=[pltpu.SemaphoreType.DMA((2, 2, RIM))],
        far=True,
        cost=SHORT,
    )(in_hbm(tiles))
    near = lax.ppermute(near, "tm", [(i, i ^ 1) for i in range(devices)])
    cross = lax.ppermute(cross, "tm", [(i, (i + 1 if i % 2 else i - 1) % devices) for i in range(devices)])
    strips = (2, 2, 2, ROWS * 8, LANES)
    held, part, had, send, taps, table, twist = on_core(
        held_kernel,
        [
            (2, HELD, ROWS, LANES),
            (2, 2 * RIM, ROWS, LANES),
            (ROWS, LANES),
            (ROWS, LANES),
            (ROWS * TAPS, LANES),
            pltpu.VMEM(table.shape, table.dtype),
            twist.shape,
        ],
        scratch=[
            strips,
            (2, 2, HELD, ROWS, LANES),
            pltpu.SemaphoreType.DMA((ROWS // 8,)),
            pltpu.SemaphoreType.DMA((3,)),
        ],
        far=True,
        cost=pl.CostEstimate(flops=2 * 10**9, bytes_accessed=6 << 20, transcendentals=0),
    )(in_hbm(tiles.reshape(strips)), in_hbm(by_rows(filter_taps)), in_hbm(table), in_hbm(twist))
    other = lax.ppermute(send, BOTH, CORES)
    early, had = on_core(
        near_kernel,
        [(RIM, ROWS, LANES), (ROWS, LANES)],
        cost=pl.CostEstimate(flops=10**9, bytes_accessed=3 << 20, transcendentals=0),
    )(part, near, taps, table, twist, had)
    ahead, back, sums = on_core(
        functools.partial(cross_kernel, devices - 1),
        [(RIM, ROWS, LANES), (RIM, ROWS, LANES), (ROWS, LANES)],
    )(part, cross, taps, table, twist, had, other, early)
    mine, other, back = total_over_all(sums, back)
    scale = 1.0 / (FRAMES * devices * lax.axis_size("beam"))
    out = clean(scale, held, ahead, mine)
    out = clean(scale, held, back, other, out)
    out = jnp.swapaxes(out.reshape(2, 2, ROWS, 8, LANES), 2, 3)
    return out.reshape(1, 2, FRAMES, CHANNELS)


def solution(mesh):
    placed = (P("beam", None, None, "tm", None), P())
    return jax.shard_map(
        body, mesh=mesh, in_specs=placed, out_specs=P("beam", None, "tm", None), check_vma=False
    )
```

```python
import functools
import math

import jax
import jax.numpy as jnp
import ml_dtypes
import numpy as np
from jax import lax
from jax.experimental import pallas as pl
from jax.experimental.pallas import tpu as pltpu
from jax.sharding import PartitionSpec as P

LANES = 128
ROWS = 64
CHANNELS = ROWS * LANES
TAPS = 8
FRAMES = 16
HELD = 9
RIM = FRAMES - HELD
SHORT = pl.CostEstimate(flops=1000, bytes_accessed=1000, transcendentals=0)
BOTH = ("beam", "tm")
X, Y, Z = 4, 4, 8

YS = ((3, 2, 1, 0), (1, 0, 3, 2))
XS = ((1, 0, 3, 2), (3, 2, 1, 0))
ZS = ((1, 0, 3, 2, 5, 4, 7, 6), (2, 3, 0, 1, 6, 7, 4, 5), (7, 6, 5, 4, 3, 2, 1, 0))


def place(z, x, y, core):
    return ((z * X + x) * Y + y) * 2 + core


def swap_pairs(axis, partner):
    pairs = []
    for z in range(Z):
        for x in range(X):
            for y in range(Y):
                there = {
                    "z": lambda: (partner[z], x, y),
                    "x": lambda: (z, partner[x], y),
                    "y": lambda: (z, x, partner[y]),
                }[axis]()
                pairs += [(place(z, x, y, c), place(*there, c if axis == "y" else 1 - c)) for c in range(2)]
    return pairs


def kept_half():
    tm, beam = lax.axis_index("tm"), lax.axis_index("beam")
    x, z = beam % X, beam // X
    return (tm + x + z + z // 2 + z // 4) % 2


def in_two(table):
    high = table.astype(ml_dtypes.bfloat16)
    low = (table - high.astype(np.float64)).astype(ml_dtypes.bfloat16)
    return high, low


def dft_tables():
    q = np.arange(ROWS)
    angle = 2.0 * np.pi * (np.outer(q, q) % ROWS) / ROWS
    cos, sin = np.cos(angle), np.sin(angle)
    first = np.block([[cos, sin], [-sin, cos]])
    high, low = in_two(first)
    first = np.block([[high, high], [low, low]])
    lane = np.arange(LANES)
    order = np.concatenate([np.arange(0, LANES, 2), np.arange(1, LANES, 2)])
    angle = 2.0 * np.pi * (np.outer(order, lane) % LANES) / LANES
    cos, sin = np.cos(angle), np.sin(angle)
    second = np.block([[cos, sin], [-sin, cos]])
    second = np.concatenate(in_two(second), axis=0)
    angle = 2.0 * np.pi * np.outer(q, lane) / CHANNELS
    twist = np.stack([np.cos(angle), np.sin(angle)]).astype(np.float32)
    return np.concatenate([first, second], axis=0), twist


def halves(values):
    high = values.astype(jnp.bfloat16)
    low = (values - high.astype(jnp.float32)).astype(jnp.bfloat16)
    return high, low


def power_rows(frames, table_ref, twist_ref):
    count = len(frames)
    cols = [jnp.concatenate([re, im], axis=0) for re, im in frames]
    high, low = halves(jnp.concatenate(cols, axis=1))
    both = jnp.dot(
        table_ref[: 4 * ROWS],
        jnp.concatenate([high, low], axis=0),
        preferred_element_type=jnp.float32,
    )
    section = both[: 2 * ROWS] + both[2 * ROWS :]
    cos, sin = twist_ref[0], twist_ref[1]
    rows = []
    for g in range(count):
        re = section[:ROWS, g * LANES : (g + 1) * LANES]
        im = section[ROWS:, g * LANES : (g + 1) * LANES]
        rows.append(jnp.concatenate([re * cos + im * sin, im * cos - re * sin], axis=1))
    high, low = halves(jnp.concatenate(rows, axis=0))
    across = (((1,), (1,)), ((), ()))
    table = table_ref[4 * ROWS :]
    both = lax.dot_general(table, high, across, preferred_element_type=jnp.float32)
    both += lax.dot_general(table, low, across, preferred_element_type=jnp.float32)
    spec = both[: 2 * LANES] + both[2 * LANES :]
    re, im = spec[:LANES], spec[LANES:]
    powers = (re * re + im * im) * (1.0 / CHANNELS)
    left = lax.broadcasted_iota(jnp.int32, (ROWS, LANES), 1) < ROWS
    out = []
    for g in range(0, count, 2):
        if g + 1 == count:
            out.append(jnp.concatenate([powers[:ROWS, g * ROWS :], powers[ROWS:, g * ROWS :]], axis=1))
            break
        even = powers[:ROWS, g * ROWS : (g + 2) * ROWS]
        odd = powers[ROWS:, g * ROWS : (g + 2) * ROWS]
        out.append(jnp.where(left, even, pltpu.roll(odd, ROWS, 1)))
        out.append(jnp.where(left, pltpu.roll(even, ROWS, 1), odd))
    return out


def rim_copies(volt_ref, out_ref, sems, last):
    p = 1 - kept_half()
    copies = []
    for n in range(RIM):
        f = HELD + n if last else n
        for c in range(2):
            frame = volt_ref.at[p, c, f // 8, :, f % 8, :]
            copies.append(pltpu.make_async_copy(frame, out_ref.at[c, n], sems.at[c, n]))
    return copies


def rim_kernel(volt_ref, cross_ref, near_ref, sems):
    for core in range(2):

        @pl.when(lax.axis_index("tm") % 2 == core)
        def _():
            copies = rim_copies(volt_ref, cross_ref, sems.at[1], core == 1)
            copies += rim_copies(volt_ref, near_ref, sems.at[0], core == 0)
            for copy in copies:
                copy.start()
            for copy in copies:
                copy.wait()


def held_kernel(
    volt_in, taps_in, table_in, twist_in,
    pow_ref, part_ref, mine_ref, send_ref, taps_ref, table_ref, twist_ref,
    volt_ref, filt_ref, strip_sems, table_sems,
):
    def strip_copy(s):
        rows = pl.ds(pl.multiple_of(s * 64, 64), 64)
        return pltpu.make_async_copy(volt_in.at[:, :, :, rows, :], volt_ref.at[:, :, :, rows, :], strip_sems.at[s])

    taps_copy = pltpu.make_async_copy(taps_in, taps_ref, table_sems.at[0])
    table_copy = pltpu.make_async_copy(table_in, table_ref, table_sems.at[1])
    twist_copy = pltpu.make_async_copy(twist_in, twist_ref, table_sems.at[2])
    taps_copy.start()
    for s in range(ROWS // 8):
        strip_copy(s).start()
    table_copy.start()
    twist_copy.start()
    taps_copy.wait()
    keep = lax.axis_index("tm") > 0
    own = kept_half()

    def strip(s, _):
        strip_copy(s).wait()
        at = pl.multiple_of(s * 64, 64)
        rows = pl.ds(pl.multiple_of(s * 8, 8), 8)
        taps = [taps_ref[pl.ds(at + t, 8, stride=8), :] for t in range(TAPS)]
        for p in range(2):
            for c in range(2):
                x = [volt_ref[p, c, f // 8, pl.ds(at + f % 8, 8, stride=8), :] for f in range(FRAMES)]
                for f in range(HELD):
                    total = taps[0] * x[f]
                    for t in range(1, TAPS):
                        total = total + taps[t] * x[f + t]
                    filt_ref[p, c, f, rows, :] = total
        for c in range(2):
            x = [volt_ref[own, c, f // 8, pl.ds(at + f % 8, 8, stride=8), :] for f in range(FRAMES)]
            for j in range(RIM):
                total = taps[0] * x[HELD + j]
                for t in range(1, RIM - j):
                    total = total + taps[t] * x[HELD + j + t]
                part_ref[c, j, rows, :] = total
                reach = RIM - j
                total = taps[reach] * x[0]
                for t in range(reach + 1, TAPS):
                    total = total + taps[t] * x[t - reach]
                part_ref[c, RIM + j, rows, :] = jnp.where(keep, total, 0.0)
        return 0

    lax.fori_loop(0, ROWS // 8, strip, 0)
    table_copy.wait()
    twist_copy.wait()
    sums = [None, None]
    for start in range(0, HELD, 2):
        which = [(p, f) for f in range(start, min(start + 2, HELD)) for p in range(2)]
        frames = [(filt_ref[p, 0, f], filt_ref[p, 1, f]) for p, f in which]
        for (p, f), power in zip(which, power_rows(frames, table_ref, twist_ref)):
            pow_ref[p, f] = power
            sums[p] = power if sums[p] is None else sums[p] + power
    mine_ref[...] = jnp.where(own == 1, sums[1], sums[0])
    send_ref[...] = jnp.where(own == 1, sums[0], sums[1])


def rim_powers(role, part_ref, came_ref, taps_ref, table_ref, twist_ref, total_sum, keep, store):
    taps = [taps_ref[pl.ds(t, ROWS, stride=8), :] for t in range(TAPS)]

    def finished(j):
        out = []
        for c in range(2):
            if role == "ahead":
                terms = [(RIM + i - j, i) for i in range(j + 1)]
                total = part_ref[c, j]
            else:
                terms = [(t, j + t) for t in range(RIM - j)]
                total = part_ref[c, RIM + j]
            rest = None
            for t, i in terms:
                term = taps[t] * came_ref[c, i]
                rest = term if rest is None else rest + term
            out.append(total + (rest if keep is None else jnp.where(keep, rest, 0.0)))
        return tuple(out)

    for start in range(0, RIM, 4):
        which = range(start, min(start + 4, RIM))
        for j, power in zip(which, power_rows([finished(j) for j in which], table_ref, twist_ref)):
            store[j] = power
            total_sum = total_sum + power
    return total_sum


def near_kernel(part_ref, near_ref, taps_ref, table_ref, twist_ref, had_ref, early_ref, sum_ref):
    for core, role in enumerate(("ahead", "back")):

        @pl.when(lax.axis_index("tm") % 2 == core)
        def _():
            sum_ref[...] = rim_powers(
                role, part_ref, near_ref, taps_ref, table_ref, twist_ref, had_ref[...], None, early_ref
            )


def cross_kernel(last, part_ref, cross_ref, taps_ref, table_ref, twist_ref, had_ref, other_ref, early_ref, ahead_ref, back_ref, sum_ref):
    tm = lax.axis_index("tm")
    for core, role in enumerate(("back", "ahead")):

        @pl.when(tm % 2 == core)
        def _():
            store, keep = (back_ref, None) if core == 0 else (ahead_ref, tm < last)
            had = had_ref[...] + other_ref[...]
            sum_ref[...] = rim_powers(
                role, part_ref, cross_ref, taps_ref, table_ref, twist_ref, had, keep, store
            )
            kept_ref = ahead_ref if core == 0 else back_ref
            kept_ref[...] = early_ref[...]


def clean_kernel(scale, held_ref, rim_ref, sum_ref, *refs):
    out_ref, tile_ref, sems = refs[-3:]
    p = kept_half() if len(refs) == 3 else 1 - kept_half()
    base = sum_ref[...] * scale
    copies = []
    for half in range(2):
        for f in range(8 * half, 8 * half + 8):
            power = held_ref[p, f] if f < HELD else rim_ref[f - HELD]
            tile_ref[half, pl.ds(f % 8, ROWS, stride=8), :] = power - base
        copies.append(pltpu.make_async_copy(tile_ref.at[half], out_ref.at[p, half], sems.at[half]))
        copies[-1].start()
    for copy in copies:
        copy.wait()


def clean(scale, *args):
    far = [pl.BlockSpec(memory_space=pl.ANY)]
    return pl.pallas_call(
        functools.partial(clean_kernel, scale),
        out_shape=pltpu.HBM((2, 2, 8 * ROWS, LANES), jnp.float32),
        in_specs=[pl.BlockSpec(memory_space=pltpu.VMEM)] * 3 + far * (len(args) - 3),
        out_specs=far[0],
        scratch_shapes=[pltpu.VMEM((2, 8 * ROWS, LANES), jnp.float32), pltpu.SemaphoreType.DMA((2,))],
        input_output_aliases={3: 0} if len(args) == 4 else {},
        compiler_params=pltpu.CompilerParams(vmem_limit_bytes=16 << 20),
        cost_estimate=pl.CostEstimate(flops=10**6, bytes_accessed=2 << 20, transcendentals=0),
    )(*args)


def on_core(kernel, out_shape, scratch=(), far=False, vmem=16 << 20, cost=None):
    space = pl.ANY if far else pltpu.VMEM
    where = pltpu.VMEM if far else jax.ShapeDtypeStruct
    shapes = [s if not isinstance(s, tuple) else where(s, jnp.float32) for s in out_shape]
    return lambda *args: pl.pallas_call(
        kernel,
        out_shape=shapes,
        in_specs=[pl.BlockSpec(memory_space=space)] * len(args),
        out_specs=[pl.BlockSpec(memory_space=pltpu.VMEM)] * len(out_shape),
        scratch_shapes=[pltpu.VMEM(s, jnp.float32) if isinstance(s, tuple) else s for s in scratch],
        compiler_params=pltpu.CompilerParams(vmem_limit_bytes=vmem),
        cost_estimate=cost,
    )(*args)


def in_hbm(x):
    return pltpu.with_memory_space_constraint(x, pltpu.HBM)


def by_rows(x):
    lead, frames = x.shape[:-2], x.shape[-2]
    x = x.reshape(*lead, frames, ROWS, LANES)
    return jnp.swapaxes(x, -3, -2).reshape(*lead, ROWS * frames, LANES)


CORES = [(i, i ^ 1) for i in range(2 * X * Y * Z)]


def total_over_all(sums, back):
    left = [(i, (i - 1) % (2 * Y)) for i in range(2 * Y)]
    steps = [("y", YS[0])] + [("x", r) for r in XS] + [("y", YS[1])] + [("z", r) for r in ZS]
    for n, (axis, partner) in enumerate(steps):
        if n == 1:
            sums, back = lax.optimization_barrier((sums, back))
            back = lax.ppermute(back, "tm", left)
        sums = sums + lax.ppermute(sums, BOTH, swap_pairs(axis, partner))
    return sums, lax.ppermute(sums, BOTH, CORES), back


def body(voltages, filter_taps):
    devices = lax.axis_size("tm")
    table, twist = (jnp.asarray(t) for t in dft_tables())
    tiles = jnp.swapaxes(voltages[0].reshape(2, 2, 2, 8, ROWS, LANES), 3, 4)
    rim = (2, RIM, ROWS, LANES)
    cross, near = on_core(
        rim_kernel,
        [rim, rim],
        scratch=[pltpu.SemaphoreType.DMA((2, 2, RIM))],
        far=True,
        cost=SHORT,
    )(in_hbm(tiles))
    near = lax.ppermute(near, "tm", [(i, i ^ 1) for i in range(devices)])
    cross = lax.ppermute(cross, "tm", [(i, (i + 1 if i % 2 else i - 1) % devices) for i in range(devices)])
    strips = (2, 2, 2, ROWS * 8, LANES)
    held, part, had, send, taps, table, twist = on_core(
        held_kernel,
        [
            (2, HELD, ROWS, LANES),
            (2, 2 * RIM, ROWS, LANES),
            (ROWS, LANES),
            (ROWS, LANES),
            (ROWS * TAPS, LANES),
            pltpu.VMEM(table.shape, table.dtype),
            twist.shape,
        ],
        scratch=[
            strips,
            (2, 2, HELD, ROWS, LANES),
            pltpu.SemaphoreType.DMA((ROWS // 8,)),
            pltpu.SemaphoreType.DMA((3,)),
        ],
        far=True,
        cost=pl.CostEstimate(flops=2 * 10**9, bytes_accessed=6 << 20, transcendentals=0),
    )(in_hbm(tiles.reshape(strips)), in_hbm(by_rows(filter_taps)), in_hbm(table), in_hbm(twist))
    other = lax.ppermute(send, BOTH, CORES)
    early, had = on_core(
        near_kernel,
        [(RIM, ROWS, LANES), (ROWS, LANES)],
        cost=pl.CostEstimate(flops=10**9, bytes_accessed=3 << 20, transcendentals=0),
    )(part, near, taps, table, twist, had)
    ahead, back, sums = on_core(
        functools.partial(cross_kernel, devices - 1),
        [(RIM, ROWS, LANES), (RIM, ROWS, LANES), (ROWS, LANES)],
    )(part, cross, taps, table, twist, had, other, early)
    mine, other, back = total_over_all(sums, back)
    scale = 1.0 / (FRAMES * devices * lax.axis_size("beam"))
    out = clean(scale, held, ahead, mine)
    out = clean(scale, held, back, other, out)
    out = jnp.swapaxes(out.reshape(2, 2, ROWS, 8, LANES), 2, 3)
    return out.reshape(1, 2, FRAMES, CHANNELS)


def solution(mesh):
    placed = (P("beam", None, None, "tm", None), P())
    return jax.shard_map(
        body, mesh=mesh, in_specs=placed, out_specs=P("beam", None, "tm", None), check_vma=False
    )
```

```python
import functools
import math

import jax
import jax.numpy as jnp
import ml_dtypes
import numpy as np
from jax import lax
from jax.experimental import pallas as pl
from jax.experimental.pallas import tpu as pltpu
from jax.sharding import PartitionSpec as P

LANES = 128
ROWS = 64
CHANNELS = ROWS * LANES
TAPS = 8
FRAMES = 16
HELD = 9
RIM = FRAMES - HELD
SHORT = pl.CostEstimate(flops=1000, bytes_accessed=1000, transcendentals=0)
BOTH = ("beam", "tm")
X, Y, Z = 4, 4, 8

YS = ((3, 2, 1, 0), (1, 0, 3, 2))
XS = ((1, 0, 3, 2), (3, 2, 1, 0))
ZS = ((1, 0, 3, 2, 5, 4, 7, 6), (2, 3, 0, 1, 6, 7, 4, 5), (7, 6, 5, 4, 3, 2, 1, 0))


def place(z, x, y, core):
    return ((z * X + x) * Y + y) * 2 + core


def swap_pairs(axis, partner):
    pairs = []
    for z in range(Z):
        for x in range(X):
            for y in range(Y):
                there = {
                    "z": lambda: (partner[z], x, y),
                    "x": lambda: (z, partner[x], y),
                    "y": lambda: (z, x, partner[y]),
                }[axis]()
                pairs += [(place(z, x, y, c), place(*there, c if axis == "y" else 1 - c)) for c in range(2)]
    return pairs


def kept_half():
    tm, beam = lax.axis_index("tm"), lax.axis_index("beam")
    x, z = beam % X, beam // X
    return (tm + x + z + z // 2 + z // 4) % 2


def in_two(table):
    high = table.astype(ml_dtypes.bfloat16)
    low = (table - high.astype(np.float64)).astype(ml_dtypes.bfloat16)
    return high, low


def dft_tables():
    q = np.arange(ROWS)
    angle = 2.0 * np.pi * (np.outer(q, q) % ROWS) / ROWS
    cos, sin = np.cos(angle), np.sin(angle)
    first = np.block([[cos, sin], [-sin, cos]])
    high, low = in_two(first)
    first = np.block([[high, high], [low, low]])
    lane = np.arange(LANES)
    order = np.concatenate([np.arange(0, LANES, 2), np.arange(1, LANES, 2)])
    angle = 2.0 * np.pi * (np.outer(order, lane) % LANES) / LANES
    cos, sin = np.cos(angle), np.sin(angle)
    second = np.block([[cos, sin], [-sin, cos]])
    second = np.concatenate(in_two(second), axis=0)
    angle = 2.0 * np.pi * np.outer(q, lane) / CHANNELS
    twist = np.stack([np.cos(angle), np.sin(angle)]).astype(np.float32)
    return np.concatenate([first, second], axis=0), twist


def halves(values):
    high = values.astype(jnp.bfloat16)
    low = (values - high.astype(jnp.float32)).astype(jnp.bfloat16)
    return high, low


def power_rows(frames, table_ref, twist_ref):
    count = len(frames)
    cols = [jnp.concatenate([re, im], axis=0) for re, im in frames]
    high, low = halves(jnp.concatenate(cols, axis=1))
    both = jnp.dot(
        table_ref[: 4 * ROWS],
        jnp.concatenate([high, low], axis=0),
        preferred_element_type=jnp.float32,
    )
    section = both[: 2 * ROWS] + both[2 * ROWS :]
    cos, sin = twist_ref[0], twist_ref[1]
    rows = []
    for g in range(count):
        re = section[:ROWS, g * LANES : (g + 1) * LANES]
        im = section[ROWS:, g * LANES : (g + 1) * LANES]
        rows.append(jnp.concatenate([re * cos + im * sin, im * cos - re * sin], axis=1))
    high, low = halves(jnp.concatenate(rows, axis=0))
    across = (((1,), (1,)), ((), ()))
    table = table_ref[4 * ROWS :]
    both = lax.dot_general(table, high, across, preferred_element_type=jnp.float32)
    rest = lax.dot_general(table[: 2 * LANES], low, across, preferred_element_type=jnp.float32)
    spec = both[: 2 * LANES] + (both[2 * LANES :] + rest)
    re, im = spec[:LANES], spec[LANES:]
    powers = (re * re + im * im) * (1.0 / CHANNELS)
    left = lax.broadcasted_iota(jnp.int32, (ROWS, LANES), 1) < ROWS
    out = []
    for g in range(0, count, 2):
        if g + 1 == count:
            out.append(jnp.concatenate([powers[:ROWS, g * ROWS :], powers[ROWS:, g * ROWS :]], axis=1))
            break
        even = powers[:ROWS, g * ROWS : (g + 2) * ROWS]
        odd = powers[ROWS:, g * ROWS : (g + 2) * ROWS]
        out.append(jnp.where(left, even, pltpu.roll(odd, ROWS, 1)))
        out.append(jnp.where(left, pltpu.roll(even, ROWS, 1), odd))
    return out


def rim_copies(volt_ref, out_ref, sems, last):
    p = 1 - kept_half()
    copies = []
    for n in range(RIM):
        f = HELD + n if last else n
        for c in range(2):
            frame = volt_ref.at[p, c, f // 8, :, f % 8, :]
            copies.append(pltpu.make_async_copy(frame, out_ref.at[c, n], sems.at[c, n]))
    return copies


def rim_kernel(volt_ref, cross_ref, near_ref, sems):
    for core in range(2):

        @pl.when(lax.axis_index("tm") % 2 == core)
        def _():
            copies = rim_copies(volt_ref, cross_ref, sems.at[1], core == 1)
            copies += rim_copies(volt_ref, near_ref, sems.at[0], core == 0)
            for copy in copies:
                copy.start()
            for copy in copies:
                copy.wait()


def held_kernel(
    volt_in, taps_in, table_in, twist_in,
    pow_ref, part_ref, mine_ref, send_ref, taps_ref, table_ref, twist_ref,
    volt_ref, filt_ref, strip_sems, table_sems,
):
    def strip_copy(s):
        rows = pl.ds(pl.multiple_of(s * 64, 64), 64)
        return pltpu.make_async_copy(volt_in.at[:, :, :, rows, :], volt_ref.at[:, :, :, rows, :], strip_sems.at[s])

    taps_copy = pltpu.make_async_copy(taps_in, taps_ref, table_sems.at[0])
    table_copy = pltpu.make_async_copy(table_in, table_ref, table_sems.at[1])
    twist_copy = pltpu.make_async_copy(twist_in, twist_ref, table_sems.at[2])
    taps_copy.start()
    for s in range(ROWS // 8):
        strip_copy(s).start()
    table_copy.start()
    twist_copy.start()
    taps_copy.wait()
    keep = lax.axis_index("tm") > 0
    own = kept_half()

    def strip(s, _):
        strip_copy(s).wait()
        at = pl.multiple_of(s * 64, 64)
        rows = pl.ds(pl.multiple_of(s * 8, 8), 8)
        taps = [taps_ref[pl.ds(at + t, 8, stride=8), :] for t in range(TAPS)]
        for p in range(2):
            for c in range(2):
                x = [volt_ref[p, c, f // 8, pl.ds(at + f % 8, 8, stride=8), :] for f in range(FRAMES)]
                for f in range(HELD):
                    total = taps[0] * x[f]
                    for t in range(1, TAPS):
                        total = total + taps[t] * x[f + t]
                    filt_ref[p, c, f, rows, :] = total
        for c in range(2):
            x = [volt_ref[own, c, f // 8, pl.ds(at + f % 8, 8, stride=8), :] for f in range(FRAMES)]
            for j in range(RIM):
                total = taps[0] * x[HELD + j]
                for t in range(1, RIM - j):
                    total = total + taps[t] * x[HELD + j + t]
                part_ref[c, j, rows, :] = total
                reach = RIM - j
                total = taps[reach] * x[0]
                for t in range(reach + 1, TAPS):
                    total = total + taps[t] * x[t - reach]
                part_ref[c, RIM + j, rows, :] = jnp.where(keep, total, 0.0)
        return 0

    lax.fori_loop(0, ROWS // 8, strip, 0)
    table_copy.wait()
    twist_copy.wait()
    sums = [None, None]
    for start in range(0, HELD, 2):
        which = [(p, f) for f in range(start, min(start + 2, HELD)) for p in range(2)]
        frames = [(filt_ref[p, 0, f], filt_ref[p, 1, f]) for p, f in which]
        for (p, f), power in zip(which, power_rows(frames, table_ref, twist_ref)):
            pow_ref[p, f] = power
            sums[p] = power if sums[p] is None else sums[p] + power
    mine_ref[...] = jnp.where(own == 1, sums[1], sums[0])
    send_ref[...] = jnp.where(own == 1, sums[0], sums[1])


def rim_powers(role, part_ref, came_ref, taps_ref, table_ref, twist_ref, total_sum, keep, store):
    taps = [taps_ref[pl.ds(t, ROWS, stride=8), :] for t in range(TAPS)]

    def finished(j):
        out = []
        for c in range(2):
            if role == "ahead":
                terms = [(RIM + i - j, i) for i in range(j + 1)]
                total = part_ref[c, j]
            else:
                terms = [(t, j + t) for t in range(RIM - j)]
                total = part_ref[c, RIM + j]
            rest = None
            for t, i in terms:
                term = taps[t] * came_ref[c, i]
                rest = term if rest is None else rest + term
            out.append(total + (rest if keep is None else jnp.where(keep, rest, 0.0)))
        return tuple(out)

    for start in range(0, RIM, 4):
        which = range(start, min(start + 4, RIM))
        for j, power in zip(which, power_rows([finished(j) for j in which], table_ref, twist_ref)):
            store[j] = power
            total_sum = total_sum + power
    return total_sum


def near_kernel(part_ref, near_ref, taps_ref, table_ref, twist_ref, had_ref, early_ref, sum_ref):
    for core, role in enumerate(("ahead", "back")):

        @pl.when(lax.axis_index("tm") % 2 == core)
        def _():
            sum_ref[...] = rim_powers(
                role, part_ref, near_ref, taps_ref, table_ref, twist_ref, had_ref[...], None, early_ref
            )


def cross_kernel(last, part_ref, cross_ref, taps_ref, table_ref, twist_ref, had_ref, other_ref, early_ref, ahead_ref, back_ref, sum_ref):
    tm = lax.axis_index("tm")
    for core, role in enumerate(("back", "ahead")):

        @pl.when(tm % 2 == core)
        def _():
            store, keep = (back_ref, None) if core == 0 else (ahead_ref, tm < last)
            had = had_ref[...] + other_ref[...]
            sum_ref[...] = rim_powers(
                role, part_ref, cross_ref, taps_ref, table_ref, twist_ref, had, keep, store
            )
            kept_ref = ahead_ref if core == 0 else back_ref
            kept_ref[...] = early_ref[...]


def clean_kernel(scale, held_ref, rim_ref, sum_ref, *refs):
    out_ref, tile_ref, sems = refs[-3:]
    p = kept_half() if len(refs) == 3 else 1 - kept_half()
    base = sum_ref[...] * scale
    copies = []
    for half in range(2):
        for f in range(8 * half, 8 * half + 8):
            power = held_ref[p, f] if f < HELD else rim_ref[f - HELD]
            tile_ref[half, pl.ds(f % 8, ROWS, stride=8), :] = power - base
        copies.append(pltpu.make_async_copy(tile_ref.at[half], out_ref.at[p, half], sems.at[half]))
        copies[-1].start()
    for copy in copies:
        copy.wait()


def clean(scale, *args):
    far = [pl.BlockSpec(memory_space=pl.ANY)]
    return pl.pallas_call(
        functools.partial(clean_kernel, scale),
        out_shape=pltpu.HBM((2, 2, 8 * ROWS, LANES), jnp.float32),
        in_specs=[pl.BlockSpec(memory_space=pltpu.VMEM)] * 3 + far * (len(args) - 3),
        out_specs=far[0],
        scratch_shapes=[pltpu.VMEM((2, 8 * ROWS, LANES), jnp.float32), pltpu.SemaphoreType.DMA((2,))],
        input_output_aliases={3: 0} if len(args) == 4 else {},
        compiler_params=pltpu.CompilerParams(vmem_limit_bytes=16 << 20),
        cost_estimate=pl.CostEstimate(flops=10**6, bytes_accessed=2 << 20, transcendentals=0),
    )(*args)


def on_core(kernel, out_shape, scratch=(), far=False, vmem=16 << 20, cost=None):
    space = pl.ANY if far else pltpu.VMEM
    where = pltpu.VMEM if far else jax.ShapeDtypeStruct
    shapes = [s if not isinstance(s, tuple) else where(s, jnp.float32) for s in out_shape]
    return lambda *args: pl.pallas_call(
        kernel,
        out_shape=shapes,
        in_specs=[pl.BlockSpec(memory_space=space)] * len(args),
        out_specs=[pl.BlockSpec(memory_space=pltpu.VMEM)] * len(out_shape),
        scratch_shapes=[pltpu.VMEM(s, jnp.float32) if isinstance(s, tuple) else s for s in scratch],
        compiler_params=pltpu.CompilerParams(vmem_limit_bytes=vmem),
        cost_estimate=cost,
    )(*args)


def in_hbm(x):
    return pltpu.with_memory_space_constraint(x, pltpu.HBM)


def by_rows(x):
    lead, frames = x.shape[:-2], x.shape[-2]
    x = x.reshape(*lead, frames, ROWS, LANES)
    return jnp.swapaxes(x, -3, -2).reshape(*lead, ROWS * frames, LANES)


CORES = [(i, i ^ 1) for i in range(2 * X * Y * Z)]


def total_over_all(sums, back):
    left = [(i, (i - 1) % (2 * Y)) for i in range(2 * Y)]
    steps = [("y", YS[0])] + [("x", r) for r in XS] + [("y", YS[1])] + [("z", r) for r in ZS]
    for n, (axis, partner) in enumerate(steps):
        if n == 1:
            sums, back = lax.optimization_barrier((sums, back))
            back = lax.ppermute(back, "tm", left)
        sums = sums + lax.ppermute(sums, BOTH, swap_pairs(axis, partner))
    return sums, lax.ppermute(sums, BOTH, CORES), back


def body(voltages, filter_taps):
    devices = lax.axis_size("tm")
    table, twist = (jnp.asarray(t) for t in dft_tables())
    tiles = jnp.swapaxes(voltages[0].reshape(2, 2, 2, 8, ROWS, LANES), 3, 4)
    rim = (2, RIM, ROWS, LANES)
    cross, near = on_core(
        rim_kernel,
        [rim, rim],
        scratch=[pltpu.SemaphoreType.DMA((2, 2, RIM))],
        far=True,
        cost=SHORT,
    )(in_hbm(tiles))
    near = lax.ppermute(near, "tm", [(i, i ^ 1) for i in range(devices)])
    cross = lax.ppermute(cross, "tm", [(i, (i + 1 if i % 2 else i - 1) % devices) for i in range(devices)])
    strips = (2, 2, 2, ROWS * 8, LANES)
    held, part, had, send, taps, table, twist = on_core(
        held_kernel,
        [
            (2, HELD, ROWS, LANES),
            (2, 2 * RIM, ROWS, LANES),
            (ROWS, LANES),
            (ROWS, LANES),
            (ROWS * TAPS, LANES),
            pltpu.VMEM(table.shape, table.dtype),
            twist.shape,
        ],
        scratch=[
            strips,
            (2, 2, HELD, ROWS, LANES),
            pltpu.SemaphoreType.DMA((ROWS // 8,)),
            pltpu.SemaphoreType.DMA((3,)),
        ],
        far=True,
        cost=pl.CostEstimate(flops=2 * 10**9, bytes_accessed=6 << 20, transcendentals=0),
    )(in_hbm(tiles.reshape(strips)), in_hbm(by_rows(filter_taps)), in_hbm(table), in_hbm(twist))
    other = lax.ppermute(send, BOTH, CORES)
    early, had = on_core(
        near_kernel,
        [(RIM, ROWS, LANES), (ROWS, LANES)],
        cost=pl.CostEstimate(flops=10**9, bytes_accessed=3 << 20, transcendentals=0),
    )(part, near, taps, table, twist, had)
    ahead, back, sums = on_core(
        functools.partial(cross_kernel, devices - 1),
        [(RIM, ROWS, LANES), (RIM, ROWS, LANES), (ROWS, LANES)],
    )(part, cross, taps, table, twist, had, other, early)
    mine, other, back = total_over_all(sums, back)
    scale = 1.0 / (FRAMES * devices * lax.axis_size("beam"))
    out = clean(scale, held, ahead, mine)
    out = clean(scale, held, back, other, out)
    out = jnp.swapaxes(out.reshape(2, 2, ROWS, 8, LANES), 2, 3)
    return out.reshape(1, 2, FRAMES, CHANNELS)


def solution(mesh):
    placed = (P("beam", None, None, "tm", None), P())
    return jax.shard_map(
        body, mesh=mesh, in_specs=placed, out_specs=P("beam", None, "tm", None), check_vma=False
    )
```

```python
import functools
import math

import jax
import jax.numpy as jnp
import ml_dtypes
import numpy as np
from jax import lax
from jax.experimental import pallas as pl
from jax.experimental.pallas import tpu as pltpu
from jax.sharding import PartitionSpec as P

LANES = 128
ROWS = 64
CHANNELS = ROWS * LANES
TAPS = 8
FRAMES = 16
HELD = 9
RIM = FRAMES - HELD
SHORT = pl.CostEstimate(flops=1000, bytes_accessed=1000, transcendentals=0)
BOTH = ("beam", "tm")
X, Y, Z = 4, 4, 8

YS = ((3, 2, 1, 0), (1, 0, 3, 2))
XS = ((1, 0, 3, 2), (3, 2, 1, 0))
ZS = ((1, 0, 3, 2, 5, 4, 7, 6), (2, 3, 0, 1, 6, 7, 4, 5), (7, 6, 5, 4, 3, 2, 1, 0))


def place(z, x, y, core):
    return ((z * X + x) * Y + y) * 2 + core


def swap_pairs(axis, partner, crosswise=True):
    pairs = []
    for z in range(Z):
        for x in range(X):
            for y in range(Y):
                there = {
                    "z": lambda: (partner[z], x, y),
                    "x": lambda: (z, partner[x], y),
                    "y": lambda: (z, x, partner[y]),
                }[axis]()
                pairs += [(place(z, x, y, c), place(*there, 1 - c if crosswise and axis != "y" else c)) for c in range(2)]
    return pairs


def kept_half():
    tm, beam = lax.axis_index("tm"), lax.axis_index("beam")
    x, z = beam % X, beam // X
    return (tm + x + z + z // 2 + z // 4) % 2


def in_two(table):
    high = table.astype(ml_dtypes.bfloat16)
    low = (table - high.astype(np.float64)).astype(ml_dtypes.bfloat16)
    return high, low


def dft_tables():
    q = np.arange(ROWS)
    angle = 2.0 * np.pi * (np.outer(q, q) % ROWS) / ROWS
    cos, sin = np.cos(angle), np.sin(angle)
    first = np.block([[cos, sin], [-sin, cos]])
    high, low = in_two(first)
    first = np.block([[high, high], [low, low]])
    lane = np.arange(LANES)
    order = np.concatenate([np.arange(0, LANES, 2), np.arange(1, LANES, 2)])
    angle = 2.0 * np.pi * (np.outer(order, lane) % LANES) / LANES
    cos, sin = np.cos(angle), np.sin(angle)
    second = np.block([[cos, sin], [-sin, cos]])
    second = np.concatenate(in_two(second), axis=0)
    angle = 2.0 * np.pi * np.outer(q, lane) / CHANNELS
    twist = np.stack([np.cos(angle), np.sin(angle)]).astype(np.float32)
    return np.concatenate([first, second], axis=0), twist


def halves(values):
    high = values.astype(jnp.bfloat16)
    low = (values - high.astype(jnp.float32)).astype(jnp.bfloat16)
    return high, low


def power_rows(frames, table_ref, twist_ref):
    count = len(frames)
    cols = [jnp.concatenate([re, im], axis=0) for re, im in frames]
    high, low = halves(jnp.concatenate(cols, axis=1))
    both = jnp.dot(
        table_ref[: 4 * ROWS],
        jnp.concatenate([high, low], axis=0),
        preferred_element_type=jnp.float32,
    )
    section = both[: 2 * ROWS] + both[2 * ROWS :]
    cos, sin = twist_ref[0], twist_ref[1]
    rows = []
    for g in range(count):
        re = section[:ROWS, g * LANES : (g + 1) * LANES]
        im = section[ROWS:, g * LANES : (g + 1) * LANES]
        rows.append(jnp.concatenate([re * cos + im * sin, im * cos - re * sin], axis=1))
    high, low = halves(jnp.concatenate(rows, axis=0))
    across = (((1,), (1,)), ((), ()))
    table = table_ref[4 * ROWS :]
    both = lax.dot_general(table, high, across, preferred_element_type=jnp.float32)
    both += lax.dot_general(table, low, across, preferred_element_type=jnp.float32)
    spec = both[: 2 * LANES] + both[2 * LANES :]
    re, im = spec[:LANES], spec[LANES:]
    powers = (re * re + im * im) * (1.0 / CHANNELS)
    left = lax.broadcasted_iota(jnp.int32, (ROWS, LANES), 1) < ROWS
    out = []
    for g in range(0, count, 2):
        if g + 1 == count:
            out.append(jnp.concatenate([powers[:ROWS, g * ROWS :], powers[ROWS:, g * ROWS :]], axis=1))
            break
        even = powers[:ROWS, g * ROWS : (g + 2) * ROWS]
        odd = powers[ROWS:, g * ROWS : (g + 2) * ROWS]
        out.append(jnp.where(left, even, pltpu.roll(odd, ROWS, 1)))
        out.append(jnp.where(left, pltpu.roll(even, ROWS, 1), odd))
    return out


def rim_copies(volt_ref, out_ref, sems, last):
    p = 1 - kept_half()
    copies = []
    for n in range(RIM):
        f = HELD + n if last else n
        for c in range(2):
            frame = volt_ref.at[p, c, f // 8, :, f % 8, :]
            copies.append(pltpu.make_async_copy(frame, out_ref.at[c, n], sems.at[c, n]))
    return copies


def rim_kernel(volt_ref, cross_ref, near_ref, sems):
    for core in range(2):

        @pl.when(lax.axis_index("tm") % 2 == core)
        def _():
            copies = rim_copies(volt_ref, cross_ref, sems.at[1], core == 1)
            copies += rim_copies(volt_ref, near_ref, sems.at[0], core == 0)
            for copy in copies:
                copy.start()
            for copy in copies:
                copy.wait()


def held_kernel(
    volt_in, taps_in, table_in, twist_in,
    pow_ref, part_ref, mine_ref, send_ref, taps_ref, table_ref, twist_ref,
    volt_ref, filt_ref, strip_sems, table_sems,
):
    def strip_copy(s):
        rows = pl.ds(pl.multiple_of(s * 64, 64), 64)
        return pltpu.make_async_copy(volt_in.at[:, :, :, rows, :], volt_ref.at[:, :, :, rows, :], strip_sems.at[s])

    taps_copy = pltpu.make_async_copy(taps_in, taps_ref, table_sems.at[0])
    table_copy = pltpu.make_async_copy(table_in, table_ref, table_sems.at[1])
    twist_copy = pltpu.make_async_copy(twist_in, twist_ref, table_sems.at[2])
    taps_copy.start()
    for s in range(ROWS // 8):
        strip_copy(s).start()
    table_copy.start()
    twist_copy.start()
    taps_copy.wait()
    keep = lax.axis_index("tm") > 0
    own = kept_half()

    def strip(s, _):
        strip_copy(s).wait()
        at = pl.multiple_of(s * 64, 64)
        rows = pl.ds(pl.multiple_of(s * 8, 8), 8)
        taps = [taps_ref[pl.ds(at + t, 8, stride=8), :] for t in range(TAPS)]
        for p in range(2):
            for c in range(2):
                x = [volt_ref[p, c, f // 8, pl.ds(at + f % 8, 8, stride=8), :] for f in range(FRAMES)]
                for f in range(HELD):
                    total = taps[0] * x[f]
                    for t in range(1, TAPS):
                        total = total + taps[t] * x[f + t]
                    filt_ref[p, c, f, rows, :] = total
        for c in range(2):
            x = [volt_ref[own, c, f // 8, pl.ds(at + f % 8, 8, stride=8), :] for f in range(FRAMES)]
            for j in range(RIM):
                total = taps[0] * x[HELD + j]
                for t in range(1, RIM - j):
                    total = total + taps[t] * x[HELD + j + t]
                part_ref[c, j, rows, :] = total
                reach = RIM - j
                total = taps[reach] * x[0]
                for t in range(reach + 1, TAPS):
                    total = total + taps[t] * x[t - reach]
                part_ref[c, RIM + j, rows, :] = jnp.where(keep, total, 0.0)
        return 0

    lax.fori_loop(0, ROWS // 8, strip, 0)
    table_copy.wait()
    twist_copy.wait()
    sums = [None, None]
    for start in range(0, HELD, 2):
        which = [(p, f) for f in range(start, min(start + 2, HELD)) for p in range(2)]
        frames = [(filt_ref[p, 0, f], filt_ref[p, 1, f]) for p, f in which]
        for (p, f), power in zip(which, power_rows(frames, table_ref, twist_ref)):
            pow_ref[p, f] = power
            sums[p] = power if sums[p] is None else sums[p] + power
    mine_ref[...] = jnp.where(own == 1, sums[1], sums[0])
    send_ref[...] = jnp.where(own == 1, sums[0], sums[1])


def rim_powers(role, part_ref, came_ref, taps_ref, table_ref, twist_ref, total_sum, keep, store):
    taps = [taps_ref[pl.ds(t, ROWS, stride=8), :] for t in range(TAPS)]

    def finished(j):
        out = []
        for c in range(2):
            if role == "ahead":
                terms = [(RIM + i - j, i) for i in range(j + 1)]
                total = part_ref[c, j]
            else:
                terms = [(t, j + t) for t in range(RIM - j)]
                total = part_ref[c, RIM + j]
            rest = None
            for t, i in terms:
                term = taps[t] * came_ref[c, i]
                rest = term if rest is None else rest + term
            out.append(total + (rest if keep is None else jnp.where(keep, rest, 0.0)))
        return tuple(out)

    for start in range(0, RIM, 4):
        which = range(start, min(start + 4, RIM))
        for j, power in zip(which, power_rows([finished(j) for j in which], table_ref, twist_ref)):
            store[j] = power
            total_sum = total_sum + power
    return total_sum


def near_kernel(part_ref, near_ref, taps_ref, table_ref, twist_ref, had_ref, early_ref, sum_ref):
    for core, role in enumerate(("ahead", "back")):

        @pl.when(lax.axis_index("tm") % 2 == core)
        def _():
            sum_ref[...] = rim_powers(
                role, part_ref, near_ref, taps_ref, table_ref, twist_ref, had_ref[...], None, early_ref
            )


def cross_kernel(last, part_ref, cross_ref, taps_ref, table_ref, twist_ref, had_ref, other_ref, early_ref, ahead_ref, back_ref, sum_ref):
    tm = lax.axis_index("tm")
    for core, role in enumerate(("back", "ahead")):

        @pl.when(tm % 2 == core)
        def _():
            store, keep = (back_ref, None) if core == 0 else (ahead_ref, tm < last)
            had = had_ref[...] + other_ref[...]
            sum_ref[...] = rim_powers(
                role, part_ref, cross_ref, taps_ref, table_ref, twist_ref, had, keep, store
            )
            kept_ref = ahead_ref if core == 0 else back_ref
            kept_ref[...] = early_ref[...]


def clean_kernel(scale, held_ref, ahead_ref, back_ref, mine_ref, other_ref, out_ref, tile_ref, sems):
    copies = []
    for n, (rim_ref, sum_ref) in enumerate(((ahead_ref, mine_ref), (back_ref, other_ref))):
        p = 1 - kept_half() if n else kept_half()
        base = sum_ref[...] * scale
        for half in range(2):
            for f in range(8 * half, 8 * half + 8):
                power = held_ref[p, f] if f < HELD else rim_ref[f - HELD]
                tile_ref[n, half, pl.ds(f % 8, ROWS, stride=8), :] = power - base
            copies.append(pltpu.make_async_copy(tile_ref.at[n, half], out_ref.at[p, half], sems.at[n, half]))
            copies[-1].start()
    for copy in copies:
        copy.wait()


def clean(scale, *args):
    return pl.pallas_call(
        functools.partial(clean_kernel, scale),
        out_shape=pltpu.HBM((2, 2, 8 * ROWS, LANES), jnp.float32),
        in_specs=[pl.BlockSpec(memory_space=pltpu.VMEM)] * len(args),
        out_specs=pl.BlockSpec(memory_space=pl.ANY),
        scratch_shapes=[pltpu.VMEM((2, 2, 8 * ROWS, LANES), jnp.float32), pltpu.SemaphoreType.DMA((2, 2))],
        compiler_params=pltpu.CompilerParams(vmem_limit_bytes=16 << 20),
        cost_estimate=pl.CostEstimate(flops=10**6, bytes_accessed=4 << 20, transcendentals=0),
    )(*args)


def on_core(kernel, out_shape, scratch=(), far=False, vmem=16 << 20, cost=None):
    space = pl.ANY if far else pltpu.VMEM
    where = pltpu.VMEM if far else jax.ShapeDtypeStruct
    shapes = [s if not isinstance(s, tuple) else where(s, jnp.float32) for s in out_shape]
    return lambda *args: pl.pallas_call(
        kernel,
        out_shape=shapes,
        in_specs=[pl.BlockSpec(memory_space=space)] * len(args),
        out_specs=[pl.BlockSpec(memory_space=pltpu.VMEM)] * len(out_shape),
        scratch_shapes=[pltpu.VMEM(s, jnp.float32) if isinstance(s, tuple) else s for s in scratch],
        compiler_params=pltpu.CompilerParams(vmem_limit_bytes=vmem),
        cost_estimate=cost,
    )(*args)


def in_hbm(x):
    return pltpu.with_memory_space_constraint(x, pltpu.HBM)


def by_rows(x):
    lead, frames = x.shape[:-2], x.shape[-2]
    x = x.reshape(*lead, frames, ROWS, LANES)
    return jnp.swapaxes(x, -3, -2).reshape(*lead, ROWS * frames, LANES)


CORES = [(i, i ^ 1) for i in range(2 * X * Y * Z)]


def total_over_all(sums, back):
    left = [(i, (i - 1) % (2 * Y)) for i in range(2 * Y)]
    steps = [("y", YS[0])] + [("x", r) for r in XS] + [("y", YS[1])] + [("z", r) for r in ZS]
    for n, (axis, partner) in enumerate(steps):
        if n == 0:
            back = lax.ppermute(back, "tm", left)
        if n == len(steps) - 1:
            there = lax.ppermute(sums, BOTH, swap_pairs(axis, partner, crosswise=False))
            here = lax.ppermute(sums, BOTH, CORES)
        sums = sums + lax.ppermute(sums, BOTH, swap_pairs(axis, partner))
    return sums, here + there, back


def body(voltages, filter_taps):
    devices = lax.axis_size("tm")
    table, twist = (jnp.asarray(t) for t in dft_tables())
    tiles = jnp.swapaxes(voltages[0].reshape(2, 2, 2, 8, ROWS, LANES), 3, 4)
    rim = (2, RIM, ROWS, LANES)
    cross, near = on_core(
        rim_kernel,
        [rim, rim],
        scratch=[pltpu.SemaphoreType.DMA((2, 2, RIM))],
        far=True,
        cost=SHORT,
    )(in_hbm(tiles))
    near = lax.ppermute(near, "tm", [(i, i ^ 1) for i in range(devices)])
    cross = lax.ppermute(cross, "tm", [(i, (i + 1 if i % 2 else i - 1) % devices) for i in range(devices)])
    strips = (2, 2, 2, ROWS * 8, LANES)
    held, part, had, send, taps, table, twist = on_core(
        held_kernel,
        [
            (2, HELD, ROWS, LANES),
            (2, 2 * RIM, ROWS, LANES),
            (ROWS, LANES),
            (ROWS, LANES),
            (ROWS * TAPS, LANES),
            pltpu.VMEM(table.shape, table.dtype),
            twist.shape,
        ],
        scratch=[
            strips,
            (2, 2, HELD, ROWS, LANES),
            pltpu.SemaphoreType.DMA((ROWS // 8,)),
            pltpu.SemaphoreType.DMA((3,)),
        ],
        far=True,
        cost=pl.CostEstimate(flops=2 * 10**9, bytes_accessed=6 << 20, transcendentals=0),
    )(in_hbm(tiles.reshape(strips)), in_hbm(by_rows(filter_taps)), in_hbm(table), in_hbm(twist))
    other = lax.ppermute(send, BOTH, CORES)
    early, had = on_core(
        near_kernel,
        [(RIM, ROWS, LANES), (ROWS, LANES)],
        cost=pl.CostEstimate(flops=10**9, bytes_accessed=3 << 20, transcendentals=0),
    )(part, near, taps, table, twist, had)
    ahead, back, sums = on_core(
        functools.partial(cross_kernel, devices - 1),
        [(RIM, ROWS, LANES), (RIM, ROWS, LANES), (ROWS, LANES)],
    )(part, cross, taps, table, twist, had, other, early)
    mine, other, back = total_over_all(sums, back)
    scale = 1.0 / (FRAMES * devices * lax.axis_size("beam"))
    out = clean(scale, held, ahead, back, mine, other)
    out = jnp.swapaxes(out.reshape(2, 2, ROWS, 8, LANES), 2, 3)
    return out.reshape(1, 2, FRAMES, CHANNELS)


def solution(mesh):
    placed = (P("beam", None, None, "tm", None), P())
    return jax.shard_map(
        body, mesh=mesh, in_specs=placed, out_specs=P("beam", None, "tm", None), check_vma=False
    )
```

```python
import functools
import math

import jax
import jax.numpy as jnp
import ml_dtypes
import numpy as np
from jax import lax
from jax.experimental import pallas as pl
from jax.experimental.pallas import tpu as pltpu
from jax.sharding import PartitionSpec as P

LANES = 128
ROWS = 64
CHANNELS = ROWS * LANES
TAPS = 8
FRAMES = 16
HELD = 9
RIM = FRAMES - HELD
PIECES = 4
SHORT = pl.CostEstimate(flops=1000, bytes_accessed=1000, transcendentals=0)
BOTH = ("beam", "tm")
X, Y, Z = 4, 4, 8

YS = ((3, 2, 1, 0), (1, 0, 3, 2))
XS = ((1, 0, 3, 2), (3, 2, 1, 0))
ZS = ((1, 0, 3, 2, 5, 4, 7, 6), (2, 3, 0, 1, 6, 7, 4, 5), (7, 6, 5, 4, 3, 2, 1, 0))


def place(z, x, y, core):
    return ((z * X + x) * Y + y) * 2 + core


def swap_pairs(axis, partner):
    pairs = []
    for z in range(Z):
        for x in range(X):
            for y in range(Y):
                there = {
                    "z": lambda: (partner[z], x, y),
                    "x": lambda: (z, partner[x], y),
                    "y": lambda: (z, x, partner[y]),
                }[axis]()
                pairs += [(place(z, x, y, c), place(*there, c if axis == "y" else 1 - c)) for c in range(2)]
    return pairs


def kept_half():
    tm, beam = lax.axis_index("tm"), lax.axis_index("beam")
    x, z = beam % X, beam // X
    return (tm + x + z + z // 2 + z // 4) % 2


def in_two(table):
    high = table.astype(ml_dtypes.bfloat16)
    low = (table - high.astype(np.float64)).astype(ml_dtypes.bfloat16)
    return high, low


def dft_tables():
    q = np.arange(ROWS)
    angle = 2.0 * np.pi * (np.outer(q, q) % ROWS) / ROWS
    cos, sin = np.cos(angle), np.sin(angle)
    first = np.block([[cos, sin], [-sin, cos]])
    high, low = in_two(first)
    first = np.block([[high, high], [low, low]])
    lane = np.arange(LANES)
    order = np.concatenate([np.arange(0, LANES, 2), np.arange(1, LANES, 2)])
    angle = 2.0 * np.pi * (np.outer(order, lane) % LANES) / LANES
    cos, sin = np.cos(angle), np.sin(angle)
    second = np.block([[cos, sin], [-sin, cos]])
    second = np.concatenate(in_two(second), axis=0)
    angle = 2.0 * np.pi * np.outer(q, lane) / CHANNELS
    twist = np.stack([np.cos(angle), np.sin(angle)]).astype(np.float32)
    return np.concatenate([first, second], axis=0), twist


def halves(values):
    high = values.astype(jnp.bfloat16)
    low = (values - high.astype(jnp.float32)).astype(jnp.bfloat16)
    return high, low


def power_rows(frames, table_ref, twist_ref):
    count = len(frames)
    cols = [jnp.concatenate([re, im], axis=0) for re, im in frames]
    high, low = halves(jnp.concatenate(cols, axis=1))
    both = jnp.dot(
        table_ref[: 4 * ROWS],
        jnp.concatenate([high, low], axis=0),
        preferred_element_type=jnp.float32,
    )
    section = both[: 2 * ROWS] + both[2 * ROWS :]
    cos, sin = twist_ref[0], twist_ref[1]
    rows = []
    for g in range(count):
        re = section[:ROWS, g * LANES : (g + 1) * LANES]
        im = section[ROWS:, g * LANES : (g + 1) * LANES]
        rows.append(jnp.concatenate([re * cos + im * sin, im * cos - re * sin], axis=1))
    high, low = halves(jnp.concatenate(rows, axis=0))
    across = (((1,), (1,)), ((), ()))
    table = table_ref[4 * ROWS :]
    both = lax.dot_general(table, high, across, preferred_element_type=jnp.float32)
    both += lax.dot_general(table, low, across, preferred_element_type=jnp.float32)
    spec = both[: 2 * LANES] + both[2 * LANES :]
    re, im = spec[:LANES], spec[LANES:]
    powers = (re * re + im * im) * (1.0 / CHANNELS)
    left = lax.broadcasted_iota(jnp.int32, (ROWS, LANES), 1) < ROWS
    out = []
    for g in range(0, count, 2):
        if g + 1 == count:
            out.append(jnp.concatenate([powers[:ROWS, g * ROWS :], powers[ROWS:, g * ROWS :]], axis=1))
            break
        even = powers[:ROWS, g * ROWS : (g + 2) * ROWS]
        odd = powers[ROWS:, g * ROWS : (g + 2) * ROWS]
        out.append(jnp.where(left, even, pltpu.roll(odd, ROWS, 1)))
        out.append(jnp.where(left, pltpu.roll(even, ROWS, 1), odd))
    return out


def rim_copies(volt_ref, out_ref, sems, last):
    p = 1 - kept_half()
    copies = []
    for n in range(RIM):
        f = HELD + n if last else n
        for c in range(2):
            frame = volt_ref.at[p, c, f // 8, :, f % 8, :]
            copies.append(pltpu.make_async_copy(frame, out_ref.at[c, n], sems.at[c, n]))
    return copies


def rim_kernel(volt_ref, cross_ref, near_ref, sems):
    for core in range(2):

        @pl.when(lax.axis_index("tm") % 2 == core)
        def _():
            copies = rim_copies(volt_ref, cross_ref, sems.at[1], core == 1)
            copies += rim_copies(volt_ref, near_ref, sems.at[0], core == 0)
            for copy in copies:
                copy.start()
            for copy in copies:
                copy.wait()


def held_kernel(
    volt_in, taps_in, table_in, twist_in,
    pow_ref, part_ref, mine_ref, send_ref, taps_ref, table_ref, twist_ref,
    volt_ref, filt_ref, strip_sems, table_sems,
):
    def strip_copy(s):
        rows = pl.ds(pl.multiple_of(s * 64, 64), 64)
        return pltpu.make_async_copy(volt_in.at[:, :, :, rows, :], volt_ref.at[:, :, :, rows, :], strip_sems.at[s])

    taps_copy = pltpu.make_async_copy(taps_in, taps_ref, table_sems.at[0])
    table_copy = pltpu.make_async_copy(table_in, table_ref, table_sems.at[1])
    twist_copy = pltpu.make_async_copy(twist_in, twist_ref, table_sems.at[2])
    taps_copy.start()
    for s in range(ROWS // 8):
        strip_copy(s).start()
    table_copy.start()
    twist_copy.start()
    taps_copy.wait()
    keep = lax.axis_index("tm") > 0
    own = kept_half()

    def strip(s, _):
        strip_copy(s).wait()
        at = pl.multiple_of(s * 64, 64)
        rows = pl.ds(pl.multiple_of(s * 8, 8), 8)
        taps = [taps_ref[pl.ds(at + t, 8, stride=8), :] for t in range(TAPS)]
        for p in range(2):
            for c in range(2):
                x = [volt_ref[p, c, f // 8, pl.ds(at + f % 8, 8, stride=8), :] for f in range(FRAMES)]
                for f in range(HELD):
                    total = taps[0] * x[f]
                    for t in range(1, TAPS):
                        total = total + taps[t] * x[f + t]
                    filt_ref[p, c, f, rows, :] = total
        for c in range(2):
            x = [volt_ref[own, c, f // 8, pl.ds(at + f % 8, 8, stride=8), :] for f in range(FRAMES)]
            for j in range(RIM):
                total = taps[0] * x[HELD + j]
                for t in range(1, RIM - j):
                    total = total + taps[t] * x[HELD + j + t]
                part_ref[c, j, rows, :] = total
                reach = RIM - j
                total = taps[reach] * x[0]
                for t in range(reach + 1, TAPS):
                    total = total + taps[t] * x[t - reach]
                part_ref[c, RIM + j, rows, :] = jnp.where(keep, total, 0.0)
        return 0

    lax.fori_loop(0, ROWS // 8, strip, 0)
    table_copy.wait()
    twist_copy.wait()
    sums = [None, None]
    for start in range(0, HELD, 2):
        which = [(p, f) for f in range(start, min(start + 2, HELD)) for p in range(2)]
        frames = [(filt_ref[p, 0, f], filt_ref[p, 1, f]) for p, f in which]
        for (p, f), power in zip(which, power_rows(frames, table_ref, twist_ref)):
            pow_ref[p, f] = power
            sums[p] = power if sums[p] is None else sums[p] + power
    mine_ref[...] = jnp.where(own == 1, sums[1], sums[0])
    send_ref[...] = jnp.where(own == 1, sums[0], sums[1])


def rim_powers(role, part_ref, came_ref, taps_ref, table_ref, twist_ref, total_sum, keep, store):
    taps = [taps_ref[pl.ds(t, ROWS, stride=8), :] for t in range(TAPS)]

    def finished(j):
        out = []
        for c in range(2):
            if role == "ahead":
                terms = [(RIM + i - j, i) for i in range(j + 1)]
                total = part_ref[c, j]
            else:
                terms = [(t, j + t) for t in range(RIM - j)]
                total = part_ref[c, RIM + j]
            rest = None
            for t, i in terms:
                term = taps[t] * came_ref[c, i]
                rest = term if rest is None else rest + term
            out.append(total + (rest if keep is None else jnp.where(keep, rest, 0.0)))
        return tuple(out)

    for start in range(0, RIM, 4):
        which = range(start, min(start + 4, RIM))
        for j, power in zip(which, power_rows([finished(j) for j in which], table_ref, twist_ref)):
            store[j] = power
            total_sum = total_sum + power
    return total_sum


def near_kernel(part_ref, near_ref, taps_ref, table_ref, twist_ref, had_ref, early_ref, sum_ref):
    for core, role in enumerate(("ahead", "back")):

        @pl.when(lax.axis_index("tm") % 2 == core)
        def _():
            sum_ref[...] = rim_powers(
                role, part_ref, near_ref, taps_ref, table_ref, twist_ref, had_ref[...], None, early_ref
            )


def cross_kernel(last, part_ref, cross_ref, taps_ref, table_ref, twist_ref, had_ref, other_ref, early_ref, ahead_ref, back_ref, sum_ref):
    tm = lax.axis_index("tm")
    for core, role in enumerate(("back", "ahead")):

        @pl.when(tm % 2 == core)
        def _():
            store, keep = (back_ref, None) if core == 0 else (ahead_ref, tm < last)
            had = had_ref[...] + other_ref[...]
            sum_ref[...] = rim_powers(
                role, part_ref, cross_ref, taps_ref, table_ref, twist_ref, had, keep, store
            )
            kept_ref = ahead_ref if core == 0 else back_ref
            kept_ref[...] = early_ref[...]


def clean_kernel(scale, held_ref, rim_ref, sum_ref, *refs):
    out_ref, tile_ref, sems = refs[-3:]
    p = kept_half() if len(refs) == 3 else 1 - kept_half()
    copies = []
    for n in range(2 * PIECES):
        half, at = n % 2, n // 2 * (ROWS // PIECES)
        rows = pl.ds(at, ROWS // PIECES)
        base = sum_ref[rows, :] * scale
        for f in range(8 * half, 8 * half + 8):
            power = held_ref[p, f, rows, :] if f < HELD else rim_ref[f - HELD, rows, :]
            tile_ref[half, pl.ds(8 * at + f % 8, ROWS // PIECES, stride=8), :] = power - base
        piece = pl.ds(8 * at, 8 * ROWS // PIECES)
        copies.append(pltpu.make_async_copy(tile_ref.at[half, piece, :], out_ref.at[p, half, piece, :], sems.at[n]))
        copies[-1].start()
    for copy in copies:
        copy.wait()


def clean(scale, *args):
    far = [pl.BlockSpec(memory_space=pl.ANY)]
    return pl.pallas_call(
        functools.partial(clean_kernel, scale),
        out_shape=pltpu.HBM((2, 2, 8 * ROWS, LANES), jnp.float32),
        in_specs=[pl.BlockSpec(memory_space=pltpu.VMEM)] * 3 + far * (len(args) - 3),
        out_specs=far[0],
        scratch_shapes=[pltpu.VMEM((2, 8 * ROWS, LANES), jnp.float32), pltpu.SemaphoreType.DMA((2 * PIECES,))],
        input_output_aliases={3: 0} if len(args) == 4 else {},
        compiler_params=pltpu.CompilerParams(vmem_limit_bytes=16 << 20),
        cost_estimate=pl.CostEstimate(flops=10**6, bytes_accessed=2 << 20, transcendentals=0),
    )(*args)


def on_core(kernel, out_shape, scratch=(), far=False, vmem=16 << 20, cost=None):
    space = pl.ANY if far else pltpu.VMEM
    where = pltpu.VMEM if far else jax.ShapeDtypeStruct
    shapes = [s if not isinstance(s, tuple) else where(s, jnp.float32) for s in out_shape]
    return lambda *args: pl.pallas_call(
        kernel,
        out_shape=shapes,
        in_specs=[pl.BlockSpec(memory_space=space)] * len(args),
        out_specs=[pl.BlockSpec(memory_space=pltpu.VMEM)] * len(out_shape),
        scratch_shapes=[pltpu.VMEM(s, jnp.float32) if isinstance(s, tuple) else s for s in scratch],
        compiler_params=pltpu.CompilerParams(vmem_limit_bytes=vmem),
        cost_estimate=cost,
    )(*args)


def in_hbm(x):
    return pltpu.with_memory_space_constraint(x, pltpu.HBM)


def by_rows(x):
    lead, frames = x.shape[:-2], x.shape[-2]
    x = x.reshape(*lead, frames, ROWS, LANES)
    return jnp.swapaxes(x, -3, -2).reshape(*lead, ROWS * frames, LANES)


CORES = [(i, i ^ 1) for i in range(2 * X * Y * Z)]


def total_over_all(sums, back):
    left = [(i, (i - 1) % (2 * Y)) for i in range(2 * Y)]
    steps = [("y", YS[0])] + [("x", r) for r in XS] + [("y", YS[1])] + [("z", r) for r in ZS]
    for n, (axis, partner) in enumerate(steps):
        if n == 1:
            sums, back = lax.optimization_barrier((sums, back))
            back = lax.ppermute(back, "tm", left)
        sums = sums + lax.ppermute(sums, BOTH, swap_pairs(axis, partner))
    return sums, lax.ppermute(sums, BOTH, CORES), back


def body(voltages, filter_taps):
    devices = lax.axis_size("tm")
    table, twist = (jnp.asarray(t) for t in dft_tables())
    tiles = jnp.swapaxes(voltages[0].reshape(2, 2, 2, 8, ROWS, LANES), 3, 4)
    rim = (2, RIM, ROWS, LANES)
    cross, near = on_core(
        rim_kernel,
        [rim, rim],
        scratch=[pltpu.SemaphoreType.DMA((2, 2, RIM))],
        far=True,
        cost=SHORT,
    )(in_hbm(tiles))
    near = lax.ppermute(near, "tm", [(i, i ^ 1) for i in range(devices)])
    cross = lax.ppermute(cross, "tm", [(i, (i + 1 if i % 2 else i - 1) % devices) for i in range(devices)])
    strips = (2, 2, 2, ROWS * 8, LANES)
    held, part, had, send, taps, table, twist = on_core(
        held_kernel,
        [
            (2, HELD, ROWS, LANES),
            (2, 2 * RIM, ROWS, LANES),
            (ROWS, LANES),
            (ROWS, LANES),
            (ROWS * TAPS, LANES),
            pltpu.VMEM(table.shape, table.dtype),
            twist.shape,
        ],
        scratch=[
            strips,
            (2, 2, HELD, ROWS, LANES),
            pltpu.SemaphoreType.DMA((ROWS // 8,)),
            pltpu.SemaphoreType.DMA((3,)),
        ],
        far=True,
        cost=pl.CostEstimate(flops=2 * 10**9, bytes_accessed=6 << 20, transcendentals=0),
    )(in_hbm(tiles.reshape(strips)), in_hbm(by_rows(filter_taps)), in_hbm(table), in_hbm(twist))
    other = lax.ppermute(send, BOTH, CORES)
    early, had = on_core(
        near_kernel,
        [(RIM, ROWS, LANES), (ROWS, LANES)],
        cost=pl.CostEstimate(flops=10**9, bytes_accessed=3 << 20, transcendentals=0),
    )(part, near, taps, table, twist, had)
    ahead, back, sums = on_core(
        functools.partial(cross_kernel, devices - 1),
        [(RIM, ROWS, LANES), (RIM, ROWS, LANES), (ROWS, LANES)],
    )(part, cross, taps, table, twist, had, other, early)
    mine, other, back = total_over_all(sums, back)
    scale = 1.0 / (FRAMES * devices * lax.axis_size("beam"))
    out = clean(scale, held, ahead, mine)
    out = clean(scale, held, back, other, out)
    out = jnp.swapaxes(out.reshape(2, 2, ROWS, 8, LANES), 2, 3)
    return out.reshape(1, 2, FRAMES, CHANNELS)


def solution(mesh):
    placed = (P("beam", None, None, "tm", None), P())
    return jax.shard_map(
        body, mesh=mesh, in_specs=placed, out_specs=P("beam", None, "tm", None), check_vma=False
    )
```

```python
import functools
import math

import jax
import jax.numpy as jnp
import ml_dtypes
import numpy as np
from jax import lax
from jax.experimental import pallas as pl
from jax.experimental.pallas import tpu as pltpu
from jax.sharding import PartitionSpec as P

LANES = 128
ROWS = 64
CHANNELS = ROWS * LANES
TAPS = 8
FRAMES = 16
HELD = 9
RIM = FRAMES - HELD
SHORT = pl.CostEstimate(flops=1000, bytes_accessed=1000, transcendentals=0)
BOTH = ("beam", "tm")
X, Y, Z = 4, 4, 8

YS = ((3, 2, 1, 0), (1, 0, 3, 2))
XS = ((1, 0, 3, 2), (3, 2, 1, 0))
ZS = ((1, 0, 3, 2, 5, 4, 7, 6), (2, 3, 0, 1, 6, 7, 4, 5), (7, 6, 5, 4, 3, 2, 1, 0))


def place(z, x, y, core):
    return ((z * X + x) * Y + y) * 2 + core


def swap_pairs(axis, partner):
    pairs = []
    for z in range(Z):
        for x in range(X):
            for y in range(Y):
                there = {
                    "z": lambda: (partner[z], x, y),
                    "x": lambda: (z, partner[x], y),
                    "y": lambda: (z, x, partner[y]),
                }[axis]()
                pairs += [(place(z, x, y, c), place(*there, c if axis == "y" else 1 - c)) for c in range(2)]
    return pairs


def kept_half():
    tm, beam = lax.axis_index("tm"), lax.axis_index("beam")
    x, z = beam % X, beam // X
    return (tm + x + z + z // 2 + z // 4) % 2


def in_two(table):
    high = table.astype(ml_dtypes.bfloat16)
    low = (table - high.astype(np.float64)).astype(ml_dtypes.bfloat16)
    return high, low


def dft_tables():
    q = np.arange(ROWS)
    angle = 2.0 * np.pi * (np.outer(q, q) % ROWS) / ROWS
    cos, sin = np.cos(angle), np.sin(angle)
    first = np.block([[cos, sin], [-sin, cos]])
    high, low = in_two(first)
    first = np.block([[high, high], [low, low]])
    lane = np.arange(LANES)
    order = np.concatenate([np.arange(0, LANES, 2), np.arange(1, LANES, 2)])
    angle = 2.0 * np.pi * (np.outer(order, lane) % LANES) / LANES
    cos, sin = np.cos(angle), np.sin(angle)
    second = np.block([[cos, sin], [-sin, cos]])
    second = np.concatenate(in_two(second), axis=0)
    angle = 2.0 * np.pi * np.outer(q, lane) / CHANNELS
    twist = np.stack([np.cos(angle), np.sin(angle)]).astype(np.float32)
    return np.concatenate([first, second], axis=0), twist


def halves(values):
    high = values.astype(jnp.bfloat16)
    low = (values - high.astype(jnp.float32)).astype(jnp.bfloat16)
    return high, low


def power_rows(frames, table_ref, twist_ref):
    count = len(frames)
    cols = [jnp.concatenate([re, im], axis=0) for re, im in frames]
    high, low = halves(jnp.concatenate(cols, axis=1))
    both = jnp.dot(
        table_ref[: 4 * ROWS],
        jnp.concatenate([high, low], axis=0),
        preferred_element_type=jnp.float32,
    )
    section = both[: 2 * ROWS] + both[2 * ROWS :]
    cos, sin = twist_ref[0], twist_ref[1]
    rows = []
    for g in range(count):
        re = section[:ROWS, g * LANES : (g + 1) * LANES]
        im = section[ROWS:, g * LANES : (g + 1) * LANES]
        rows.append(jnp.concatenate([re * cos + im * sin, im * cos - re * sin], axis=1))
    high, low = halves(jnp.concatenate(rows, axis=0))
    across = (((1,), (1,)), ((), ()))
    table = table_ref[4 * ROWS :]
    both = lax.dot_general(table, high, across, preferred_element_type=jnp.float32)
    both += lax.dot_general(table, low, across, preferred_element_type=jnp.float32)
    spec = both[: 2 * LANES] + both[2 * LANES :]
    re, im = spec[:LANES], spec[LANES:]
    powers = (re * re + im * im) * (1.0 / CHANNELS)
    left = lax.broadcasted_iota(jnp.int32, (ROWS, LANES), 1) < ROWS
    out = []
    for g in range(0, count, 2):
        if g + 1 == count:
            out.append(jnp.concatenate([powers[:ROWS, g * ROWS :], powers[ROWS:, g * ROWS :]], axis=1))
            break
        even = powers[:ROWS, g * ROWS : (g + 2) * ROWS]
        odd = powers[ROWS:, g * ROWS : (g + 2) * ROWS]
        out.append(jnp.where(left, even, pltpu.roll(odd, ROWS, 1)))
        out.append(jnp.where(left, pltpu.roll(even, ROWS, 1), odd))
    return out


def rim_copies(volt_ref, out_ref, sems, last):
    p = 1 - kept_half()
    copies = []
    for n in range(RIM):
        f = HELD + n if last else n
        for c in range(2):
            frame = volt_ref.at[p, c, f // 8, :, f % 8, :]
            copies.append(pltpu.make_async_copy(frame, out_ref.at[c, n], sems.at[c, n]))
    return copies


def rim_kernel(volt_ref, cross_ref, near_ref, sems):
    for core in range(2):

        @pl.when(lax.axis_index("tm") % 2 == core)
        def _():
            copies = rim_copies(volt_ref, cross_ref, sems.at[1], core == 1)
            copies += rim_copies(volt_ref, near_ref, sems.at[0], core == 0)
            for copy in copies:
                copy.start()
            for copy in copies:
                copy.wait()


def held_kernel(
    volt_in, taps_in, table_in, twist_in,
    pow_ref, part_ref, mine_ref, send_ref, taps_ref, table_ref, twist_ref,
    volt_ref, filt_ref, strip_sems, table_sems,
):
    def strip_copy(s):
        rows = pl.ds(pl.multiple_of(s * 64, 64), 64)
        return pltpu.make_async_copy(volt_in.at[:, :, :, rows, :], volt_ref.at[:, :, :, rows, :], strip_sems.at[s])

    taps_copy = pltpu.make_async_copy(taps_in, taps_ref, table_sems.at[0])
    table_copy = pltpu.make_async_copy(table_in, table_ref, table_sems.at[1])
    twist_copy = pltpu.make_async_copy(twist_in, twist_ref, table_sems.at[2])
    taps_copy.start()
    for s in range(ROWS // 8):
        strip_copy(s).start()
    table_copy.start()
    twist_copy.start()
    taps_copy.wait()
    keep = lax.axis_index("tm") > 0
    own = kept_half()

    def strip(s, _):
        strip_copy(s).wait()
        at = pl.multiple_of(s * 64, 64)
        rows = pl.ds(pl.multiple_of(s * 8, 8), 8)
        taps = [taps_ref[pl.ds(at + t, 8, stride=8), :] for t in range(TAPS)]
        for p in range(2):
            for c in range(2):
                x = [volt_ref[p, c, f // 8, pl.ds(at + f % 8, 8, stride=8), :] for f in range(FRAMES)]
                for f in range(HELD):
                    total = taps[0] * x[f]
                    for t in range(1, TAPS):
                        total = total + taps[t] * x[f + t]
                    filt_ref[p, c, f, rows, :] = total
        for c in range(2):
            x = [volt_ref[own, c, f // 8, pl.ds(at + f % 8, 8, stride=8), :] for f in range(FRAMES)]
            for j in range(RIM):
                total = taps[0] * x[HELD + j]
                for t in range(1, RIM - j):
                    total = total + taps[t] * x[HELD + j + t]
                part_ref[c, j, rows, :] = total
                reach = RIM - j
                total = taps[reach] * x[0]
                for t in range(reach + 1, TAPS):
                    total = total + taps[t] * x[t - reach]
                part_ref[c, RIM + j, rows, :] = jnp.where(keep, total, 0.0)
        return 0

    lax.fori_loop(0, ROWS // 8, strip, 0)
    table_copy.wait()
    twist_copy.wait()
    sums = [None, None]
    for start in range(0, HELD, 2):
        which = [(p, f) for f in range(start, min(start + 2, HELD)) for p in range(2)]
        frames = [(filt_ref[p, 0, f], filt_ref[p, 1, f]) for p, f in which]
        for (p, f), power in zip(which, power_rows(frames, table_ref, twist_ref)):
            pow_ref[p, f] = power
            sums[p] = power if sums[p] is None else sums[p] + power
    mine_ref[...] = jnp.where(own == 1, sums[1], sums[0])
    send_ref[...] = jnp.where(own == 1, sums[0], sums[1])


def rim_powers(role, part_ref, came_ref, taps_ref, table_ref, twist_ref, total_sum, keep, store):
    taps = [taps_ref[pl.ds(t, ROWS, stride=8), :] for t in range(TAPS)]

    def finished(j):
        out = []
        for c in range(2):
            if role == "ahead":
                terms = [(RIM + i - j, i) for i in range(j + 1)]
                total = part_ref[c, j]
            else:
                terms = [(t, j + t) for t in range(RIM - j)]
                total = part_ref[c, RIM + j]
            rest = None
            for t, i in terms:
                term = taps[t] * came_ref[c, i]
                rest = term if rest is None else rest + term
            out.append(total + (rest if keep is None else jnp.where(keep, rest, 0.0)))
        return tuple(out)

    for start in range(0, RIM, 4):
        which = range(start, min(start + 4, RIM))
        for j, power in zip(which, power_rows([finished(j) for j in which], table_ref, twist_ref)):
            store[j] = power
            total_sum = total_sum + power
    return total_sum


def near_kernel(part_ref, near_ref, taps_ref, table_ref, twist_ref, had_ref, early_ref, sum_ref):
    for core, role in enumerate(("ahead", "back")):

        @pl.when(lax.axis_index("tm") % 2 == core)
        def _():
            sum_ref[...] = rim_powers(
                role, part_ref, near_ref, taps_ref, table_ref, twist_ref, had_ref[...], None, early_ref
            )


def cross_kernel(last, part_ref, cross_ref, taps_ref, table_ref, twist_ref, had_ref, other_ref, early_ref, ahead_ref, back_ref, sum_ref):
    tm = lax.axis_index("tm")
    for core, role in enumerate(("back", "ahead")):

        @pl.when(tm % 2 == core)
        def _():
            store, keep = (back_ref, None) if core == 0 else (ahead_ref, tm < last)
            had = had_ref[...] + other_ref[...]
            sum_ref[...] = rim_powers(
                role, part_ref, cross_ref, taps_ref, table_ref, twist_ref, had, keep, store
            )
            kept_ref = ahead_ref if core == 0 else back_ref
            kept_ref[...] = early_ref[...]


def clean_kernel(scale, held_ref, rim_ref, sum_ref, *refs):
    out_ref, tile_ref, sems = refs[-3:]
    p = kept_half() if len(refs) == 3 else 1 - kept_half()
    base = sum_ref[...] * scale
    copies = []
    for half in range(2):
        for f in range(8 * half, 8 * half + 8):
            power = held_ref[p, f] if f < HELD else rim_ref[f - HELD]
            tile_ref[half, pl.ds(f % 8, ROWS, stride=8), :] = power - base
        copies.append(pltpu.make_async_copy(tile_ref.at[half], out_ref.at[p, half], sems.at[half]))
        copies[-1].start()
    for copy in copies:
        copy.wait()


def clean(scale, *args):
    far = [pl.BlockSpec(memory_space=pl.ANY)]
    return pl.pallas_call(
        functools.partial(clean_kernel, scale),
        out_shape=pltpu.HBM((2, 2, 8 * ROWS, LANES), jnp.float32),
        in_specs=[pl.BlockSpec(memory_space=pltpu.VMEM)] * 3 + far * (len(args) - 3),
        out_specs=far[0],
        scratch_shapes=[pltpu.VMEM((2, 8 * ROWS, LANES), jnp.float32), pltpu.SemaphoreType.DMA((2,))],
        input_output_aliases={3: 0} if len(args) == 4 else {},
        compiler_params=pltpu.CompilerParams(vmem_limit_bytes=16 << 20),
        cost_estimate=pl.CostEstimate(flops=10**6, bytes_accessed=2 << 20, transcendentals=0),
    )(*args)


def on_core(kernel, out_shape, scratch=(), far=False, vmem=16 << 20, cost=None):
    space = pl.ANY if far else pltpu.VMEM
    where = pltpu.VMEM if far else jax.ShapeDtypeStruct
    shapes = [s if not isinstance(s, tuple) else where(s, jnp.float32) for s in out_shape]
    return lambda *args: pl.pallas_call(
        kernel,
        out_shape=shapes,
        in_specs=[pl.BlockSpec(memory_space=space)] * len(args),
        out_specs=[pl.BlockSpec(memory_space=pltpu.VMEM)] * len(out_shape),
        scratch_shapes=[pltpu.VMEM(s, jnp.float32) if isinstance(s, tuple) else s for s in scratch],
        compiler_params=pltpu.CompilerParams(vmem_limit_bytes=vmem),
        cost_estimate=cost,
    )(*args)


def in_hbm(x):
    return pltpu.with_memory_space_constraint(x, pltpu.HBM)


def by_rows(x):
    lead, frames = x.shape[:-2], x.shape[-2]
    x = x.reshape(*lead, frames, ROWS, LANES)
    return jnp.swapaxes(x, -3, -2).reshape(*lead, ROWS * frames, LANES)


CORES = [(i, i ^ 1) for i in range(2 * X * Y * Z)]


def total_over_all(sums, back):
    left = [(i, (i - 1) % (2 * Y)) for i in range(2 * Y)]
    steps = [("y", YS[0])] + [("x", r) for r in XS] + [("z", ZS[0]), ("y", YS[1])] + [("z", r) for r in ZS[1:]]
    for n, (axis, partner) in enumerate(steps):
        if n == 1:
            sums, back = lax.optimization_barrier((sums, back))
            back = lax.ppermute(back, "tm", left)
        sums = sums + lax.ppermute(sums, BOTH, swap_pairs(axis, partner))
    return sums, lax.ppermute(sums, BOTH, CORES), back


def body(voltages, filter_taps):
    devices = lax.axis_size("tm")
    table, twist = (jnp.asarray(t) for t in dft_tables())
    tiles = jnp.swapaxes(voltages[0].reshape(2, 2, 2, 8, ROWS, LANES), 3, 4)
    rim = (2, RIM, ROWS, LANES)
    cross, near = on_core(
        rim_kernel,
        [rim, rim],
        scratch=[pltpu.SemaphoreType.DMA((2, 2, RIM))],
        far=True,
        cost=SHORT,
    )(in_hbm(tiles))
    near = lax.ppermute(near, "tm", [(i, i ^ 1) for i in range(devices)])
    cross = lax.ppermute(cross, "tm", [(i, (i + 1 if i % 2 else i - 1) % devices) for i in range(devices)])
    strips = (2, 2, 2, ROWS * 8, LANES)
    held, part, had, send, taps, table, twist = on_core(
        held_kernel,
        [
            (2, HELD, ROWS, LANES),
            (2, 2 * RIM, ROWS, LANES),
            (ROWS, LANES),
            (ROWS, LANES),
            (ROWS * TAPS, LANES),
            pltpu.VMEM(table.shape, table.dtype),
            twist.shape,
        ],
        scratch=[
            strips,
            (2, 2, HELD, ROWS, LANES),
            pltpu.SemaphoreType.DMA((ROWS // 8,)),
            pltpu.SemaphoreType.DMA((3,)),
        ],
        far=True,
        cost=pl.CostEstimate(flops=2 * 10**9, bytes_accessed=6 << 20, transcendentals=0),
    )(in_hbm(tiles.reshape(strips)), in_hbm(by_rows(filter_taps)), in_hbm(table), in_hbm(twist))
    other = lax.ppermute(send, BOTH, CORES)
    early, had = on_core(
        near_kernel,
        [(RIM, ROWS, LANES), (ROWS, LANES)],
        cost=pl.CostEstimate(flops=10**9, bytes_accessed=3 << 20, transcendentals=0),
    )(part, near, taps, table, twist, had)
    ahead, back, sums = on_core(
        functools.partial(cross_kernel, devices - 1),
        [(RIM, ROWS, LANES), (RIM, ROWS, LANES), (ROWS, LANES)],
    )(part, cross, taps, table, twist, had, other, early)
    mine, other, back = total_over_all(sums, back)
    scale = 1.0 / (FRAMES * devices * lax.axis_size("beam"))
    out = clean(scale, held, ahead, mine)
    out = clean(scale, held, back, other, out)
    out = jnp.swapaxes(out.reshape(2, 2, ROWS, 8, LANES), 2, 3)
    return out.reshape(1, 2, FRAMES, CHANNELS)


def solution(mesh):
    placed = (P("beam", None, None, "tm", None), P())
    return jax.shard_map(
        body, mesh=mesh, in_specs=placed, out_specs=P("beam", None, "tm", None), check_vma=False
    )
```
